128 devices in a mesh: pb: 64 (over y, x, z), ha: 2 (over core).
Axes of the slice: x: 4, y: 4, z: 4, core: 2. Of those that a mesh axis runs over, the one named last changes fastest.
Arguments:
- tokens: bfloat16 [65536, 768], P('pb')
- shift_attn: float32 [768], replicated, may hold values from -3 to 3
- scale_attn: float32 [768], replicated, may hold values from -3 to 3
- gate_attn: float32 [768], replicated, may hold values from 0.5 to 2
- shift_mlp: float32 [768], replicated, may hold values from -3 to 3
- scale_mlp: float32 [768], replicated, may hold values from -3 to 3
- gate_mlp: float32 [768], replicated, may hold values from 0.5 to 2
- w_query: bfloat16 [768, 768], P(None, 'ha')
- w_key: bfloat16 [768, 768], P(None, 'ha')
- w_value: bfloat16 [768, 768], P(None, 'ha'), may hold values from -0.875 to 0.875
- w_out: bfloat16 [768, 768], P('ha'), may hold values from -0.21875 to 0.21875
- w_fc1: bfloat16 [768, 3072], P(None, 'ha'), may hold values from -0.21875 to 0.21875
- w_fc2: bfloat16 [3072, 768], P('ha'), may hold values from -0.109375 to 0.109375
- contact_owner: int32 [512, 8], replicated, may hold values from 0 to 63, all different within a row; in each aligned block of 8 rows (0 to 7, 8 to 15, ...) at most 2 rows name the same one
- contact_local: int32 [512, 8], replicated, may hold values from 0 to 7
- contact_count: int32 [512], P('pb'), may hold values from 1 to 8
Outputs:
- block_output: bfloat16 [65536, 768], P(('pb', 'ha'))
The draws below stay inside these ranges and needn't reach their ends.
Inputs may be any that keep to these rules, and one draw needn't show every extreme that they name: `contact_owner`: each query block lists 8 different owners. Among the 8 query blocks of one index of pb (aligned blocks of rows), no owner is named by more than 2 of them, a bound that some block reaches.
All inputs are finite; a program needn't handle non-finite values.
Results may differ from the reference program's by a relative error of at most 0.017.
Values may be sent and summed in bfloat16 or wider, within the bound.
A program may use at most 192 MiB of HBM per device.

```python
import math
import jax
import jax.numpy as jnp
import numpy as np
from jax import lax

D = 768
HEADS = 16
FF = 3072
HDIM = 48
QBLK = 128
KT = 8
QB_DEV = 8
CAP = 2
NQB = 512
SEQ = 65536
N_PB = 64


def shared_normal(key):
    return jax.random.normal(jax.random.fold_in(key, 5), (D, D), jnp.float32)


def draw_w_key(key, part):
    shared = shared_normal(key)
    key = jax.random.fold_in(key, 11)
    noise = jax.random.normal(key, (D, D), jnp.float32)
    return ((shared + 0.3 * noise) * D ** (-0.5)).astype(jnp.bfloat16)


def draw_w_query(key, part):
    key = jax.random.fold_in(key, 12)
    noise_key = jax.random.fold_in(key, 0)
    noise = jax.random.normal(noise_key, (D, D), jnp.float32)
    result = 2.0 * noise * D ** (-0.5)
    return result.astype(jnp.bfloat16)


def draw_tokens(key, part):
    key = jax.random.fold_in(key, 13)
    first_key = jax.random.fold_in(key, 0)
    result = jnp.clip(jax.random.normal(first_key, (SEQ, D), jnp.float32), -6.0, 6.0)
    return result.astype(jnp.bfloat16)


def place_ends(values, stream_key, low, top_value):
    dims = values.shape
    index_at = [jax.random.randint(jax.random.fold_in(stream_key, axis), (), 0, dims[axis]) for axis in range(len(dims))]
    values = values.at[tuple(index_at)].set(low)
    longest = dims.index(max(dims))
    index_at[longest] = (index_at[longest] + 1) % dims[longest]
    return values.at[tuple(index_at)].set(top_value)


def block_levels(key, shape, cuts, low, high):
    loudness, own = 1.0, jax.random.fold_in(key, 6)
    for dim, parts in cuts:
        heights = jnp.exp(jax.random.uniform(jax.random.fold_in(own, dim), (parts,), jnp.float32, low / len(cuts), high / len(cuts)))
        loudness = loudness * jnp.repeat(heights, shape[dim] // parts).reshape([-1 if axis == dim else 1 for axis in range(len(shape))])
    return loudness


def assign_block(own_key, own, number, rows, amount, top, limit, lean):
    order = jax.random.permutation(own_key, amount)
    crowded, common = shares(amount, rows * top, limit, lean, True), shares(amount, rows * top, limit, lean, False)
    places = jnp.arange(amount)

    def named(sizes, rotation):
        used = int((sizes > 0).sum())
        fixed = max(1, used // 4)
        moved = fixed + (places - fixed + rotation * (used - fixed)) % max(1, amount - fixed)
        return jnp.zeros((amount,), jnp.int32).at[order[jnp.where(places < fixed, places, moved)]].set(jnp.asarray(sizes, jnp.int32))

    sizes = jnp.where(number % 4 == 0, named(crowded, number // 4), named(common, number - number // 4 - 1))
    mixed = jax.random.permutation(jax.random.fold_in(own, 3), amount)
    giver, sink = mixed[0:amount // 2 * 2:2], mixed[1:amount // 2 * 2:2]
    slack = jnp.minimum(sizes[giver] - 1, limit - sizes[sink]) // 2
    slack = jnp.where((giver == order[0]) | (sink == order[0]) | (sizes[sink] == 0), 0, jnp.maximum(slack, 0))
    moved = jax.random.randint(jax.random.fold_in(own, 4), (amount // 2,), 0, 1 << 20) % (slack + 1)
    sizes = sizes.at[giver].add(-moved).at[sink].add(moved)
    items = jnp.searchsorted(jnp.cumsum(sizes), jnp.arange(rows * top), side="right").astype(jnp.int32)
    listing = items.reshape(top, rows).T
    listing = listing[jax.random.permutation(jax.random.fold_in(own, 1), rows)]
    rotation = jax.random.randint(jax.random.fold_in(own, 2), (rows, 1), 0, top)
    return jnp.take_along_axis(listing, (jnp.arange(top)[None, :] + rotation) % top, axis=1)


def shares(count, total, most, skew, full):
    portions = [(1 << 20) // math.isqrt(standing ** skew) + 1 for standing in range(1, count + 1)]
    largest = most if full else min(most, max(-(-total // count), total * portions[0] // sum(portions)))
    least = 1 if total - largest >= count - 1 else 0
    counts, surplus = [largest] + [least] * (count - 1), total - largest - least * (count - 1)
    while surplus > 0:
        candidates = [i for i in range(1, count) if counts[i] < largest] or [i for i in range(1, count) if counts[i] < most]
        pool, remaining = sum([portions[i] for i in candidates]), surplus
        for i in candidates:
            extra = min(most - counts[i], max(1, remaining * portions[i] // pool), surplus)
            counts[i] = counts[i] + extra
            surplus = surplus - extra
    return np.array(counts)


def centred(key, shape, deviation, limit, shards=(), held_as=jnp.bfloat16):
    level = block_levels(key, shape, shards, -0.22, 0.18) if shards else 1.0
    entries = jax.random.normal(key, shape, jnp.float32) * deviation * level
    return jnp.minimum(jnp.maximum(entries, -limit), limit).astype(held_as)


def setup_inputs(seed: int = 0) -> dict:
    key_of = jax.random.split(jax.random.key(seed), 17)
    tokens = draw_tokens(jax.random.fold_in(key_of[16], 71), 0)
    shift_attn = centred(key_of[1], (D,), 0.5, 3.0, (), jnp.float32)
    scale_attn = centred(key_of[2], (D,), 0.5, 3.0, (), jnp.float32)
    gate_attn = jnp.clip(jax.random.uniform(key_of[3], (D,), jnp.float32, 0.5, 2.0), 0.5, 2.0)
    shift_mlp = centred(key_of[4], (D,), 0.5, 3.0, (), jnp.float32)
    scale_mlp = centred(key_of[5], (D,), 0.5, 3.0, (), jnp.float32)
    gate_mlp = jnp.clip(jax.random.uniform(key_of[6], (D,), jnp.float32, 0.5, 2.0), 0.5, 2.0)
    w_query = draw_w_query(jax.random.fold_in(key_of[16], 71), 0)
    w_key = draw_w_key(jax.random.fold_in(key_of[16], 71), 0)
    w_value = centred(key_of[9], (D, D), (D // 16) ** -0.5, 0.875, ((1, 2),))
    w_out = centred(key_of[10], (D, D), D ** -0.5, 0.21875, ((0, 2),))
    w_fc1 = centred(key_of[11], (D, FF), D ** -0.5, 0.21875, ((1, 2),))
    w_fc2 = centred(key_of[12], (FF, D), FF ** -0.5, 0.109375, ((0, 2),))
    contact_owner_keys = jax.random.split(jax.random.fold_in(key_of[13], 1), NQB // QB_DEV)
    contact_owner_turns = jax.random.permutation(jax.random.fold_in(key_of[13], 3), NQB // QB_DEV)
    contact_owner = jax.vmap(lambda own, number: assign_block(jax.random.fold_in(key_of[13], 2), own, number, QB_DEV, N_PB, KT, CAP, 2))(contact_owner_keys, contact_owner_turns).reshape((NQB, KT))
    contact_local = place_ends(jax.random.randint(key_of[14], (NQB, KT), 0, QB_DEV), jax.random.fold_in(key_of[14], 1), 0, QB_DEV - 1).astype(jnp.int32)
    contact_count = place_ends(jax.random.randint(key_of[15], (NQB,), 1, KT + 1), jax.random.fold_in(key_of[15], 1), 1, KT).astype(jnp.int32)
    return dict(tokens=tokens, shift_attn=shift_attn, scale_attn=scale_attn, gate_attn=gate_attn, shift_mlp=shift_mlp, scale_mlp=scale_mlp, gate_mlp=gate_mlp, w_query=w_query, w_key=w_key, w_value=w_value, w_out=w_out, w_fc1=w_fc1, w_fc2=w_fc2, contact_owner=contact_owner, contact_local=contact_local, contact_count=contact_count)


epsilon = 1e-06

def modulate(stream, shift, scale):
    center = stream - lax.optimization_barrier(jnp.mean(stream, -1, keepdims=True))
    spread = lax.optimization_barrier(jnp.mean(center * center, -1, keepdims=True))
    return center * lax.rsqrt(spread + epsilon) * (1.0 + scale) + shift

def reference(tokens, shift_attn, scale_attn, gate_attn, shift_mlp, scale_mlp, gate_mlp, w_query, w_key, w_value, w_out, w_fc1, w_fc2, contact_owner, contact_local, contact_count):
    stream = tokens.astype(jnp.float32)
    normed = modulate(stream, shift_attn, scale_attn).astype(jnp.bfloat16)
    queries = lax.optimization_barrier(jnp.dot(normed, w_query, preferred_element_type=jnp.float32).astype(jnp.bfloat16))
    keys_all = lax.optimization_barrier(jnp.dot(normed, w_key, preferred_element_type=jnp.float32).astype(jnp.bfloat16))
    values_all = lax.optimization_barrier(jnp.dot(normed, w_value, preferred_element_type=jnp.float32).astype(jnp.bfloat16))
    block_count = SEQ // QBLK
    query_blocks = queries.reshape(block_count, QBLK, HEADS, HDIM)
    key_blocks = keys_all.reshape(block_count, QBLK, HEADS, HDIM)
    value_blocks = values_all.reshape(block_count, QBLK, HEADS, HDIM)
    own_block = jnp.arange(block_count, dtype=jnp.int32)[:, None]
    tile_list = jnp.concatenate([own_block, (contact_owner * QB_DEV + contact_local).astype(jnp.int32)], 1)
    slot_ids = jnp.arange(KT, dtype=jnp.int32)[None, :]
    live_tiles = jnp.concatenate([jnp.ones((block_count, 1), bool), slot_ids < contact_count[:, None]], 1)
    factor = HDIM ** (-0.5)

    def attend_block(index):
        query_rows = query_blocks[index].astype(jnp.float32)
        picked = tile_list[index]
        key_rows = key_blocks[picked].reshape((1 + KT) * QBLK, HEADS, HDIM).astype(jnp.float32)
        value_rows = value_blocks[picked].reshape((1 + KT) * QBLK, HEADS, HDIM).astype(jnp.float32)
        scores = jnp.einsum('ihd,jhd->hij', query_rows, key_rows) * factor
        live_mask = jnp.repeat(live_tiles[index], QBLK)
        scores = jnp.where(live_mask[None, None, :], scores, -1e+30)
        row_max = lax.optimization_barrier(jnp.max(scores, -1, keepdims=True))
        weights = jnp.exp(scores - row_max)
        totals = lax.optimization_barrier(jnp.sum(weights, -1))
        rounded = lax.optimization_barrier(weights.astype(jnp.bfloat16)).astype(jnp.float32)
        outputs = jnp.einsum('hij,jhd->ihd', rounded, value_rows)
        outputs = outputs / jnp.transpose(totals)[:, :, None]
        return outputs.astype(jnp.bfloat16).reshape(QBLK, D)
    attention = lax.map(attend_block, jnp.arange(block_count, dtype=jnp.int32)).reshape(SEQ, D)
    projected = jnp.dot(attention, w_out, preferred_element_type=jnp.float32)
    residual = lax.optimization_barrier((stream + gate_attn * projected).astype(jnp.bfloat16))
    resid_f = residual.astype(jnp.float32)
    normed_mlp = modulate(resid_f, shift_mlp, scale_mlp).astype(jnp.bfloat16)
    hidden = jax.nn.gelu(jnp.dot(normed_mlp, w_fc1, preferred_element_type=jnp.float32), approximate=True).astype(jnp.bfloat16)
    expanded = jnp.dot(hidden, w_fc2, preferred_element_type=jnp.float32)
    return (resid_f + gate_mlp * expanded).astype(jnp.bfloat16)
```

```python
import jax
import jax.numpy as jnp
from jax import lax
from jax.experimental import pallas as pl
from jax.experimental.pallas import tpu as pltpu
from jax.sharding import PartitionSpec as P

D = 768
HEADS = 16
HDIM = 48
FF = 3072
QBLK = 128
KT = 8
QB_DEV = 8
N_PB = 64
SIDE = 4
HALF = QBLK // 2
PART = D // 3
GRP = D // 2
MIB = 2**20
MESH = pl.DeviceIdType.MESH

ORDERS = ((2, 1, 0), (1, 0, 2), (0, 2, 1))
STRIDES = (16, 4, 1)
OFFS = (0, 1, 3, 2)

epsilon = 1e-06


def modulate(stream, shift, scale):
    center = stream - jnp.mean(stream, -1, keepdims=True)
    spread = jnp.mean(center * center, -1, keepdims=True)
    return center * lax.rsqrt(spread + epsilon) * (1.0 + scale) + shift


def exchange_kernel(
    tokens_ref, shift_ref, scale_ref, sel_ref, *refs
):
    w_in = refs[0:6]
    kv_ref = refs[6]
    w_out = refs[7:13]
    rows = [refs[13 + 4 * p : 17 + 4 * p] for p in range(3)]
    picked = refs[25]
    (a_s, a_r, af_s, af_r, b_s, b_r, bf_s, bf_r, c_s, c_r, x_s, x_r, l_s, w_s, w_r, wl_s) = refs[26:]

    pb = lax.axis_index("pb")
    ha = lax.axis_index("ha")
    me = (pb // 16, (pb // 4) % 4, pb % 4)

    def moved(base, axis, off):
        return base + (lax.rem(me[axis] + off, SIDE) - me[axis]) * STRIDES[axis]

    def chip(axis, off):
        return {"pb": moved(pb, axis, off), "ha": ha}

    other = {"pb": pb, "ha": 1 - ha}

    def remote(src, dst, ssem, rsem, dev):
        return pltpu.make_async_remote_copy(
            src_ref=src, dst_ref=dst, send_sem=ssem, recv_sem=rsem, device_id=dev, device_id_type=MESH
        )

    def norm_tile(t, carry):
        x = tokens_ref[pl.ds(pl.multiple_of(t * QBLK + ha * HALF, HALF), HALF), :].astype(jnp.float32)
        n = modulate(x, shift_ref[...], scale_ref[...]).astype(jnp.bfloat16)
        for p in range(3):
            rows[p][0][0, t] = n[:, p * PART : (p + 1) * PART]
        return carry

    barrier = pltpu.get_barrier_semaphore()
    for axis in range(3):
        for off in (1, 2, 3):
            pl.semaphore_signal(barrier, 1, device_id=chip(axis, off), device_id_type=MESH)
    pl.semaphore_signal(barrier, 1, device_id=other, device_id_type=MESH)
    lax.fori_loop(0, QB_DEV, norm_tile, 0)
    pl.semaphore_wait(barrier, 10)

    started = []

    def go(copy):
        copy.start()
        started.append(copy)

    local = []

    def send_a(p, d):
        a = ORDERS[p][0]
        return remote(
            rows[p][0].at[0], rows[p][0].at[3 if d == 0 else 1], a_s.at[p, d], a_r.at[p, d], chip(a, 1 if d == 0 else 3)
        )

    def forward_a(p, d):
        a = ORDERS[p][0]
        part = pl.ds(4 * d, 4)
        return remote(
            rows[p][0].at[3 if d == 0 else 1, part],
            rows[p][0].at[2, part],
            af_s.at[p, d],
            af_r.at[p, d],
            chip(a, 1 if d == 0 else 3),
        )

    def send_b(p, da, d):
        b = ORDERS[p][1]
        return remote(
            rows[p][0].at[da],
            rows[p][3 if d == 0 else 1].at[da],
            b_s.at[p, da, d],
            b_r.at[p, da, d],
            chip(b, 1 if d == 0 else 3),
        )

    def forward_b(p, da, d):
        b = ORDERS[p][1]
        part = pl.ds(4 * d, 4)
        return remote(
            rows[p][3 if d == 0 else 1].at[da, part],
            rows[p][2].at[da, part],
            bf_s.at[p, da, d],
            bf_r.at[p, da, d],
            chip(b, 1 if d == 0 else 3),
        )

    def send_c(p, db, g):
        c = ORDERS[p][2]
        off = OFFS[g]
        return remote(
            picked.at[p, g, db],
            kv_ref.at[p, 0, SIDE - off, db],
            c_s.at[p, db, g],
            c_r.at[p, db, g],
            chip(c, off),
        )

    def cross(p, db, g):
        src = picked.at[p, 0, db] if g == 0 else kv_ref.at[p, 0, SIDE - OFFS[g], db]
        return remote(
            src, kv_ref.at[p, 1, (SIDE - OFFS[g]) % SIDE, db], x_s.at[p, db, g], x_r.at[p, db, g], other
        )

    def keep(p, db):
        return pltpu.make_async_copy(picked.at[p, 0, db], kv_ref.at[p, 0, 0, db], l_s.at[p, db])

    def select(p, db):
        a, b, c = ORDERS[p]
        for g in range(4):
            dest = moved(pb, c, OFFS[g])

            def pick(j, carry):
                da, k = j // 2, j % 2
                owner = moved(moved(pb, b, db), a, da)
                code = sel_ref[dest, owner]
                number = jnp.where(k == 0, code & 7, (code >> 9) & 7)
                picked[p, g, db, j] = rows[p][db][da, number]
                return carry

            lax.fori_loop(0, 8, pick, 0)
        for g in (3, 1, 2):
            go(send_c(p, db, g))
        local.append(keep(p, db))
        local[-1].start()
        go(cross(p, db, 0))

    def relay(p, db):
        for g in (1, 2, 3):
            send_c(p, db, g).wait_recv()
            go(cross(p, db, g))

    for p in range(3):
        for d in range(2):
            go(send_a(p, d))
    for p in range(3):
        for d in range(2):
            go(send_b(p, 0, d))
    weights = [remote(w_in[i], w_out[i].at[ha], w_s.at[i], w_r.at[i], other) for i in range(6)]
    kept = [pltpu.make_async_copy(w_in[i], w_out[i].at[ha], wl_s.at[i]) for i in range(6)]
    for copy in weights:
        go(copy)
    for copy in kept:
        local.append(copy)
        copy.start()
    for p in range(3):
        for d in range(2):
            send_a(p, d).wait_recv()
            go(forward_a(p, d))
        for d in range(2):
            for da in (3, 1):
                go(send_b(p, da, d))
    for p in range(3):
        for d in range(2):
            forward_a(p, d).wait_recv()
        for d in range(2):
            go(send_b(p, 2, d))
    for da in (0, 3, 1, 2):
        for p in range(3):
            for d in range(2):
                send_b(p, da, d).wait_recv()
                go(forward_b(p, da, d))
        if da == 0:
            for p in range(3):
                select(p, 0)
    for p in range(3):
        for db in (3, 1):
            select(p, db)
    for p in range(3):
        relay(p, 0)
    for p in range(3):
        for da in (0, 3, 1, 2):
            for d in range(2):
                forward_b(p, da, d).wait_recv()
        select(p, 2)
    for db in (3, 1, 2):
        for p in range(3):
            relay(p, db)
    for p in range(3):
        for db in range(4):
            for g in range(4):
                cross(p, db, g).wait_recv()
    for copy in weights:
        copy.wait_recv()
    for copy in started:
        copy.wait_send()
    for copy in local:
        copy.wait()


def exchange(tokens, shift, scale, sel, weights):
    any_space = pl.BlockSpec(memory_space=pl.ANY)
    vmem = pl.BlockSpec(memory_space=pltpu.VMEM)
    dma = pltpu.SemaphoreType.DMA
    kv_shape = jax.ShapeDtypeStruct((3, 2, SIDE, SIDE, 8, HALF, PART), jnp.bfloat16)
    return pl.pallas_call(
        exchange_kernel,
        out_shape=[kv_shape] + [jax.ShapeDtypeStruct((2,) + w.shape, w.dtype) for w in weights],
        in_specs=[vmem, vmem, vmem, pl.BlockSpec(memory_space=pltpu.SMEM)] + [any_space] * 6,
        out_specs=[any_space] * 7,
        scratch_shapes=[pltpu.VMEM((SIDE, QB_DEV, HALF, PART), jnp.bfloat16)] * 12
        + [pltpu.VMEM((3, 4, SIDE, 8, HALF, PART), jnp.bfloat16)]
        + [dma((3, 2))] * 4
        + [dma((3, 4, 2))] * 4
        + [dma((3, 4, 4))] * 4
        + [dma((3, 4))]
        + [dma((6,))] * 3,
        compiler_params=pltpu.CompilerParams(
            collective_id=0, has_side_effects=True, vmem_limit_bytes=48 * MIB
        ),
        name="exchange",
    )(tokens, shift, scale, sel, *weights)


ROWS = (1 + KT) * QBLK
OWN = 4 * QBLK
SHARP = HDIM**-0.5 * 1.4426950408889634
WINDOWS = ((0, (0, 1, 2, 3, 4)), (128, (5, 6, 7)))
CHUNK = 512


def block_kernel(
    owner_ref,
    sel_ref,
    count_ref,
    shift_a,
    scale_a,
    gate_a,
    shift_m,
    scale_m,
    gate_m,
    tokens_ref,
    kv_ref,
    wq_h,
    wk_h,
    wv_h,
    wo_h,
    w1_h,
    w2_h,
    out_ref,
    x_ref,
    tok,
    normed,
    queries,
    keys,
    values,
    att,
    wq,
    wk,
    wv,
    wo,
    w1,
    w2,
    sem,
    gsem,
):
    pb = lax.axis_index("pb")
    ha = lax.axis_index("ha")
    me = (pb // 16, (pb // 4) % 4, pb % 4)

    loads = [pltpu.make_async_copy(tokens_ref.at[pl.ds(pl.multiple_of(ha * OWN, OWN), OWN)], tok, sem.at[6])]
    for i, (src, dst) in enumerate(((wq_h, wq), (wk_h, wk), (wv_h, wv), (wo_h, wo), (w1_h, w1), (w2_h, w2))):
        loads.append(pltpu.make_async_copy(src, dst, sem.at[i]))

    def gathers(blk, slot, act):
        for j in range(KT):
            entry = (ha * 4 + blk) * KT + j
            owner = owner_ref[pb, entry]
            first = (sel_ref[pb, owner] & 511) >> 3
            k = jnp.where(first == entry, 0, 1)
            rel = [
                (owner // 16 - me[0]) & 3,
                (owner // 4 - me[1]) & 3,
                (owner - me[2]) & 3,
            ]
            for p in range(3):
                a, b, c = ORDERS[p]
                act(
                    pltpu.make_async_copy(
                        kv_ref.at[p, :, rel[c], rel[b], rel[a] * 2 + k],
                        x_ref.at[slot, 1 + j, :, :, pl.ds(p * PART, PART)],
                        gsem.at[slot, j, p],
                    )
                )

    loads[0].start()
    loads[1].start()
    gathers(0, 0, lambda c: c.start())
    for copy in loads[2:]:
        copy.start()
    loads[0].wait()
    normed[...] = modulate(tok[...].astype(jnp.float32), shift_a[...], scale_a[...]).astype(jnp.bfloat16)
    loads[1].wait()
    for g in range(2):
        queries[g] = jnp.dot(normed[...], wq[g], preferred_element_type=jnp.float32).astype(jnp.bfloat16)
    loads[2].wait()
    loads[3].wait()

    lane = lax.broadcasted_iota(jnp.int32, (QBLK, 256), 1)
    key_pos = lax.broadcasted_iota(jnp.int32, (1, ROWS), 1)

    def one_block(blk, carry):
        slot = lax.rem(blk, 2)

        @pl.when(blk < 3)
        def _():
            gathers(blk + 1, 1 - slot, lambda c: c.start())

        gathers(blk, slot, lambda c: c.wait())
        base = pl.multiple_of(blk * QBLK, QBLK)
        x_ref[slot, 0] = normed[pl.ds(base, QBLK), :].reshape(2, HALF, D)
        x = x_ref[slot].reshape(ROWS, D)
        for g in range(2):
            keys[g] = jnp.dot(x, wk[g], preferred_element_type=jnp.float32).astype(jnp.bfloat16)
            values[g] = jnp.dot(x, wv[g], preferred_element_type=jnp.float32).astype(jnp.bfloat16)
        live = (1 + count_ref[ha * 4 + blk]) * QBLK
        bias = jnp.where(key_pos < live, 0.0, -1e30)

        def one_group(g, carry):
            for lo, heads in WINDOWS:
                q = queries[g, pl.ds(base, QBLK), lo : lo + 256]
                masks = [(lane >= h * HDIM - lo) & (lane < (h + 1) * HDIM - lo) for h in heads]
                stacked = jnp.concatenate([jnp.where(m, q, jnp.zeros_like(q)) for m in masks], 0)
                scores = lax.dot_general(
                    stacked,
                    keys[g, :, lo : lo + 256],
                    (((1,), (1,)), ((), ())),
                    preferred_element_type=jnp.float32,
                )
                scores = scores + bias
                top = jnp.max(scores, -1, keepdims=True)
                weights = jnp.exp2((scores - top) * SHARP)
                totals = jnp.sum(weights, -1, keepdims=True)
                outs = jnp.dot(
                    weights.astype(jnp.bfloat16), values[g, :, lo : lo + 256], preferred_element_type=jnp.float32
                )
                outs = outs / totals
                mixed = jnp.zeros((QBLK, 256), jnp.float32)
                for i, m in enumerate(masks):
                    mixed = jnp.where(m, outs[i * QBLK : (i + 1) * QBLK], mixed)
                mixed = mixed.astype(jnp.bfloat16)
                if lo == 0:
                    att[g, pl.ds(base, QBLK), 0:256] = mixed
                else:
                    first = att[g, pl.ds(base, QBLK), 128:256]
                    att[g, pl.ds(base, QBLK), 128:256] = jnp.where(
                        lane[:, :128] + 128 < 5 * HDIM, first, mixed[:, :128]
                    )
                    att[g, pl.ds(base, QBLK), 256:384] = mixed[:, 128:]
            return carry

        lax.fori_loop(0, 2, one_group, 0)
        return carry

    lax.fori_loop(0, 4, one_block, 0)

    loads[4].wait()
    projected = jnp.dot(att[0], wo[0], preferred_element_type=jnp.float32)
    projected += jnp.dot(att[1], wo[1], preferred_element_type=jnp.float32)
    residual = (tok[...].astype(jnp.float32) + gate_a[...] * projected).astype(jnp.bfloat16)
    tok[...] = residual
    normed[...] = modulate(residual.astype(jnp.float32), shift_m[...], scale_m[...]).astype(jnp.bfloat16)
    loads[5].wait()
    loads[6].wait()
    expanded = jnp.zeros((OWN, D), jnp.float32)
    for g in range(2):
        for lo in range(0, FF // 2, CHUNK):
            hidden = jnp.dot(normed[...], w1[g, :, lo : lo + CHUNK], preferred_element_type=jnp.float32)
            hidden = jax.nn.gelu(hidden, approximate=True).astype(jnp.bfloat16)
            expanded += jnp.dot(hidden, w2[g, lo : lo + CHUNK, :], preferred_element_type=jnp.float32)
    out_ref[...] = (tok[...].astype(jnp.float32) + gate_m[...] * expanded).astype(jnp.bfloat16)


def block(owners, sel, counts, vectors, tokens, kv, weights):
    any_space = pl.BlockSpec(memory_space=pl.ANY)
    vmem = pl.BlockSpec(memory_space=pltpu.VMEM)
    smem = pl.BlockSpec(memory_space=pltpu.SMEM)
    bf16 = jnp.bfloat16
    return pl.pallas_call(
        block_kernel,
        out_shape=jax.ShapeDtypeStruct((OWN, D), bf16),
        in_specs=[smem] * 3 + [vmem] * 6 + [any_space] * 8,
        out_specs=vmem,
        scratch_shapes=[
            pltpu.VMEM((2, 1 + KT, 2, HALF, D), bf16),
            pltpu.VMEM((OWN, D), bf16),
            pltpu.VMEM((OWN, D), bf16),
            pltpu.VMEM((2, OWN, GRP), bf16),
            pltpu.VMEM((2, ROWS, GRP), bf16),
            pltpu.VMEM((2, ROWS, GRP), bf16),
            pltpu.VMEM((2, OWN, GRP), bf16),
        ]
        + [pltpu.VMEM(w.shape, bf16) for w in weights]
        + [pltpu.SemaphoreType.DMA((7,)), pltpu.SemaphoreType.DMA((2, KT, 3))],
        compiler_params=pltpu.CompilerParams(vmem_limit_bytes=56 * MIB),
        name="block",
    )(owners, sel, counts, *vectors, tokens, kv, *weights)


def shards(
    tokens,
    shift_attn,
    scale_attn,
    gate_attn,
    shift_mlp,
    scale_mlp,
    gate_mlp,
    w_query,
    w_key,
    w_value,
    w_out,
    w_fc1,
    w_fc2,
    contact_owner,
    contact_local,
    contact_count,
):
    vectors = [
        v.reshape(1, D) for v in (shift_attn, scale_attn, gate_attn, shift_mlp, scale_mlp, gate_mlp)
    ]
    owners = contact_owner.reshape(N_PB, QB_DEV * KT)
    code = jnp.arange(QB_DEV * KT, dtype=jnp.int32)[None, :] * 8 + contact_local.reshape(N_PB, -1)
    hit = owners[:, :, None] == jnp.arange(N_PB, dtype=jnp.int32)[None, None, :]
    first = jnp.min(jnp.where(hit, code[:, :, None], 511), 1)
    last = jnp.max(jnp.where(hit, code[:, :, None], 0), 1)
    sel = first + (last & 7) * 512
    kv, *weights = exchange(
        tokens, vectors[0], vectors[1], sel, (w_query, w_key, w_value, w_out, w_fc1, w_fc2)
    )
    return block(owners, sel, contact_count, vectors, tokens, kv, weights)


def solution(mesh):
    placed = (
        P("pb", None),
        P(),
        P(),
        P(),
        P(),
        P(),
        P(),
        P(None, "ha"),
        P(None, "ha"),
        P(None, "ha"),
        P("ha", None),
        P(None, "ha"),
        P("ha", None),
        P(),
        P(),
        P("pb"),
    )
    return jax.shard_map(
        shards, mesh=mesh, in_specs=placed, out_specs=P(("pb", "ha"), None), check_vma=False
    )
```

```python
import jax
import jax.numpy as jnp
from jax import lax
from jax.experimental import pallas as pl
from jax.experimental.pallas import tpu as pltpu
from jax.sharding import PartitionSpec as P

D = 768
HEADS = 16
HDIM = 48
FF = 3072
QBLK = 128
KT = 8
QB_DEV = 8
N_PB = 64
SIDE = 4
HALF = QBLK // 2
PART = D // 3
GRP = D // 2
MIB = 2**20
MESH = pl.DeviceIdType.MESH

ORDERS = ((2, 1, 0), (1, 0, 2), (0, 2, 1))
STRIDES = (16, 4, 1)
OFFS = (0, 1, 3, 2)

epsilon = 1e-06


def modulate(stream, shift, scale):
    center = stream - jnp.mean(stream, -1, keepdims=True)
    spread = jnp.mean(center * center, -1, keepdims=True)
    return center * lax.rsqrt(spread + epsilon) * (1.0 + scale) + shift


def exchange_kernel(tokens_ref, shift_ref, scale_ref, owner_ref, block_ref, *refs):
    w_in = refs[0:6]
    kv_ref = refs[6]
    sel_out = refs[7]
    w_out = refs[8:14]
    rows = [refs[14 + 4 * p : 18 + 4 * p] for p in range(3)]
    picked = refs[26]
    tok, shift, scale, owners, blocks, table, sel_ref = refs[27:34]
    (a_s, a_r, af_s, af_r, b_s, b_r, bf_s, bf_r, c_s, c_r, x_s, x_r, l_s, w_s, w_r, t_s, v_s) = refs[34:]

    pb = lax.axis_index("pb")
    ha = lax.axis_index("ha")
    me = (pb // 16, (pb // 4) % 4, pb % 4)

    def moved(base, axis, off):
        return base + (lax.rem(me[axis] + off, SIDE) - me[axis]) * STRIDES[axis]

    def chip(axis, off):
        return {"pb": moved(pb, axis, off), "ha": ha}

    other = {"pb": pb, "ha": 1 - ha}

    def remote(src, dst, ssem, rsem, dev):
        return pltpu.make_async_remote_copy(
            src_ref=src, dst_ref=dst, send_sem=ssem, recv_sem=rsem, device_id=dev, device_id_type=MESH
        )

    half_rows = [
        pltpu.make_async_copy(
            tokens_ref.at[pl.ds(pl.multiple_of(t * QBLK + ha * HALF, HALF), HALF)], tok.at[t], t_s.at[t]
        )
        for t in range(QB_DEV)
    ]
    small = [
        pltpu.make_async_copy(src, dst, v_s.at[i])
        for i, (src, dst) in enumerate(
            ((shift_ref, shift), (scale_ref, scale), (owner_ref, owners), (block_ref, blocks))
        )
    ]
    for copy in small + half_rows:
        copy.start()

    barrier = pltpu.get_barrier_semaphore()
    for axis in range(3):
        for off in (1, 2, 3):
            pl.semaphore_signal(barrier, 1, device_id=chip(axis, off), device_id_type=MESH)
    pl.semaphore_signal(barrier, 1, device_id=other, device_id_type=MESH)
    small[0].wait()
    small[1].wait()
    for t in range(QB_DEV):
        half_rows[t].wait()
        n = modulate(tok[t].astype(jnp.float32), shift[...].reshape(1, D), scale[...].reshape(1, D))
        n = n.astype(jnp.bfloat16)
        for p in range(3):
            rows[p][0][0, t] = n[:, p * PART : (p + 1) * PART]
    pl.semaphore_wait(barrier, 10)

    started = []

    def go(copy):
        copy.start()
        started.append(copy)

    local = []

    def send_a(p, d):
        a = ORDERS[p][0]
        return remote(
            rows[p][0].at[0], rows[p][0].at[3 if d == 0 else 1], a_s.at[p, d], a_r.at[p, d], chip(a, 1 if d == 0 else 3)
        )

    def forward_a(p, d):
        a = ORDERS[p][0]
        part = pl.ds(4 * d, 4)
        return remote(
            rows[p][0].at[3 if d == 0 else 1, part],
            rows[p][0].at[2, part],
            af_s.at[p, d],
            af_r.at[p, d],
            chip(a, 1 if d == 0 else 3),
        )

    def send_b(p, da, d):
        b = ORDERS[p][1]
        return remote(
            rows[p][0].at[da],
            rows[p][3 if d == 0 else 1].at[da],
            b_s.at[p, da, d],
            b_r.at[p, da, d],
            chip(b, 1 if d == 0 else 3),
        )

    def forward_b(p, da, d):
        b = ORDERS[p][1]
        part = pl.ds(4 * d, 4)
        return remote(
            rows[p][3 if d == 0 else 1].at[da, part],
            rows[p][2].at[da, part],
            bf_s.at[p, da, d],
            bf_r.at[p, da, d],
            chip(b, 1 if d == 0 else 3),
        )

    def send_c(p, db, g):
        c = ORDERS[p][2]
        off = OFFS[g]
        return remote(
            picked.at[p, g, db],
            kv_ref.at[p, 0, SIDE - off, db],
            c_s.at[p, db, g],
            c_r.at[p, db, g],
            chip(c, off),
        )

    def cross(p, db, g):
        src = picked.at[p, 0, db] if g == 0 else kv_ref.at[p, 0, SIDE - OFFS[g], db]
        return remote(
            src, kv_ref.at[p, 1, (SIDE - OFFS[g]) % SIDE, db], x_s.at[p, db, g], x_r.at[p, db, g], other
        )

    def keep(p, db):
        return pltpu.make_async_copy(picked.at[p, 0, db], kv_ref.at[p, 0, 0, db], l_s.at[p, db])

    def select(p, db):
        a, b, c = ORDERS[p]
        for g in range(4):
            dest = moved(pb, c, OFFS[g])

            def pick(j, carry):
                da, k = j // 2, j % 2
                owner = moved(moved(pb, b, db), a, da)
                code = sel_ref[owner, dest * QB_DEV]
                number = jnp.where(k == 0, code & 7, (code >> 9) & 7)
                picked[p, g, db, j] = rows[p][db][da, number]
                return carry

            lax.fori_loop(0, 8, pick, 0)
        for g in (3, 1, 2):
            go(send_c(p, db, g))
        local.append(keep(p, db))
        local[-1].start()
        go(cross(p, db, 0))

    def relay(p, db):
        for g in (1, 2, 3):
            send_c(p, db, g).wait_recv()
            go(cross(p, db, g))

    for p in range(3):
        for d in range(2):
            go(send_a(p, d))
    for p in range(3):
        for d in range(2):
            go(send_b(p, 0, d))
    weights = [remote(w_in[i], w_out[i], w_s.at[i], w_r.at[i], other) for i in range(6)]
    for copy in weights:
        go(copy)

    small[2].wait()
    small[3].wait()
    lane = lax.broadcasted_iota(jnp.int32, (KT, N_PB * QB_DEV), 1)
    order = (lane & 7) * KT + lax.broadcasted_iota(jnp.int32, (KT, N_PB * QB_DEV), 0)
    code = order * 8 + blocks[...]
    size = N_PB * QB_DEV

    def tabulate(o, carry):
        hit = owners[...] == o
        first = jnp.where(hit, code, 511)
        last = jnp.where(hit, code, 0)
        for step in (1, 2, 4):
            first = jnp.minimum(first, pltpu.roll(first, size - step, 1))
            last = jnp.maximum(last, pltpu.roll(last, size - step, 1))
        first = jnp.min(first, 0, keepdims=True)
        last = jnp.max(last, 0, keepdims=True)
        table[pl.ds(o, 1), :] = first + (last & 7) * 512
        return carry

    lax.fori_loop(0, N_PB, tabulate, 0)
    to_scalars = pltpu.make_async_copy(table, sel_ref, v_s.at[4])
    to_scalars.start()
    local.append(pltpu.make_async_copy(table, sel_out, v_s.at[5]))
    local[-1].start()
    for p in range(3):
        for d in range(2):
            send_a(p, d).wait_recv()
            go(forward_a(p, d))
        for d in range(2):
            for da in (3, 1):
                go(send_b(p, da, d))
    for p in range(3):
        for d in range(2):
            forward_a(p, d).wait_recv()
        for d in range(2):
            go(send_b(p, 2, d))
    for da in (0, 3, 1, 2):
        for p in range(3):
            for d in range(2):
                send_b(p, da, d).wait_recv()
                go(forward_b(p, da, d))
        if da == 0:
            to_scalars.wait()
            for p in range(3):
                select(p, 0)
    for p in range(3):
        for db in (3, 1):
            select(p, db)
    for p in range(3):
        relay(p, 0)
    for p in range(3):
        for da in (0, 3, 1, 2):
            for d in range(2):
                forward_b(p, da, d).wait_recv()
        select(p, 2)
    for db in (3, 1, 2):
        for p in range(3):
            relay(p, db)
    for p in range(3):
        for db in range(4):
            for g in range(4):
                cross(p, db, g).wait_recv()
    for copy in weights:
        copy.wait_recv()
    for copy in started:
        copy.wait_send()
    for copy in local:
        copy.wait()


HBM = pl.BlockSpec(memory_space=pltpu.HBM)


def exchange(tokens, shift, scale, owners, blocks, weights):
    dma = pltpu.SemaphoreType.DMA
    bf16 = jnp.bfloat16
    kv_shape = jax.ShapeDtypeStruct((3, 2, SIDE, SIDE, 8, HALF, PART), bf16)
    table = (N_PB, N_PB * QB_DEV)
    return pl.pallas_call(
        exchange_kernel,
        out_shape=[kv_shape, jax.ShapeDtypeStruct(table, jnp.int32)]
        + [jax.ShapeDtypeStruct(w.shape, w.dtype) for w in weights],
        in_specs=[HBM] * 11,
        out_specs=[HBM] * 8,
        scratch_shapes=[pltpu.VMEM((SIDE, QB_DEV, HALF, PART), bf16)] * 12
        + [pltpu.VMEM((3, 4, SIDE, 8, HALF, PART), bf16)]
        + [pltpu.VMEM((QB_DEV, HALF, D), bf16)]
        + [pltpu.VMEM((D,), jnp.float32)] * 2
        + [pltpu.VMEM((KT, N_PB * QB_DEV), jnp.int32)] * 2
        + [pltpu.VMEM(table, jnp.int32), pltpu.SMEM(table, jnp.int32)]
        + [dma((3, 2))] * 4
        + [dma((3, 4, 2))] * 4
        + [dma((3, 4, 4))] * 4
        + [dma((3, 4))]
        + [dma((6,))] * 2
        + [dma((QB_DEV,)), dma((6,))],
        compiler_params=pltpu.CompilerParams(
            collective_id=0, has_side_effects=True, vmem_limit_bytes=62 * MIB
        ),
        name="exchange",
    )(tokens, shift, scale, owners, blocks, *weights)


ROWS = (1 + KT) * QBLK
OWN = 4 * QBLK
SHARP = HDIM**-0.5 * 1.4426950408889634
WINDOWS = ((0, (0, 1, 2, 3, 4)), (128, (5, 6, 7)))
CHUNK = 512


def block_kernel(
    count_ref,
    owner_h,
    sel_h,
    *refs,
):
    vectors_h = refs[0:6]
    tokens_ref, kv_ref = refs[6:8]
    own_h, other_h = refs[8:14], refs[14:20]
    out_ref, owner_ref, sel_ref = refs[20:23]
    vectors = refs[23:29]
    x_ref, tok, normed, queries, keys, values, att = refs[29:36]
    held = refs[36:42]
    wq, wk, wv, wo, w1, w2 = held
    sem, vsem, gsem = refs[42:]
    shift_a, scale_a, gate_a, shift_m, scale_m, gate_m = vectors

    def row(vector):
        return vector[...].reshape(1, D)

    pb = lax.axis_index("pb")
    ha = lax.axis_index("ha")
    me = (pb // 16, (pb // 4) % 4, pb % 4)

    base_lane = pl.multiple_of((pb // 16) * 128, 128)
    my_lane = (pb % 16) * QB_DEV
    tables = [
        pltpu.make_async_copy(owner_h.at[:, pl.ds(base_lane, 128)], owner_ref, vsem.at[6]),
        pltpu.make_async_copy(sel_h.at[:, pl.ds(base_lane, 128)], sel_ref, vsem.at[7]),
    ]
    small = [pltpu.make_async_copy(vectors_h[i], vectors[i], vsem.at[i]) for i in range(6)]
    tokens_in = pltpu.make_async_copy(
        tokens_ref.at[pl.ds(pl.multiple_of(ha * OWN, OWN), OWN)], tok, sem.at[12]
    )
    loads = []
    for i in range(6):
        loads.append(
            (
                pltpu.make_async_copy(own_h[i], held[i].at[ha], sem.at[i]),
                pltpu.make_async_copy(other_h[i], held[i].at[1 - ha], sem.at[6 + i]),
            )
        )

    def begin(*numbers):
        for i in numbers:
            loads[i][0].start()
            loads[i][1].start()

    def ready(*numbers):
        for i in numbers:
            loads[i][0].wait()
            loads[i][1].wait()

    def gathers(blk, slot, act):
        for j in range(KT):
            entry = (ha * 4 + blk) * KT + j
            owner = owner_ref[j, my_lane + ha * 4 + blk]
            first = (sel_ref[owner, my_lane] & 511) >> 3
            k = jnp.where(first == entry, 0, 1)
            rel = [
                (owner // 16 - me[0]) & 3,
                (owner // 4 - me[1]) & 3,
                (owner - me[2]) & 3,
            ]
            for p in range(3):
                a, b, c = ORDERS[p]
                act(
                    pltpu.make_async_copy(
                        kv_ref.at[p, :, rel[c], rel[b], rel[a] * 2 + k],
                        x_ref.at[slot, 1 + j, :, :, pl.ds(p * PART, PART)],
                        gsem.at[slot, j, p],
                    )
                )

    for copy in tables + small:
        copy.start()
    tokens_in.start()
    begin(0, 1, 2)
    for copy in tables:
        copy.wait()
    gathers(0, 0, lambda c: c.start())
    begin(3, 4, 5)
    for copy in small:
        copy.wait()
    tokens_in.wait()
    normed[...] = modulate(tok[...].astype(jnp.float32), row(shift_a), row(scale_a)).astype(jnp.bfloat16)
    ready(0)
    for g in range(2):
        queries[g] = jnp.dot(normed[...], wq[g], preferred_element_type=jnp.float32).astype(jnp.bfloat16)
    ready(1, 2)

    lane = lax.broadcasted_iota(jnp.int32, (QBLK, 256), 1)
    key_pos = lax.broadcasted_iota(jnp.int32, (1, ROWS), 1)

    def one_block(blk, carry):
        slot = lax.rem(blk, 2)

        @pl.when(blk < 3)
        def _():
            gathers(blk + 1, 1 - slot, lambda c: c.start())

        gathers(blk, slot, lambda c: c.wait())
        base = pl.multiple_of(blk * QBLK, QBLK)
        x_ref[slot, 0] = normed[pl.ds(base, QBLK), :].reshape(2, HALF, D)
        x = x_ref[slot].reshape(ROWS, D)
        for g in range(2):
            keys[g] = jnp.dot(x, wk[g], preferred_element_type=jnp.float32).astype(jnp.bfloat16)
            values[g] = jnp.dot(x, wv[g], preferred_element_type=jnp.float32).astype(jnp.bfloat16)
        live = (1 + count_ref[ha * 4 + blk]) * QBLK
        bias = jnp.where(key_pos < live, 0.0, -1e30)

        def one_group(g, carry):
            for lo, heads in WINDOWS:
                q = queries[g, pl.ds(base, QBLK), lo : lo + 256]
                masks = [(lane >= h * HDIM - lo) & (lane < (h + 1) * HDIM - lo) for h in heads]
                stacked = jnp.concatenate([jnp.where(m, q, jnp.zeros_like(q)) for m in masks], 0)
                scores = lax.dot_general(
                    stacked,
                    keys[g, :, lo : lo + 256],
                    (((1,), (1,)), ((), ())),
                    preferred_element_type=jnp.float32,
                )
                scores = scores + bias
                top = jnp.max(scores, -1, keepdims=True)
                weights = jnp.exp2((scores - top) * SHARP)
                totals = jnp.sum(weights, -1, keepdims=True)
                outs = jnp.dot(
                    weights.astype(jnp.bfloat16), values[g, :, lo : lo + 256], preferred_element_type=jnp.float32
                )
                outs = outs / totals
                mixed = jnp.zeros((QBLK, 256), jnp.float32)
                for i, m in enumerate(masks):
                    mixed = jnp.where(m, outs[i * QBLK : (i + 1) * QBLK], mixed)
                mixed = mixed.astype(jnp.bfloat16)
                if lo == 0:
                    att[g, pl.ds(base, QBLK), 0:256] = mixed
                else:
                    first = att[g, pl.ds(base, QBLK), 128:256]
                    att[g, pl.ds(base, QBLK), 128:256] = jnp.where(
                        lane[:, :128] + 128 < 5 * HDIM, first, mixed[:, :128]
                    )
                    att[g, pl.ds(base, QBLK), 256:384] = mixed[:, 128:]
            return carry

        lax.fori_loop(0, 2, one_group, 0)
        return carry

    lax.fori_loop(0, 4, one_block, 0)

    ready(3)
    projected = jnp.dot(att[0], wo[0], preferred_element_type=jnp.float32)
    projected += jnp.dot(att[1], wo[1], preferred_element_type=jnp.float32)
    residual = (tok[...].astype(jnp.float32) + row(gate_a) * projected).astype(jnp.bfloat16)
    tok[...] = residual
    normed[...] = modulate(residual.astype(jnp.float32), row(shift_m), row(scale_m)).astype(jnp.bfloat16)
    ready(4, 5)
    expanded = jnp.zeros((OWN, D), jnp.float32)
    for g in range(2):
        for lo in range(0, FF // 2, CHUNK):
            hidden = jnp.dot(normed[...], w1[g, :, lo : lo + CHUNK], preferred_element_type=jnp.float32)
            hidden = jax.nn.gelu(hidden, approximate=True).astype(jnp.bfloat16)
            expanded += jnp.dot(hidden, w2[g, lo : lo + CHUNK, :], preferred_element_type=jnp.float32)
    out_ref[...] = (tok[...].astype(jnp.float32) + row(gate_m) * expanded).astype(jnp.bfloat16)


def block(counts, owners, sel, vectors, tokens, kv, own, other):
    bf16 = jnp.bfloat16
    return pl.pallas_call(
        block_kernel,
        out_shape=jax.ShapeDtypeStruct((OWN, D), bf16),
        in_specs=[pl.BlockSpec(memory_space=pltpu.SMEM)] + [HBM] * 22,
        out_specs=pl.BlockSpec(memory_space=pltpu.VMEM),
        scratch_shapes=[pltpu.SMEM((KT, 128), jnp.int32), pltpu.SMEM((N_PB, 128), jnp.int32)]
        + [pltpu.VMEM((D,), jnp.float32)] * 6
        + [
            pltpu.VMEM((2, 1 + KT, 2, HALF, D), bf16),
            pltpu.VMEM((OWN, D), bf16),
            pltpu.VMEM((OWN, D), bf16),
            pltpu.VMEM((2, OWN, GRP), bf16),
            pltpu.VMEM((2, ROWS, GRP), bf16),
            pltpu.VMEM((2, ROWS, GRP), bf16),
            pltpu.VMEM((2, OWN, GRP), bf16),
        ]
        + [pltpu.VMEM((2,) + w.shape, bf16) for w in own]
        + [
            pltpu.SemaphoreType.DMA((13,)),
            pltpu.SemaphoreType.DMA((8,)),
            pltpu.SemaphoreType.DMA((2, KT, 3)),
        ],
        compiler_params=pltpu.CompilerParams(vmem_limit_bytes=62 * MIB),
        name="block",
    )(counts, owners, sel, *vectors, tokens, kv, *own, *other)


def shards(
    tokens,
    shift_attn,
    scale_attn,
    gate_attn,
    shift_mlp,
    scale_mlp,
    gate_mlp,
    w_query,
    w_key,
    w_value,
    w_out,
    w_fc1,
    w_fc2,
    contact_owner,
    contact_local,
    contact_count,
):
    vectors = (shift_attn, scale_attn, gate_attn, shift_mlp, scale_mlp, gate_mlp)
    own = (w_query, w_key, w_value, w_out, w_fc1, w_fc2)
    owners, blocks = contact_owner.T, contact_local.T
    kv, sel, *other = exchange(tokens, shift_attn, scale_attn, owners, blocks, own)
    return block(contact_count, owners, sel, vectors, tokens, kv, own, other)


def solution(mesh):
    placed = (
        P("pb", None),
        P(),
        P(),
        P(),
        P(),
        P(),
        P(),
        P(None, "ha"),
        P(None, "ha"),
        P(None, "ha"),
        P("ha", None),
        P(None, "ha"),
        P("ha", None),
        P(),
        P(),
        P("pb"),
    )
    return jax.shard_map(
        shards, mesh=mesh, in_specs=placed, out_specs=P(("pb", "ha"), None), check_vma=False
    )
```

```python
import jax
import jax.numpy as jnp
from jax import lax
from jax.experimental import pallas as pl
from jax.experimental.pallas import tpu as pltpu
from jax.sharding import PartitionSpec as P

D = 768
HEADS = 16
HDIM = 48
FF = 3072
QBLK = 128
KT = 8
QB_DEV = 8
N_PB = 64
SIDE = 4
HALF = QBLK // 2
PART = D // 3
GRP = D // 2
MIB = 2**20
MESH = pl.DeviceIdType.MESH

ORDERS = ((2, 1, 0), (1, 0, 2), (0, 2, 1))
STRIDES = (16, 4, 1)
OFFS = (0, 1, 3, 2)

epsilon = 1e-06


def modulate(stream, shift, scale):
    center = stream - jnp.mean(stream, -1, keepdims=True)
    spread = jnp.mean(center * center, -1, keepdims=True)
    return center * lax.rsqrt(spread + epsilon) * (1.0 + scale) + shift


ROWS = (1 + KT) * QBLK
OWN = 4 * QBLK
SHARP = HDIM**-0.5 * 1.4426950408889634
WINDOWS = ((0, (0, 1, 2, 3, 4), 255), (128, (5, 6, 7), 0))
CHUNK = 512
DEAD = -1e30


def with_lane(value, lane, fill):
    at = lax.broadcasted_iota(jnp.int32, (value.shape[0], 128), 1)
    left, right = value[:, :128], value[:, 128:]
    if lane == 0:
        left = jnp.where(at == 0, fill, left)
    else:
        right = jnp.where(at == 127, fill, right)
    return jnp.concatenate([left, right], 1)


def exchange_kernel(tokens_ref, shift_ref, scale_ref, owner_ref, block_ref, *refs):
    w_in = refs[0:6]
    kv_ref, place_out, q_out, mine_out = refs[6:10]
    w_out = refs[10:15]
    rows = [refs[15 + 4 * p : 19 + 4 * p] for p in range(3)]
    picked = refs[27]
    tok, shift, scale, owners, blocks, table, sel_ref, owner_s, places = refs[28:37]
    own, qkv_w, queries, mine = refs[37:41]
    (a_s, a_r, af_s, af_r, b_s, b_r, bf_s, bf_r, c_s, c_r, x_s, x_r, l_s, w_s, w_r, t_s, v_s) = refs[41:]

    pb = lax.axis_index("pb")
    ha = lax.axis_index("ha")
    me = (pb // 16, (pb // 4) % 4, pb % 4)

    def moved(base, axis, off):
        return base + (lax.rem(me[axis] + off, SIDE) - me[axis]) * STRIDES[axis]

    def chip(axis, off):
        return {"pb": moved(pb, axis, off), "ha": ha}

    other = {"pb": pb, "ha": 1 - ha}

    def remote(src, dst, ssem, rsem, dev):
        return pltpu.make_async_remote_copy(
            src_ref=src, dst_ref=dst, send_sem=ssem, recv_sem=rsem, device_id=dev, device_id_type=MESH
        )

    half_rows = [
        pltpu.make_async_copy(
            tokens_ref.at[pl.ds(pl.multiple_of(t * QBLK + ha * HALF, HALF), HALF)], tok.at[t], t_s.at[t]
        )
        for t in range(QB_DEV)
    ]
    small = [
        pltpu.make_async_copy(src, dst, v_s.at[i])
        for i, (src, dst) in enumerate(
            (
                (shift_ref, shift),
                (scale_ref, scale),
                (owner_ref, owners),
                (block_ref, blocks),
                (owner_ref, owner_s),
                (tokens_ref.at[pl.ds(pl.multiple_of(ha * OWN, OWN), OWN)], own),
                (w_in[0], qkv_w.at[0, ha]),
                (w_in[1], qkv_w.at[1, ha]),
                (w_in[2], qkv_w.at[2, ha]),
            )
        )
    ]
    for copy in small[:2] + half_rows + small[2:]:
        copy.start()

    barrier = pltpu.get_barrier_semaphore()
    for axis in range(3):
        for off in (1, 2, 3):
            pl.semaphore_signal(barrier, 1, device_id=chip(axis, off), device_id_type=MESH)
    pl.semaphore_signal(barrier, 1, device_id=other, device_id_type=MESH)
    small[0].wait()
    small[1].wait()
    for t in range(QB_DEV):
        half_rows[t].wait()
        n = modulate(tok[t].astype(jnp.float32), shift[...].reshape(1, D), scale[...].reshape(1, D))
        n = n.astype(jnp.bfloat16)
        for p in range(3):
            rows[p][0][0, t] = n[:, p * PART : (p + 1) * PART]
    pl.semaphore_wait(barrier, 10)

    started = []

    def go(copy):
        copy.start()
        started.append(copy)

    local = []

    def send_a(p, d):
        a = ORDERS[p][0]
        return remote(
            rows[p][0].at[0], rows[p][0].at[3 if d == 0 else 1], a_s.at[p, d], a_r.at[p, d], chip(a, 1 if d == 0 else 3)
        )

    def forward_a(p, d):
        a = ORDERS[p][0]
        part = pl.ds(4 * d, 4)
        return remote(
            rows[p][0].at[3 if d == 0 else 1, part],
            rows[p][0].at[2, part],
            af_s.at[p, d],
            af_r.at[p, d],
            chip(a, 1 if d == 0 else 3),
        )

    def send_b(p, da, d):
        b = ORDERS[p][1]
        return remote(
            rows[p][0].at[da],
            rows[p][3 if d == 0 else 1].at[da],
            b_s.at[p, da, d],
            b_r.at[p, da, d],
            chip(b, 1 if d == 0 else 3),
        )

    def forward_b(p, da, d):
        b = ORDERS[p][1]
        part = pl.ds(4 * d, 4)
        return remote(
            rows[p][3 if d == 0 else 1].at[da, part],
            rows[p][2].at[da, part],
            bf_s.at[p, da, d],
            bf_r.at[p, da, d],
            chip(b, 1 if d == 0 else 3),
        )

    def send_c(p, db, g):
        c = ORDERS[p][2]
        off = OFFS[g]
        return remote(
            picked.at[p, g, db],
            kv_ref.at[p, 0, SIDE - off, db],
            c_s.at[p, db, g],
            c_r.at[p, db, g],
            chip(c, off),
        )

    def cross(p, db, g):
        src = picked.at[p, 0, db] if g == 0 else kv_ref.at[p, 0, SIDE - OFFS[g], db]
        return remote(
            src, kv_ref.at[p, 1, (SIDE - OFFS[g]) % SIDE, db], x_s.at[p, db, g], x_r.at[p, db, g], other
        )

    def keep(p, db):
        return pltpu.make_async_copy(picked.at[p, 0, db], kv_ref.at[p, 0, 0, db], l_s.at[p, db])

    def select(p, db):
        a, b, c = ORDERS[p]
        for g in range(4):
            dest = moved(pb, c, OFFS[g])

            def pick(j, carry):
                da, k = j // 2, j % 2
                owner = moved(moved(pb, b, db), a, da)
                code = sel_ref[owner, dest * QB_DEV]
                number = jnp.where(k == 0, code & 7, (code >> 9) & 7)
                picked[p, g, db, j] = rows[p][db][da, number]
                return carry

            lax.fori_loop(0, 8, pick, 0)
        for g in (3, 1, 2):
            go(send_c(p, db, g))
        local.append(keep(p, db))
        local[-1].start()
        go(cross(p, db, 0))

    def relay(p, db):
        for g in (1, 2, 3):
            send_c(p, db, g).wait_recv()
            go(cross(p, db, g))

    for p in range(3):
        for d in range(2):
            go(send_a(p, d))
    for p in range(3):
        for d in range(2):
            go(send_b(p, 0, d))
    weights = [
        remote(w_in[i], qkv_w.at[i, ha] if i < 3 else w_out[i - 1], w_s.at[i], w_r.at[i], other)
        for i in range(6)
    ]
    for copy in weights:
        go(copy)

    small[2].wait()
    small[3].wait()
    lane = lax.broadcasted_iota(jnp.int32, (KT, N_PB * QB_DEV), 1)
    order = (lane & 7) * KT + lax.broadcasted_iota(jnp.int32, (KT, N_PB * QB_DEV), 0)
    code = order * 8 + blocks[...]
    size = N_PB * QB_DEV

    def tabulate(o, carry):
        hit = owners[...] == o
        first = jnp.where(hit, code, 511)
        last = jnp.where(hit, code, 0)
        for step in (1, 2, 4):
            first = jnp.minimum(first, pltpu.roll(first, size - step, 1))
            last = jnp.maximum(last, pltpu.roll(last, size - step, 1))
        first = jnp.min(first, 0, keepdims=True)
        last = jnp.max(last, 0, keepdims=True)
        table[pl.ds(o, 1), :] = first + (last & 7) * 512
        return carry

    lax.fori_loop(0, N_PB, tabulate, 0)
    to_scalars = pltpu.make_async_copy(table, sel_ref, v_s.at[9])
    to_scalars.start()

    def keep_local(src, dst, number):
        local.append(pltpu.make_async_copy(src, dst, v_s.at[number]))
        local[-1].start()

    def place_entry(e, carry):
        i, j = e // KT, e % KT
        owner = owner_s[j, pb * QB_DEV + ha * 4 + i]
        first = (sel_ref[owner, pb * QB_DEV] & 511) >> 3
        k = jnp.where(first == ha * 4 * KT + e, 0, 1)
        rel = ((owner // 16 - me[0]) & 3, (owner // 4 - me[1]) & 3, (owner - me[2]) & 3)
        for p in range(3):
            a, b, c = ORDERS[p]
            places[p, e] = ((rel[c] * 4 + rel[b]) * 4 + rel[a]) * 2 + k
        return carry

    def own_blocks():
        small[5].wait()
        normed = modulate(own[...].astype(jnp.float32), shift[...].reshape(1, D), scale[...].reshape(1, D))
        own[...] = normed.astype(jnp.bfloat16)
        for i in range(3):
            small[6 + i].wait()
            remote(w_in[i], qkv_w.at[i, 1 - ha], w_s.at[i], w_r.at[i], other).wait_recv()
        keep_local(qkv_w.at[1, 1 - ha], w_out[0], 10)
        keep_local(qkv_w.at[2, 1 - ha], w_out[1], 11)

        def one_group(g, carry):
            def product(i):
                return jnp.dot(own[...], qkv_w[i, g], preferred_element_type=jnp.float32)

            queries[g] = (product(0) * SHARP).astype(jnp.bfloat16)
            for i in range(2):
                result = product(1 + i).astype(jnp.bfloat16)
                fill = jnp.full((QBLK, 128), float(i), jnp.bfloat16)
                for w, (lo, _, spare) in enumerate(WINDOWS):
                    for blk in range(4):
                        mine[blk, g, w, i] = with_lane(
                            result[blk * QBLK : (blk + 1) * QBLK, lo : lo + 256], spare, fill
                        )
            return carry

        lax.fori_loop(0, 2, one_group, 0)
        keep_local(queries, q_out, 12)
        keep_local(mine, mine_out, 13)
        lax.fori_loop(0, 4 * KT, place_entry, 0)
        keep_local(places, place_out, 14)

    for p in range(3):
        for d in range(2):
            send_a(p, d).wait_recv()
            go(forward_a(p, d))
        for d in range(2):
            for da in (3, 1):
                go(send_b(p, da, d))
    for p in range(3):
        for d in range(2):
            forward_a(p, d).wait_recv()
        for d in range(2):
            go(send_b(p, 2, d))
    to_scalars.wait()
    small[4].wait()
    for p in range(3):
        select(p, 0)
    own_blocks()
    for da in (0, 3, 1, 2):
        for p in range(3):
            for d in range(2):
                send_b(p, da, d).wait_recv()
                go(forward_b(p, da, d))
    for p in range(3):
        for db in (3, 1):
            select(p, db)
    for p in range(3):
        relay(p, 0)
    for p in range(3):
        for da in (0, 3, 1, 2):
            for d in range(2):
                forward_b(p, da, d).wait_recv()
        select(p, 2)
    for db in (3, 1, 2):
        for p in range(3):
            relay(p, db)
    for p in range(3):
        for db in range(4):
            for g in range(4):
                cross(p, db, g).wait_recv()
    for copy in weights[3:]:
        copy.wait_recv()
    for copy in started:
        copy.wait_send()
    for copy in local:
        copy.wait()


HBM = pl.BlockSpec(memory_space=pltpu.HBM)


def exchange(tokens, shift, scale, owners, blocks, weights):
    dma = pltpu.SemaphoreType.DMA
    bf16 = jnp.bfloat16
    kv_shape = jax.ShapeDtypeStruct((3, 2, SIDE, SIDE, 8, HALF, PART), bf16)
    table = (N_PB, N_PB * QB_DEV)
    return pl.pallas_call(
        exchange_kernel,
        out_shape=[
            kv_shape,
            jax.ShapeDtypeStruct((8, 128), jnp.int32),
            jax.ShapeDtypeStruct((2, OWN, GRP), bf16),
            jax.ShapeDtypeStruct((4, 2, 2, 2, QBLK, 256), bf16),
        ]
        + [jax.ShapeDtypeStruct(w.shape, w.dtype) for w in weights[1:]],
        in_specs=[HBM] * 11,
        out_specs=[HBM] * 9,
        scratch_shapes=[pltpu.VMEM((SIDE, QB_DEV, HALF, PART), bf16)] * 12
        + [pltpu.VMEM((3, 4, SIDE, 8, HALF, PART), bf16)]
        + [pltpu.VMEM((QB_DEV, HALF, D), bf16)]
        + [pltpu.VMEM((D,), jnp.float32)] * 2
        + [pltpu.VMEM((KT, N_PB * QB_DEV), jnp.int32)] * 2
        + [pltpu.VMEM(table, jnp.int32), pltpu.SMEM(table, jnp.int32)]
        + [pltpu.SMEM((KT, N_PB * QB_DEV), jnp.int32), pltpu.SMEM((8, 128), jnp.int32)]
        + [
            pltpu.VMEM((OWN, D), bf16),
            pltpu.VMEM((3, 2, D, GRP), bf16),
            pltpu.VMEM((2, OWN, GRP), bf16),
            pltpu.VMEM((4, 2, 2, 2, QBLK, 256), bf16),
        ]
        + [dma((3, 2))] * 4
        + [dma((3, 4, 2))] * 4
        + [dma((3, 4, 4))] * 4
        + [dma((3, 4))]
        + [dma((6,))] * 2
        + [dma((QB_DEV,)), dma((15,))],
        compiler_params=pltpu.CompilerParams(
            collective_id=0, has_side_effects=True, vmem_limit_bytes=62 * MIB
        ),
        name="exchange",
    )(tokens, shift, scale, owners, blocks, *weights)


def block_kernel(count_ref, place_ref, *refs):
    vectors_h = refs[0:4]
    tokens_ref, q_h, mine_h, kv_ref = refs[4:8]
    own_h, other_h = refs[8:13], refs[13:18]
    out_ref = refs[18]
    vectors = refs[19:23]
    x_refs = refs[23:25]
    key_refs = refs[25:27]
    value_refs = refs[27:29]
    tok, queries, mine, att = refs[29:33]
    held = refs[33:38]
    wk, wv, wo, w1, w2 = held
    sem, vsem, gsem = refs[38:]
    gate_a, shift_m, scale_m, gate_m = vectors
    bf16 = jnp.bfloat16

    def row(vector):
        return vector[...].reshape(1, D)

    ha = lax.axis_index("ha")
    tokens_in = pltpu.make_async_copy(
        tokens_ref.at[pl.ds(pl.multiple_of(ha * OWN, OWN), OWN)], tok, vsem.at[4]
    )
    q_in = pltpu.make_async_copy(q_h, queries, vsem.at[5])
    mine_in = pltpu.make_async_copy(mine_h, mine, vsem.at[6])
    small = [pltpu.make_async_copy(vectors_h[i], vectors[i], vsem.at[i]) for i in range(4)]
    loads = []
    for i in range(5):
        loads.append(
            (
                pltpu.make_async_copy(own_h[i], held[i].at[ha], sem.at[i]),
                pltpu.make_async_copy(other_h[i], held[i].at[1 - ha], sem.at[5 + i]),
            )
        )

    def begin(*numbers):
        for i in numbers:
            loads[i][0].start()
            loads[i][1].start()

    def ready(*numbers):
        for i in numbers:
            loads[i][0].wait()
            loads[i][1].wait()

    def gathers(blk, slot, act):
        for j in range(KT):
            for p in range(3):
                act(
                    pltpu.make_async_copy(
                        kv_ref.at[p, :, place_ref[p, blk * KT + j]],
                        x_refs[slot].at[j, :, :, pl.ds(p * PART, PART)],
                        gsem.at[slot, j, p],
                    )
                )

    begin(0, 1)
    gathers(0, 0, lambda c: c.start())
    mine_in.start()

    lane = lax.broadcasted_iota(jnp.int32, (QBLK, 256), 1)

    def project(blk, slot):
        x = x_refs[slot][...].reshape(KT * QBLK, D)
        live = count_ref[ha * 4 + blk] * QBLK
        place = lax.broadcasted_iota(jnp.int32, (KT * QBLK, 128), 0)
        bias = jnp.where(place < live, 0.0, DEAD).astype(bf16)
        for g in range(2):
            k = jnp.dot(x, wk[g], preferred_element_type=jnp.float32).astype(bf16)
            v = jnp.dot(x, wv[g], preferred_element_type=jnp.float32).astype(bf16)
            for w, (lo, _, spare) in enumerate(WINDOWS):
                key_refs[slot][g, w, QBLK:, :] = with_lane(k[:, lo : lo + 256], spare, bias)
                value_refs[slot][g, w, QBLK:, :] = with_lane(v[:, lo : lo + 256], spare, jnp.ones_like(bias))
                key_refs[slot][g, w, :QBLK, :] = mine[blk, g, w, 0]
                value_refs[slot][g, w, :QBLK, :] = mine[blk, g, w, 1]

    def attend(blk, slot):
        base = pl.multiple_of(blk * QBLK, QBLK)
        for g in range(2):
            parts = []
            for w, (lo, heads, spare) in enumerate(WINDOWS):
                q = queries[g, pl.ds(base, QBLK), lo : lo + 256]
                masks = [(lane >= h * HDIM - lo) & (lane < (h + 1) * HDIM - lo) for h in heads]
                fixed = jnp.where(lane == spare, jnp.ones_like(q), jnp.zeros_like(q))
                stacked = jnp.concatenate([jnp.where(m, q, fixed) for m in masks], 0)
                scores = lax.dot_general(
                    stacked, key_refs[slot][g, w], (((1,), (1,)), ((), ())), preferred_element_type=jnp.float32
                )
                top = jnp.max(scores, -1, keepdims=True)
                weights = jnp.exp2(scores - top).astype(bf16)
                outs = jnp.dot(weights, value_refs[slot][g, w], preferred_element_type=jnp.float32)
                totals = outs[:, spare : spare + 1]
                above = jnp.zeros((QBLK, 256), jnp.float32)
                below = jnp.ones((QBLK, 256), jnp.float32)
                for i, m in enumerate(masks):
                    rows = slice(i * QBLK, (i + 1) * QBLK)
                    above = jnp.where(m, outs[rows], above)
                    below = jnp.where(m, totals[rows], below)
                parts.append(above / below)
            middle = jnp.where(lane[:, :128] + 128 < 5 * HDIM, parts[0][:, 128:], parts[1][:, :128])
            att[g, pl.ds(base, QBLK), :] = jnp.concatenate(
                [parts[0][:, :128], middle, parts[1][:, 128:]], 1
            ).astype(bf16)

    ready(0, 1)
    mine_in.wait()
    gathers(0, 0, lambda c: c.wait())
    q_in.start()
    gathers(1, 1, lambda c: c.start())
    for copy in small:
        copy.start()
    tokens_in.start()
    begin(2, 3, 4)
    project(0, 0)
    q_in.wait()
    for blk in range(4):
        slot = blk % 2
        if blk < 2:
            gathers(blk + 2, slot, lambda c: c.start())
        if blk < 3:
            gathers(blk + 1, 1 - slot, lambda c: c.wait())
            project(blk + 1, 1 - slot)
        attend(blk, slot)

    for copy in small:
        copy.wait()
    tokens_in.wait()
    ready(2)
    projected = jnp.dot(att[0], wo[0], preferred_element_type=jnp.float32)
    projected += jnp.dot(att[1], wo[1], preferred_element_type=jnp.float32)
    residual = (tok[...].astype(jnp.float32) + row(gate_a) * projected).astype(bf16)
    normed = modulate(residual.astype(jnp.float32), row(shift_m), row(scale_m)).astype(bf16)
    ready(3, 4)
    expanded = jnp.zeros((OWN, D), jnp.float32)
    for g in range(2):
        for lo in range(0, FF // 2, CHUNK):
            hidden = jnp.dot(normed, w1[g, :, lo : lo + CHUNK], preferred_element_type=jnp.float32)
            hidden = jax.nn.gelu(hidden, approximate=True).astype(bf16)
            expanded += jnp.dot(hidden, w2[g, lo : lo + CHUNK, :], preferred_element_type=jnp.float32)
    out_ref[...] = (residual.astype(jnp.float32) + row(gate_m) * expanded).astype(bf16)


def block(counts, places, vectors, tokens, queries, mine, kv, own, other):
    bf16 = jnp.bfloat16
    dma = pltpu.SemaphoreType.DMA
    kv = kv.reshape(3, 2, N_PB * 2, HALF, PART)
    return pl.pallas_call(
        block_kernel,
        out_shape=jax.ShapeDtypeStruct((OWN, D), bf16),
        in_specs=[pl.BlockSpec(memory_space=pltpu.SMEM)] * 2 + [HBM] * 18,
        out_specs=pl.BlockSpec(memory_space=pltpu.VMEM),
        scratch_shapes=[pltpu.VMEM((D,), jnp.float32)] * 4
        + [pltpu.VMEM((KT, 2, HALF, D), bf16)] * 2
        + [pltpu.VMEM((2, 2, ROWS, 256), bf16)] * 4
        + [
            pltpu.VMEM((OWN, D), bf16),
            pltpu.VMEM((2, OWN, GRP), bf16),
            pltpu.VMEM((4, 2, 2, 2, QBLK, 256), bf16),
            pltpu.VMEM((2, OWN, GRP), bf16),
        ]
        + [pltpu.VMEM((2,) + w.shape, bf16) for w in own]
        + [dma((10,)), dma((7,)), dma((2, KT, 3))],
        compiler_params=pltpu.CompilerParams(vmem_limit_bytes=62 * MIB),
        name="block",
    )(counts, places, *vectors, tokens, queries, mine, kv, *own, *other)


def shards(
    tokens,
    shift_attn,
    scale_attn,
    gate_attn,
    shift_mlp,
    scale_mlp,
    gate_mlp,
    w_query,
    w_key,
    w_value,
    w_out,
    w_fc1,
    w_fc2,
    contact_owner,
    contact_local,
    contact_count,
):
    vectors = (gate_attn, shift_mlp, scale_mlp, gate_mlp)
    own = (w_query, w_key, w_value, w_out, w_fc1, w_fc2)
    owners, blocks = contact_owner.T, contact_local.T
    kv, places, queries, mine, *other = exchange(tokens, shift_attn, scale_attn, owners, blocks, own)
    return block(contact_count, places, vectors, tokens, queries, mine, kv, own[1:], other)


def solution(mesh):
    placed = (
        P("pb", None),
        P(),
        P(),
        P(),
        P(),
        P(),
        P(),
        P(None, "ha"),
        P(None, "ha"),
        P(None, "ha"),
        P("ha", None),
        P(None, "ha"),
        P("ha", None),
        P(),
        P(),
        P("pb"),
    )
    return jax.shard_map(
        shards, mesh=mesh, in_specs=placed, out_specs=P(("pb", "ha"), None), check_vma=False
    )
```

```python
import jax
import jax.numpy as jnp
from jax import lax
from jax.experimental import pallas as pl
from jax.experimental.pallas import tpu as pltpu
from jax.sharding import PartitionSpec as P

D = 768
HEADS = 16
HDIM = 48
FF = 3072
QBLK = 128
KT = 8
QB_DEV = 8
N_PB = 64
SIDE = 4
HALF = QBLK // 2
PART = D // 3
GRP = D // 2
MIB = 2**20
MESH = pl.DeviceIdType.MESH

ORDERS = ((2, 1, 0), (1, 0, 2), (0, 2, 1))
STRIDES = (16, 4, 1)
OFFS = (0, 1, 3, 2)

epsilon = 1e-06


def modulate(stream, shift, scale):
    center = stream - jnp.mean(stream, -1, keepdims=True)
    spread = jnp.mean(center * center, -1, keepdims=True)
    return center * lax.rsqrt(spread + epsilon) * (1.0 + scale) + shift


ROWS = KT * QBLK
OWN = 4 * QBLK
SHARP = HDIM**-0.5 * 1.4426950408889634
WINDOWS = ((0, (0, 1, 2, 3, 4), 255), (128, (5, 6, 7), 0))
CHUNK = 512
DEAD = -1e30


def with_lane(value, lane, fill):
    at = lax.broadcasted_iota(jnp.int32, (value.shape[0], 128), 1)
    left, right = value[:, :128], value[:, 128:]
    if lane == 0:
        left = jnp.where(at == 0, fill, left)
    else:
        right = jnp.where(at == 127, fill, right)
    return jnp.concatenate([left, right], 1)


def attend_windows(q, keys, values, biased):
    lane = lax.broadcasted_iota(jnp.int32, (QBLK, 256), 1)
    found = []
    for w, (lo, heads, spare) in enumerate(WINDOWS):
        q_part = q[:, lo : lo + 256]
        masks = [(lane >= h * HDIM - lo) & (lane < (h + 1) * HDIM - lo) for h in heads]
        fixed = jnp.zeros_like(q_part)
        if biased:
            fixed = jnp.where(lane == spare, jnp.ones_like(q_part), fixed)
        stacked = jnp.concatenate([jnp.where(m, q_part, fixed) for m in masks], 0)
        scores = lax.dot_general(
            stacked, keys[w], (((1,), (1,)), ((), ())), preferred_element_type=jnp.float32
        )
        top = jnp.max(scores, -1, keepdims=True)
        weights = jnp.exp2(scores - top).astype(jnp.bfloat16)
        outs = jnp.dot(weights, values[w], preferred_element_type=jnp.float32)
        totals = outs[:, spare : spare + 1]
        above = jnp.zeros((QBLK, 256), jnp.float32)
        below = jnp.ones((QBLK, 256), jnp.float32)
        tops = jnp.zeros((QBLK, 256), jnp.float32)
        for i, m in enumerate(masks):
            rows = slice(i * QBLK, (i + 1) * QBLK)
            above = jnp.where(m, outs[rows], above)
            below = jnp.where(m, totals[rows], below)
            tops = jnp.where(m, top[rows], tops)
        found.append((above, below, tops))
    use_first = lane[:, :128] + 128 < 5 * HDIM
    return [
        jnp.concatenate([one[:, :128], jnp.where(use_first, one[:, 128:], two[:, :128]), two[:, 128:]], 1)
        for one, two in zip(*found)
    ]


def exchange_kernel(tokens_ref, shift_ref, scale_ref, owner_ref, block_ref, *refs):
    w_in = refs[0:6]
    kv_ref, place_out, q_out, part_out, log_out = refs[6:11]
    w_out = refs[11:16]
    rows = [refs[16 + 4 * p : 20 + 4 * p] for p in range(3)]
    picked = refs[28]
    tok, shift, scale, owners, blocks, table, sel_ref, owner_s, places = refs[29:38]
    own, qkv_w, queries, mine, partial, logs = refs[38:44]
    (a_s, a_r, af_s, af_r, b_s, b_r, bf_s, bf_r, c_s, c_r, x_s, x_r, l_s, w_s, w_r, t_s, v_s) = refs[44:]

    pb = lax.axis_index("pb")
    ha = lax.axis_index("ha")
    me = (pb // 16, (pb // 4) % 4, pb % 4)

    def moved(base, axis, off):
        return base + (lax.rem(me[axis] + off, SIDE) - me[axis]) * STRIDES[axis]

    def chip(axis, off):
        return {"pb": moved(pb, axis, off), "ha": ha}

    other = {"pb": pb, "ha": 1 - ha}

    def remote(src, dst, ssem, rsem, dev):
        return pltpu.make_async_remote_copy(
            src_ref=src, dst_ref=dst, send_sem=ssem, recv_sem=rsem, device_id=dev, device_id_type=MESH
        )

    half_rows = [
        pltpu.make_async_copy(
            tokens_ref.at[pl.ds(pl.multiple_of(t * QBLK + ha * HALF, HALF), HALF)], tok.at[t], t_s.at[t]
        )
        for t in range(QB_DEV)
    ]
    small = [
        pltpu.make_async_copy(src, dst, v_s.at[i])
        for i, (src, dst) in enumerate(
            (
                (shift_ref, shift),
                (scale_ref, scale),
                (owner_ref, owners),
                (block_ref, blocks),
                (owner_ref, owner_s),
                (tokens_ref.at[pl.ds(pl.multiple_of(ha * OWN, OWN), OWN)], own),
                (w_in[0], qkv_w.at[0, ha]),
                (w_in[1], qkv_w.at[1, ha]),
                (w_in[2], qkv_w.at[2, ha]),
            )
        )
    ]
    for copy in small[:2] + half_rows + small[2:]:
        copy.start()

    barrier = pltpu.get_barrier_semaphore()
    for axis in range(3):
        for off in (1, 2, 3):
            pl.semaphore_signal(barrier, 1, device_id=chip(axis, off), device_id_type=MESH)
    pl.semaphore_signal(barrier, 1, device_id=other, device_id_type=MESH)
    small[0].wait()
    small[1].wait()
    def norm_tile(t):
        half_rows[t].wait()
        n = modulate(tok[t].astype(jnp.float32), shift[...].reshape(1, D), scale[...].reshape(1, D))
        n = n.astype(jnp.bfloat16)
        for p in range(3):
            rows[p][0][0, t] = n[:, p * PART : (p + 1) * PART]

    for t in range(4):
        norm_tile(t)
    pl.semaphore_wait(barrier, 10)

    started = []

    def go(copy):
        copy.start()
        started.append(copy)

    local = []

    def send_a(p, d, h):
        a = ORDERS[p][0]
        part = pl.ds(4 * h, 4)
        return remote(
            rows[p][0].at[0, part],
            rows[p][0].at[3 if d == 0 else 1, part],
            a_s.at[p, d, h],
            a_r.at[p, d, h],
            chip(a, 1 if d == 0 else 3),
        )

    def forward_a(p, d):
        a = ORDERS[p][0]
        part = pl.ds(4 * d, 4)
        return remote(
            rows[p][0].at[3 if d == 0 else 1, part],
            rows[p][0].at[2, part],
            af_s.at[p, d],
            af_r.at[p, d],
            chip(a, 1 if d == 0 else 3),
        )

    def send_b(p, da, d):
        b = ORDERS[p][1]
        return remote(
            rows[p][0].at[da],
            rows[p][3 if d == 0 else 1].at[da],
            b_s.at[p, da, d],
            b_r.at[p, da, d],
            chip(b, 1 if d == 0 else 3),
        )

    def forward_b(p, da, d):
        b = ORDERS[p][1]
        part = pl.ds(4 * d, 4)
        return remote(
            rows[p][3 if d == 0 else 1].at[da, part],
            rows[p][2].at[da, part],
            bf_s.at[p, da, d],
            bf_r.at[p, da, d],
            chip(b, 1 if d == 0 else 3),
        )

    def send_c(p, db, g):
        c = ORDERS[p][2]
        off = OFFS[g]
        return remote(
            picked.at[p, g, db],
            kv_ref.at[p, 0, SIDE - off, db],
            c_s.at[p, db, g],
            c_r.at[p, db, g],
            chip(c, off),
        )

    def cross(p, db, g):
        src = picked.at[p, 0, db] if g == 0 else kv_ref.at[p, 0, SIDE - OFFS[g], db]
        return remote(
            src, kv_ref.at[p, 1, (SIDE - OFFS[g]) % SIDE, db], x_s.at[p, db, g], x_r.at[p, db, g], other
        )

    def keep(p, db):
        return pltpu.make_async_copy(picked.at[p, 0, db], kv_ref.at[p, 0, 0, db], l_s.at[p, db])

    def select(p, db):
        a, b, c = ORDERS[p]
        for g in range(4):
            dest = moved(pb, c, OFFS[g])

            def pick(j, carry):
                da, k = j // 2, j % 2
                owner = moved(moved(pb, b, db), a, da)
                code = sel_ref[owner, dest * QB_DEV]
                number = jnp.where(k == 0, code & 7, (code >> 9) & 7)
                picked[p, g, db, j] = rows[p][db][da, number]
                return carry

            lax.fori_loop(0, 8, pick, 0)
        for g in (3, 1, 2):
            go(send_c(p, db, g))
        local.append(keep(p, db))
        local[-1].start()
        go(cross(p, db, 0))

    def relay(p, db):
        for g in (1, 2, 3):
            send_c(p, db, g).wait_recv()
            go(cross(p, db, g))

    for h in range(2):
        if h == 1:
            for t in range(4, QB_DEV):
                norm_tile(t)
        for p in range(3):
            for d in range(2):
                go(send_a(p, d, h))
    for p in range(3):
        for d in range(2):
            go(send_b(p, 0, d))
    weights = [
        remote(w_in[i], qkv_w.at[i, ha] if i < 3 else w_out[i - 1], w_s.at[i], w_r.at[i], other)
        for i in range(6)
    ]
    for copy in weights:
        go(copy)

    small[2].wait()
    small[3].wait()
    lane = lax.broadcasted_iota(jnp.int32, (KT, N_PB * QB_DEV), 1)
    order = (lane & 7) * KT + lax.broadcasted_iota(jnp.int32, (KT, N_PB * QB_DEV), 0)
    code = order * 8 + blocks[...]
    size = N_PB * QB_DEV

    def tabulate(o, carry):
        hit = owners[...] == o
        first = jnp.where(hit, code, 511)
        last = jnp.where(hit, code, 0)
        for step in (1, 2, 4):
            first = jnp.minimum(first, pltpu.roll(first, size - step, 1))
            last = jnp.maximum(last, pltpu.roll(last, size - step, 1))
        first = jnp.min(first, 0, keepdims=True)
        last = jnp.max(last, 0, keepdims=True)
        table[pl.ds(o, 1), :] = first + (last & 7) * 512
        return carry

    lax.fori_loop(0, N_PB, tabulate, 0)
    to_scalars = pltpu.make_async_copy(table, sel_ref, v_s.at[9])
    to_scalars.start()

    def keep_local(src, dst, number):
        local.append(pltpu.make_async_copy(src, dst, v_s.at[number]))
        local[-1].start()

    def place_entry(e, carry):
        i, j = e // KT, e % KT
        owner = owner_s[j, pb * QB_DEV + ha * 4 + i]
        first = (sel_ref[owner, pb * QB_DEV] & 511) >> 3
        k = jnp.where(first == ha * 4 * KT + e, 0, 1)
        rel = ((owner // 16 - me[0]) & 3, (owner // 4 - me[1]) & 3, (owner - me[2]) & 3)
        for p in range(3):
            a, b, c = ORDERS[p]
            places[p, e] = ((rel[c] * 4 + rel[b]) * 4 + rel[a]) * 2 + k
        return carry

    def own_blocks():
        small[5].wait()
        normed = modulate(own[...].astype(jnp.float32), shift[...].reshape(1, D), scale[...].reshape(1, D))
        own[...] = normed.astype(jnp.bfloat16)
        for i in range(3):
            small[6 + i].wait()
            remote(w_in[i], qkv_w.at[i, 1 - ha], w_s.at[i], w_r.at[i], other).wait_recv()
        keep_local(qkv_w.at[1, 1 - ha], w_out[0], 10)
        keep_local(qkv_w.at[2, 1 - ha], w_out[1], 11)

        def one_group(g, carry):
            def product(i):
                return jnp.dot(own[...], qkv_w[i, g], preferred_element_type=jnp.float32)

            queries[g] = (product(0) * SHARP).astype(jnp.bfloat16)
            for i in range(2):
                result = product(1 + i).astype(jnp.bfloat16)
                for w, (lo, _, spare) in enumerate(WINDOWS):
                    window = result[:, lo : lo + 256]
                    if i == 1:
                        window = with_lane(window, spare, jnp.ones((OWN, 128), jnp.bfloat16))
                    mine[g, w, i] = window
            return carry

        lax.fori_loop(0, 2, one_group, 0)
        keep_local(queries, q_out, 12)
        lax.fori_loop(0, 4 * KT, place_entry, 0)
        keep_local(places, place_out, 14)

    def own_attention():
        def one_block(i, carry):
            g = i // 4
            at = pl.ds(pl.multiple_of((i % 4) * QBLK, QBLK), QBLK)
            above, below, tops = attend_windows(
                queries[g, at, :], [mine[g, w, 0, at, :] for w in range(2)], [mine[g, w, 1, at, :] for w in range(2)], False
            )
            partial[g, at, :] = above / below
            logs[g, at, :] = tops + jnp.log2(below)
            return carry

        lax.fori_loop(0, 8, one_block, 0)
        keep_local(partial, part_out, 13)
        keep_local(logs, log_out, 15)

    for p in range(3):
        for d in range(2):
            send_a(p, d, d).wait_recv()
            go(forward_a(p, d))
        for d in range(2):
            send_a(p, d, 1 - d).wait_recv()
        for d in range(2):
            for da in (3, 1):
                go(send_b(p, da, d))
    for p in range(3):
        for d in range(2):
            forward_a(p, d).wait_recv()
        for d in range(2):
            go(send_b(p, 2, d))
    to_scalars.wait()
    small[4].wait()
    for p in range(3):
        select(p, 0)
    own_blocks()
    for da in (0, 3, 1, 2):
        for p in range(3):
            for d in range(2):
                send_b(p, da, d).wait_recv()
                go(forward_b(p, da, d))
    for p in range(3):
        for db in (3, 1):
            select(p, db)
    own_attention()
    for p in range(3):
        relay(p, 0)
    for p in range(3):
        for da in (0, 3, 1, 2):
            for d in range(2):
                forward_b(p, da, d).wait_recv()
        select(p, 2)
    for db in (3, 1, 2):
        for p in range(3):
            relay(p, db)
    for p in range(3):
        for db in range(4):
            for g in range(4):
                cross(p, db, g).wait_recv()
    for copy in weights[3:]:
        copy.wait_recv()
    for copy in started:
        copy.wait_send()
    for copy in local:
        copy.wait()


HBM = pl.BlockSpec(memory_space=pltpu.HBM)


def exchange(tokens, shift, scale, owners, blocks, weights):
    dma = pltpu.SemaphoreType.DMA
    bf16 = jnp.bfloat16
    kv_shape = jax.ShapeDtypeStruct((3, 2, SIDE, SIDE, 8, HALF, PART), bf16)
    table = (N_PB, N_PB * QB_DEV)
    return pl.pallas_call(
        exchange_kernel,
        out_shape=[
            kv_shape,
            jax.ShapeDtypeStruct((8, 128), jnp.int32),
            jax.ShapeDtypeStruct((2, OWN, GRP), bf16),
            jax.ShapeDtypeStruct((2, OWN, GRP), jnp.float32),
            jax.ShapeDtypeStruct((2, OWN, GRP), jnp.float32),
        ]
        + [jax.ShapeDtypeStruct(w.shape, w.dtype) for w in weights[1:]],
        in_specs=[HBM] * 11,
        out_specs=[HBM] * 10,
        scratch_shapes=[pltpu.VMEM((SIDE, QB_DEV, HALF, PART), bf16)] * 12
        + [pltpu.VMEM((3, 4, SIDE, 8, HALF, PART), bf16)]
        + [pltpu.VMEM((QB_DEV, HALF, D), bf16)]
        + [pltpu.VMEM((D,), jnp.float32)] * 2
        + [pltpu.VMEM((KT, N_PB * QB_DEV), jnp.int32)] * 2
        + [pltpu.VMEM(table, jnp.int32), pltpu.SMEM(table, jnp.int32)]
        + [pltpu.SMEM((KT, N_PB * QB_DEV), jnp.int32), pltpu.SMEM((8, 128), jnp.int32)]
        + [
            pltpu.VMEM((OWN, D), bf16),
            pltpu.VMEM((3, 2, D, GRP), bf16),
            pltpu.VMEM((2, OWN, GRP), bf16),
            pltpu.VMEM((2, 2, 2, OWN, 256), bf16),
            pltpu.VMEM((2, OWN, GRP), jnp.float32),
            pltpu.VMEM((2, OWN, GRP), jnp.float32),
        ]
        + [dma((3, 2, 2))] * 2
        + [dma((3, 2))] * 2
        + [dma((3, 4, 2))] * 4
        + [dma((3, 4, 4))] * 4
        + [dma((3, 4))]
        + [dma((6,))] * 2
        + [dma((QB_DEV,)), dma((16,))],
        compiler_params=pltpu.CompilerParams(
            collective_id=0, has_side_effects=True, vmem_limit_bytes=62 * MIB
        ),
        name="exchange",
    )(tokens, shift, scale, owners, blocks, *weights)


def block_kernel(count_ref, place_ref, *refs):
    vectors_h = refs[0:4]
    tokens_ref, q_h, part_h, log_h, kv_ref = refs[4:9]
    own_h, other_h = refs[9:14], refs[14:19]
    out_ref = refs[19]
    vectors = refs[20:24]
    x_refs = refs[24:26]
    key_refs = refs[26:28]
    value_refs = refs[28:30]
    tok, queries, partial, logs, att = refs[30:35]
    wkv, wo, w1, w2 = refs[35:39]
    sem, vsem, gsem = refs[39:]
    gate_a, shift_m, scale_m, gate_m = vectors
    bf16 = jnp.bfloat16

    def row(vector):
        return vector[...].reshape(1, D)

    ha = lax.axis_index("ha")
    late = [
        pltpu.make_async_copy(src, dst, vsem.at[i])
        for i, (src, dst) in enumerate(
            [(vectors_h[i], vectors[i]) for i in range(4)]
            + [(tokens_ref.at[pl.ds(pl.multiple_of(ha * OWN, OWN), OWN)], tok)]
        )
    ]
    early = [
        pltpu.make_async_copy(src, dst, vsem.at[5 + i])
        for i, (src, dst) in enumerate(((q_h, queries), (part_h, partial), (log_h, logs)))
    ]
    loads = []
    for i in range(5):
        pair = []
        for src, at, number in ((own_h[i], ha, i), (other_h[i], 1 - ha, 5 + i)):
            if i < 2:
                dst = wkv.at[at, :, pl.ds(i * GRP, GRP)]
            elif i == 2:
                dst = wo.at[pl.ds(pl.multiple_of(at * GRP, GRP), GRP)]
            else:
                dst = (w1, w2)[i - 3].at[at]
            pair.append(pltpu.make_async_copy(src, dst, sem.at[number]))
        loads.append(pair)

    def begin(*numbers):
        for i in numbers:
            loads[i][0].start()
            loads[i][1].start()

    def ready(*numbers):
        for i in numbers:
            loads[i][0].wait()
            loads[i][1].wait()

    def gathers(blk, slot, act):
        for j in range(KT):
            for p in range(3):
                act(
                    pltpu.make_async_copy(
                        kv_ref.at[p, :, place_ref[p, blk * KT + j]],
                        x_refs[slot].at[j, :, :, pl.ds(p * PART, PART)],
                        gsem.at[slot, j, p],
                    )
                )

    def project(blk, slot):
        x = x_refs[slot][...].reshape(ROWS, D)
        live = count_ref[ha * 4 + blk] * QBLK
        place = lax.broadcasted_iota(jnp.int32, (ROWS, 128), 0)
        bias = jnp.where(place < live, 0.0, DEAD).astype(bf16)
        for g in range(2):
            both = jnp.dot(x, wkv[g], preferred_element_type=jnp.float32).astype(bf16)
            k, v = both[:, :GRP], both[:, GRP:]
            for w, (lo, _, spare) in enumerate(WINDOWS):
                key_refs[slot][g, w] = with_lane(k[:, lo : lo + 256], spare, bias)
                value_refs[slot][g, w] = with_lane(v[:, lo : lo + 256], spare, jnp.ones_like(bias))

    def attend(blk, slot):
        at = slice(blk * QBLK, (blk + 1) * QBLK)
        for g in range(2):
            above, below, tops = attend_windows(
                queries[g, at, :],
                [key_refs[slot].at[g, w][...] for w in range(2)],
                [value_refs[slot].at[g, w][...] for w in range(2)],
                True,
            )
            log = logs[g, at, :]
            most = jnp.maximum(tops, log)
            listed, mine = jnp.exp2(tops - most), jnp.exp2(log - most)
            result = (above * listed + partial[g, at, :] * mine) / (below * listed + mine)
            att[at, g * GRP : (g + 1) * GRP] = result.astype(bf16)

    begin(0, 1)
    gathers(0, 0, lambda c: c.start())
    ready(0, 1)
    gathers(0, 0, lambda c: c.wait())
    for copy in early:
        copy.start()
    gathers(1, 1, lambda c: c.start())
    for copy in late:
        copy.start()
    begin(2, 3, 4)
    project(0, 0)
    for copy in early:
        copy.wait()
    for blk in range(4):
        slot = blk % 2
        if blk < 2:
            gathers(blk + 2, slot, lambda c: c.start())
        if blk < 3:
            gathers(blk + 1, 1 - slot, lambda c: c.wait())
            project(blk + 1, 1 - slot)
        attend(blk, slot)

    for copy in late:
        copy.wait()
    ready(2)
    projected = jnp.dot(att[...], wo[...], preferred_element_type=jnp.float32)
    residual = (tok[...].astype(jnp.float32) + row(gate_a) * projected).astype(bf16)
    normed = modulate(residual.astype(jnp.float32), row(shift_m), row(scale_m)).astype(bf16)
    ready(3, 4)
    expanded = jnp.zeros((OWN, D), jnp.float32)
    for g in range(2):
        for lo in range(0, FF // 2, CHUNK):
            hidden = jnp.dot(normed, w1[g, :, lo : lo + CHUNK], preferred_element_type=jnp.float32)
            hidden = jax.nn.gelu(hidden, approximate=True).astype(bf16)
            expanded += jnp.dot(hidden, w2[g, lo : lo + CHUNK, :], preferred_element_type=jnp.float32)
    out_ref[...] = (residual.astype(jnp.float32) + row(gate_m) * expanded).astype(bf16)


def block(counts, places, vectors, tokens, queries, partial, logs, kv, own, other):
    bf16 = jnp.bfloat16
    dma = pltpu.SemaphoreType.DMA
    kv = kv.reshape(3, 2, N_PB * 2, HALF, PART)
    return pl.pallas_call(
        block_kernel,
        out_shape=jax.ShapeDtypeStruct((OWN, D), bf16),
        in_specs=[pl.BlockSpec(memory_space=pltpu.SMEM)] * 2 + [HBM] * 19,
        out_specs=pl.BlockSpec(memory_space=pltpu.VMEM),
        scratch_shapes=[pltpu.VMEM((D,), jnp.float32)] * 4
        + [pltpu.VMEM((KT, 2, HALF, D), bf16)] * 2
        + [pltpu.VMEM((2, 2, ROWS, 256), bf16)] * 4
        + [
            pltpu.VMEM((OWN, D), bf16),
            pltpu.VMEM((2, OWN, GRP), bf16),
            pltpu.VMEM((2, OWN, GRP), jnp.float32),
            pltpu.VMEM((2, OWN, GRP), jnp.float32),
            pltpu.VMEM((OWN, D), bf16),
            pltpu.VMEM((2, D, 2 * GRP), bf16),
            pltpu.VMEM((D, D), bf16),
            pltpu.VMEM((2, D, FF // 2), bf16),
            pltpu.VMEM((2, FF // 2, D), bf16),
        ]
        + [dma((10,)), dma((8,)), dma((2, KT, 3))],
        compiler_params=pltpu.CompilerParams(vmem_limit_bytes=62 * MIB),
        name="block",
    )(counts, places, *vectors, tokens, queries, partial, logs, kv, *own, *other)


def shards(
    tokens,
    shift_attn,
    scale_attn,
    gate_attn,
    shift_mlp,
    scale_mlp,
    gate_mlp,
    w_query,
    w_key,
    w_value,
    w_out,
    w_fc1,
    w_fc2,
    contact_owner,
    contact_local,
    contact_count,
):
    vectors = (gate_attn, shift_mlp, scale_mlp, gate_mlp)
    own = (w_query, w_key, w_value, w_out, w_fc1, w_fc2)
    owners, blocks = contact_owner.T, contact_local.T
    kv, places, queries, partial, logs, *other = exchange(tokens, shift_attn, scale_attn, owners, blocks, own)
    return block(contact_count, places, vectors, tokens, queries, partial, logs, kv, own[1:], other)


def solution(mesh):
    placed = (
        P("pb", None),
        P(),
        P(),
        P(),
        P(),
        P(),
        P(),
        P(None, "ha"),
        P(None, "ha"),
        P(None, "ha"),
        P("ha", None),
        P(None, "ha"),
        P("ha", None),
        P(),
        P(),
        P("pb"),
    )
    return jax.shard_map(
        shards, mesh=mesh, in_specs=placed, out_specs=P(("pb", "ha"), None), check_vma=False
    )
```

```python
import jax
import jax.numpy as jnp
from jax import lax
from jax.experimental import pallas as pl
from jax.experimental.pallas import tpu as pltpu
from jax.sharding import PartitionSpec as P

D = 768
HEADS = 16
HDIM = 48
FF = 3072
QBLK = 128
KT = 8
QB_DEV = 8
N_PB = 64
SIDE = 4
HALF = QBLK // 2
PART = D // 3
GRP = D // 2
MIB = 2**20
MESH = pl.DeviceIdType.MESH

ORDERS = ((2, 1, 0), (1, 0, 2), (0, 2, 1))
STRIDES = (16, 4, 1)
OFFS = (0, 1, 3, 2)

epsilon = 1e-06


def modulate(stream, shift, scale):
    center = stream - jnp.mean(stream, -1, keepdims=True)
    spread = jnp.mean(center * center, -1, keepdims=True)
    return center * lax.rsqrt(spread + epsilon) * (1.0 + scale) + shift


ROWS = KT * QBLK
OWN = 4 * QBLK
SHARP = HDIM**-0.5 * 1.4426950408889634
WINDOWS = ((0, (0, 1, 2, 3, 4), 255), (128, (5, 6, 7), 0))
CHUNK = 512
DEAD = -1e30


def with_lane(value, lane, fill):
    at = lax.broadcasted_iota(jnp.int32, (value.shape[0], 128), 1)
    left, right = value[:, :128], value[:, 128:]
    if lane == 0:
        left = jnp.where(at == 0, fill, left)
    else:
        right = jnp.where(at == 127, fill, right)
    return jnp.concatenate([left, right], 1)


def attend_windows(q, keys, values, biased):
    lane = lax.broadcasted_iota(jnp.int32, (QBLK, 256), 1)
    found = []
    for w, (lo, heads, spare) in enumerate(WINDOWS):
        q_part = q[:, lo : lo + 256]
        masks = [(lane >= h * HDIM - lo) & (lane < (h + 1) * HDIM - lo) for h in heads]
        fixed = jnp.zeros_like(q_part)
        if biased:
            fixed = jnp.where(lane == spare, jnp.ones_like(q_part), fixed)
        stacked = jnp.concatenate([jnp.where(m, q_part, fixed) for m in masks], 0)
        scores = lax.dot_general(
            stacked, keys[w], (((1,), (1,)), ((), ())), preferred_element_type=jnp.float32
        )
        top = jnp.max(scores, -1, keepdims=True)
        weights = jnp.exp2(scores - top).astype(jnp.bfloat16)
        outs = jnp.dot(weights, values[w], preferred_element_type=jnp.float32)
        totals = outs[:, spare : spare + 1]
        above = jnp.zeros((QBLK, 256), jnp.float32)
        below = jnp.ones((QBLK, 256), jnp.float32)
        tops = jnp.zeros((QBLK, 256), jnp.float32)
        for i, m in enumerate(masks):
            rows = slice(i * QBLK, (i + 1) * QBLK)
            above = jnp.where(m, outs[rows], above)
            below = jnp.where(m, totals[rows], below)
            tops = jnp.where(m, top[rows], tops)
        found.append((above, below, tops))
    use_first = lane[:, :128] + 128 < 5 * HDIM
    return [
        jnp.concatenate([one[:, :128], jnp.where(use_first, one[:, 128:], two[:, :128]), two[:, 128:]], 1)
        for one, two in zip(*found)
    ]


def exchange_kernel(tokens_ref, shift_ref, scale_ref, owner_ref, block_ref, *refs):
    w_in = refs[0:6]
    kv_ref, place_out, q_out, part_out, log_out = refs[6:11]
    w_out = refs[11:16]
    rows = [refs[16 + 4 * p : 20 + 4 * p] for p in range(3)]
    picked = refs[28]
    tok, shift, scale, owners, blocks, table, sel_ref, owner_s, places = refs[29:38]
    own, qkv_w, queries, mine, partial, logs = refs[38:44]
    (a_s, a_r, af_s, af_r, b_s, b_r, bf_s, bf_r, c_s, c_r, last_r, x_s, x_r, l_s, w_s, w_r, t_s, v_s) = refs[44:]

    pb = lax.axis_index("pb")
    ha = lax.axis_index("ha")
    me = (pb // 16, (pb // 4) % 4, pb % 4)

    def moved(base, axis, off):
        return base + (lax.rem(me[axis] + off, SIDE) - me[axis]) * STRIDES[axis]

    def chip(axis, off):
        return {"pb": moved(pb, axis, off), "ha": ha}

    other = {"pb": pb, "ha": 1 - ha}

    def remote(src, dst, ssem, rsem, dev):
        return pltpu.make_async_remote_copy(
            src_ref=src, dst_ref=dst, send_sem=ssem, recv_sem=rsem, device_id=dev, device_id_type=MESH
        )

    half_rows = pltpu.make_async_copy(
        tokens_ref.at[:, pl.ds(pl.multiple_of(ha * HALF, HALF), HALF)], tok, t_s
    )
    small = [
        pltpu.make_async_copy(src, dst, v_s.at[i])
        for i, (src, dst) in enumerate(
            (
                (shift_ref, shift),
                (scale_ref, scale),
                (owner_ref, owners),
                (block_ref, blocks),
                (owner_ref, owner_s),
                (tokens_ref.at[pl.ds(ha * 4, 4)], own),
                (w_in[0], qkv_w.at[0, ha]),
                (w_in[1], qkv_w.at[1, ha]),
                (w_in[2], qkv_w.at[2, ha]),
            )
        )
    ]
    for copy in small[:2] + [half_rows] + small[2:]:
        copy.start()

    barrier = pltpu.get_barrier_semaphore()
    for axis in range(3):
        for off in (1, 2, 3):
            pl.semaphore_signal(barrier, 1, device_id=chip(axis, off), device_id_type=MESH)
    pl.semaphore_signal(barrier, 1, device_id=other, device_id_type=MESH)
    small[0].wait()
    small[1].wait()
    half_rows.wait()
    for t in range(QB_DEV):
        n = modulate(tok[t].astype(jnp.float32), shift[...].reshape(1, D), scale[...].reshape(1, D))
        n = n.astype(jnp.bfloat16)
        for p in range(3):
            rows[p][0][0, t] = n[:, p * PART : (p + 1) * PART]
    pl.semaphore_wait(barrier, 10)

    def go(copy):
        copy.start()

    def arrived(ref, semaphore):
        remote(ref, ref, x_s, semaphore, other).wait_recv()

    local = []

    def send_a(p, d):
        a = ORDERS[p][0]
        return remote(
            rows[p][0].at[0],
            rows[p][0].at[3 if d == 0 else 1],
            a_s,
            a_r.at[p, d],
            chip(a, 1 if d == 0 else 3),
        )

    def forward_a(p, d):
        a = ORDERS[p][0]
        part = pl.ds(4 * d, 4)
        return remote(
            rows[p][0].at[3 if d == 0 else 1, part],
            rows[p][0].at[2, part],
            af_s,
            af_r.at[p],
            chip(a, 1 if d == 0 else 3),
        )

    def send_b(p, da, d):
        b = ORDERS[p][1]
        return remote(
            rows[p][0].at[da],
            rows[p][3 if d == 0 else 1].at[da],
            b_s,
            b_r.at[p, da, d],
            chip(b, 1 if d == 0 else 3),
        )

    def forward_b(p, da, d):
        b = ORDERS[p][1]
        part = pl.ds(4 * d, 4)
        return remote(
            rows[p][3 if d == 0 else 1].at[da, part],
            rows[p][2].at[da, part],
            bf_s,
            bf_r.at[p],
            chip(b, 1 if d == 0 else 3),
        )

    def send_c(p, db, g):
        c = ORDERS[p][2]
        off = OFFS[g]
        return remote(
            picked.at[p, g, db],
            kv_ref.at[p, 0, SIDE - off, db],
            c_s,
            last_r.at[p, g - 1] if db == 2 else c_r.at[p, db],
            chip(c, off),
        )

    def cross(p, db, g):
        src = picked.at[p, 0, db] if g == 0 else kv_ref.at[p, 0, SIDE - OFFS[g], db]
        return remote(src, kv_ref.at[p, 1, (SIDE - OFFS[g]) % SIDE, db], x_s, x_r, other)

    def keep(p, db):
        return pltpu.make_async_copy(picked.at[p, 0, db], kv_ref.at[p, 0, 0, db], l_s)

    def select(p, db):
        a, b, c = ORDERS[p]
        for g in range(4):
            dest = moved(pb, c, OFFS[g])

            def pick(j, carry):
                da, k = j // 2, j % 2
                owner = moved(moved(pb, b, db), a, da)
                code = sel_ref[owner, dest * QB_DEV]
                number = jnp.where(k == 0, code & 7, (code >> 9) & 7)
                picked[p, g, db, j] = rows[p][db][da, number]
                return carry

            lax.fori_loop(0, 8, pick, 0)
        for g in (3, 1, 2):
            go(send_c(p, db, g))
        keep(p, db).start()
        go(cross(p, db, 0))

    def relay(p, db, *groups):
        if db != 2:
            arrived(kv_ref.at[p, 0, pl.ds(1, 3), db], c_r.at[p, db])
        for g in groups:
            if db == 2:
                send_c(p, db, g).wait_recv()
            go(cross(p, db, g))

    for p in range(3):
        for d in range(2):
            go(send_a(p, d))
    for p in range(3):
        for d in range(2):
            go(send_b(p, 0, d))
    weights = [
        remote(w_in[i], qkv_w.at[i, ha] if i < 3 else w_out[i - 1], w_s.at[i], w_r.at[i], other)
        for i in range(6)
    ]
    for copy in weights:
        go(copy)

    def keep_local(src, dst, number):
        local.append(pltpu.make_async_copy(src, dst, v_s.at[number]))
        local[-1].start()

    def place_entry(e, carry):
        i, j = e // KT, e % KT
        owner = owner_s[j, pb * QB_DEV + ha * 4 + i]
        first = (sel_ref[owner, pb * QB_DEV] & 511) >> 3
        k = jnp.where(first == ha * 4 * KT + e, 0, 1)
        rel = ((owner // 16 - me[0]) & 3, (owner // 4 - me[1]) & 3, (owner - me[2]) & 3)
        for p in range(3):
            a, b, c = ORDERS[p]
            places[p, e] = ((rel[c] * 4 + rel[b]) * 4 + rel[a]) * 2 + k
        return carry

    def own_blocks():
        small[5].wait()
        stream = own[...].reshape(OWN, D).astype(jnp.float32)
        normed = modulate(stream, shift[...].reshape(1, D), scale[...].reshape(1, D))
        own[...] = normed.astype(jnp.bfloat16).reshape(4, QBLK, D)
        for i in range(3):
            small[6 + i].wait()
            remote(w_in[i], qkv_w.at[i, 1 - ha], w_s.at[i], w_r.at[i], other).wait_recv()
        keep_local(qkv_w.at[1, 1 - ha], w_out[0], 10)
        keep_local(qkv_w.at[2, 1 - ha], w_out[1], 11)

        def one_group(g, carry):
            def product(i):
                return jnp.dot(
                    own[...].reshape(OWN, D), qkv_w[i, g], preferred_element_type=jnp.float32
                )

            queries[g] = (product(0) * SHARP).astype(jnp.bfloat16)
            for i in range(2):
                result = product(1 + i).astype(jnp.bfloat16)
                for w, (lo, _, spare) in enumerate(WINDOWS):
                    window = result[:, lo : lo + 256]
                    if i == 1:
                        window = with_lane(window, spare, jnp.ones((OWN, 128), jnp.bfloat16))
                    mine[g, w, i] = window
            return carry

        lax.fori_loop(0, 2, one_group, 0)
        keep_local(queries, q_out, 12)
        lax.fori_loop(0, 4 * KT, place_entry, 0)
        keep_local(places, place_out, 14)

    def own_attention():
        def one_block(i, carry):
            g = i // 4
            at = pl.ds(pl.multiple_of((i % 4) * QBLK, QBLK), QBLK)
            above, below, tops = attend_windows(
                queries[g, at, :], [mine[g, w, 0, at, :] for w in range(2)], [mine[g, w, 1, at, :] for w in range(2)], False
            )
            partial[g, at, :] = above / below
            logs[g, at, :] = tops + jnp.log2(below)
            return carry

        lax.fori_loop(0, 8, one_block, 0)
        keep_local(partial, part_out, 13)
        keep_local(logs, log_out, 15)

    for p in range(3):
        for d in range(2):
            send_a(p, d).wait_recv()
            go(forward_a(p, d))
        for d in range(2):
            for da in (3, 1):
                go(send_b(p, da, d))
    for p in range(3):
        arrived(rows[p][0].at[2], af_r.at[p])
        for d in range(2):
            go(send_b(p, 2, d))
    small[2].wait()
    small[3].wait()
    lane = lax.broadcasted_iota(jnp.int32, (KT, N_PB * QB_DEV), 1)
    order = (lane & 7) * KT + lax.broadcasted_iota(jnp.int32, (KT, N_PB * QB_DEV), 0)
    code = order * 8 + blocks[...]
    size = N_PB * QB_DEV

    def tabulate(i, carry):
        firsts, lasts = [], []
        for o in range(8):
            hit = owners[...] == i * 8 + o
            firsts.append(jnp.min(jnp.where(hit, code, 511), 0, keepdims=True))
            lasts.append(jnp.max(jnp.where(hit, code, 0), 0, keepdims=True))
        first, last = jnp.concatenate(firsts, 0), jnp.concatenate(lasts, 0)
        for step in (1, 2, 4):
            first = jnp.minimum(first, pltpu.roll(first, size - step, 1))
            last = jnp.maximum(last, pltpu.roll(last, size - step, 1))
        table[pl.ds(pl.multiple_of(i * 8, 8), 8), :] = first + (last & 7) * 512
        return carry

    lax.fori_loop(0, N_PB // 8, tabulate, 0)
    to_scalars = pltpu.make_async_copy(table, sel_ref, v_s.at[9])
    to_scalars.start()

    to_scalars.wait()
    small[4].wait()
    for p in range(3):
        select(p, 0)
    for da in (0, 3, 1, 2):
        for p in range(3):
            for d in range(2):
                send_b(p, da, d).wait_recv()
                go(forward_b(p, da, d))
    for p in range(3):
        for db in (3, 1):
            select(p, db)
    own_blocks()
    own_attention()
    for p in range(3):
        relay(p, 0, 1, 2, 3)
    for p in range(3):
        arrived(rows[p][2], bf_r.at[p])
        select(p, 2)
    for db in (3, 1):
        for p in range(3):
            relay(p, db, 1, 2, 3)
    for g in (3, 1, 2):
        for p in range(3):
            relay(p, 2, g)
    arrived(kv_ref.at[:, 1], x_r)
    for copy in weights[3:]:
        copy.wait_recv()
    for copy in weights:
        copy.wait_send()
    two, one = pl.ds(0, 2), pl.ds(0, 1)
    for ref, semaphore in (
        (kv_ref.at[:, 0, one, two], a_s),
        (kv_ref.at[:, 0, one, one], af_s),
        (kv_ref.at[:, 0, two], b_s),
        (kv_ref.at[:, 0, one], bf_s),
        (kv_ref.at[:, 0, pl.ds(1, 3)], c_s),
        (kv_ref.at[:, 1], x_s),
    ):
        remote(ref, ref, semaphore, x_r, other).wait_send()
    pltpu.make_async_copy(picked.at[:, 0], kv_ref.at[:, 0, 0], l_s).wait()
    for copy in local:
        copy.wait()


HBM = pl.BlockSpec(memory_space=pltpu.HBM)


def exchange(tokens, shift, scale, owners, blocks, weights):
    dma = pltpu.SemaphoreType.DMA
    bf16 = jnp.bfloat16
    kv_shape = jax.ShapeDtypeStruct((3, 2, SIDE, SIDE, 8, HALF, PART), bf16)
    table = (N_PB, N_PB * QB_DEV)
    return pl.pallas_call(
        exchange_kernel,
        out_shape=[
            kv_shape,
            jax.ShapeDtypeStruct((8, 128), jnp.int32),
            jax.ShapeDtypeStruct((2, OWN, GRP), bf16),
            jax.ShapeDtypeStruct((2, OWN, GRP), jnp.float32),
            jax.ShapeDtypeStruct((2, OWN, GRP), jnp.float32),
        ]
        + [jax.ShapeDtypeStruct(w.shape, w.dtype) for w in weights[1:]],
        in_specs=[HBM] * 11,
        out_specs=[HBM] * 10,
        scratch_shapes=[pltpu.VMEM((SIDE, QB_DEV, HALF, PART), bf16)] * 12
        + [pltpu.VMEM((3, 4, SIDE, 8, HALF, PART), bf16)]
        + [pltpu.VMEM((QB_DEV, HALF, D), bf16)]
        + [pltpu.VMEM((D,), jnp.float32)] * 2
        + [pltpu.VMEM((KT, N_PB * QB_DEV), jnp.int32)] * 2
        + [pltpu.VMEM(table, jnp.int32), pltpu.SMEM(table, jnp.int32)]
        + [pltpu.SMEM((KT, N_PB * QB_DEV), jnp.int32), pltpu.SMEM((8, 128), jnp.int32)]
        + [
            pltpu.VMEM((4, QBLK, D), bf16),
            pltpu.VMEM((3, 2, D, GRP), bf16),
            pltpu.VMEM((2, OWN, GRP), bf16),
            pltpu.VMEM((2, 2, 2, OWN, 256), bf16),
            pltpu.VMEM((2, OWN, GRP), jnp.float32),
            pltpu.VMEM((2, OWN, GRP), jnp.float32),
        ]
        + [dma, dma((3, 2)), dma, dma((3,))]
        + [dma, dma((3, 4, 2)), dma, dma((3,))]
        + [dma, dma((3, 4)), dma((3, 3)), dma, dma, dma]
        + [dma((6,)), dma((6,)), dma, dma((16,))],
        compiler_params=pltpu.CompilerParams(
            collective_id=0, has_side_effects=True, vmem_limit_bytes=62 * MIB
        ),
        name="exchange",
    )(tokens.reshape(QB_DEV, QBLK, D), shift, scale, owners, blocks, *weights)


def block_kernel(count_ref, place_ref, *refs):
    vectors_h = refs[0:4]
    tokens_ref, q_h, part_h, log_h, kv_ref = refs[4:9]
    own_h, other_h = refs[9:14], refs[14:19]
    out_ref = refs[19]
    vectors = refs[20:24]
    x_refs = refs[24:26]
    key_refs = refs[26:28]
    value_refs = refs[28:30]
    tok, queries, partial, logs, att = refs[30:35]
    wkv, wo, w1, w2 = refs[35:39]
    sem, vsem, gsem = refs[39:]
    gate_a, shift_m, scale_m, gate_m = vectors
    bf16 = jnp.bfloat16

    def row(vector):
        return vector[...].reshape(1, D)

    ha = lax.axis_index("ha")
    late = [
        pltpu.make_async_copy(src, dst, vsem.at[i])
        for i, (src, dst) in enumerate(
            [(vectors_h[i], vectors[i]) for i in range(4)]
            + [(tokens_ref.at[pl.ds(pl.multiple_of(ha * OWN, OWN), OWN)], tok)]
        )
    ]
    early = [
        pltpu.make_async_copy(src, dst, vsem.at[5 + i])
        for i, (src, dst) in enumerate(((q_h, queries), (part_h, partial), (log_h, logs)))
    ]
    loads = []
    for i in range(5):
        pair = []
        for src, at, number in ((own_h[i], ha, i), (other_h[i], 1 - ha, 5 + i)):
            if i < 2:
                dst = wkv.at[at, :, pl.ds(i * GRP, GRP)]
            elif i == 2:
                dst = wo.at[pl.ds(pl.multiple_of(at * GRP, GRP), GRP)]
            else:
                dst = (w1, w2)[i - 3].at[at]
            pair.append(pltpu.make_async_copy(src, dst, sem.at[number]))
        loads.append(pair)

    def begin(*numbers):
        for i in numbers:
            loads[i][0].start()
            loads[i][1].start()

    def ready(*numbers):
        for i in numbers:
            loads[i][0].wait()
            loads[i][1].wait()

    def gather(blk, slot):
        for j in range(KT):
            for p in range(3):
                pltpu.make_async_copy(
                    kv_ref.at[p, :, place_ref[p, blk * KT + j]],
                    x_refs[slot].at[j, :, :, pl.ds(p * PART, PART)],
                    gsem.at[slot],
                ).start()

    def gathered(slot):
        pltpu.make_async_copy(x_refs[slot], x_refs[slot], gsem.at[slot]).wait()

    def project(blk, slot):
        x = x_refs[slot][...].reshape(ROWS, D)
        live = count_ref[ha * 4 + blk] * QBLK
        place = lax.broadcasted_iota(jnp.int32, (ROWS, 128), 0)
        bias = jnp.where(place < live, 0.0, DEAD).astype(bf16)
        for g in range(2):
            both = jnp.dot(x, wkv[g], preferred_element_type=jnp.float32).astype(bf16)
            k, v = both[:, :GRP], both[:, GRP:]
            for w, (lo, _, spare) in enumerate(WINDOWS):
                key_refs[slot][g, w] = with_lane(k[:, lo : lo + 256], spare, bias)
                value_refs[slot][g, w] = with_lane(v[:, lo : lo + 256], spare, jnp.ones_like(bias))

    def attend(blk, slot):
        at = slice(blk * QBLK, (blk + 1) * QBLK)
        for g in range(2):
            above, below, tops = attend_windows(
                queries[g, at, :],
                [key_refs[slot].at[g, w][...] for w in range(2)],
                [value_refs[slot].at[g, w][...] for w in range(2)],
                True,
            )
            log = logs[g, at, :]
            most = jnp.maximum(tops, log)
            listed, mine = jnp.exp2(tops - most), jnp.exp2(log - most)
            result = (above * listed + partial[g, at, :] * mine) / (below * listed + mine)
            att[at, g * GRP : (g + 1) * GRP] = result.astype(bf16)

    begin(0, 1)
    gather(0, 0)
    ready(0, 1)
    gathered(0)
    for copy in early:
        copy.start()
    gather(1, 1)
    for copy in late:
        copy.start()
    begin(2, 3, 4)
    project(0, 0)
    for copy in early:
        copy.wait()
    for blk in range(4):
        slot = blk % 2
        if blk < 2:
            gather(blk + 2, slot)
        if blk < 3:
            gathered(1 - slot)
            project(blk + 1, 1 - slot)
        attend(blk, slot)

    for copy in late:
        copy.wait()
    ready(2)
    projected = jnp.dot(att[...], wo[...], preferred_element_type=jnp.float32)
    residual = (tok[...].astype(jnp.float32) + row(gate_a) * projected).astype(bf16)
    normed = modulate(residual.astype(jnp.float32), row(shift_m), row(scale_m)).astype(bf16)
    ready(3, 4)
    expanded = jnp.zeros((OWN, D), jnp.float32)
    for g in range(2):
        for lo in range(0, FF // 2, CHUNK):
            hidden = jnp.dot(normed, w1[g, :, lo : lo + CHUNK], preferred_element_type=jnp.float32)
            hidden = jax.nn.gelu(hidden, approximate=True).astype(bf16)
            expanded += jnp.dot(hidden, w2[g, lo : lo + CHUNK, :], preferred_element_type=jnp.float32)
    out_ref[...] = (residual.astype(jnp.float32) + row(gate_m) * expanded).astype(bf16)


def block(counts, places, vectors, tokens, queries, partial, logs, kv, own, other):
    bf16 = jnp.bfloat16
    dma = pltpu.SemaphoreType.DMA
    kv = kv.reshape(3, 2, N_PB * 2, HALF, PART)
    return pl.pallas_call(
        block_kernel,
        out_shape=jax.ShapeDtypeStruct((OWN, D), bf16),
        in_specs=[pl.BlockSpec(memory_space=pltpu.SMEM)] * 2 + [HBM] * 19,
        out_specs=pl.BlockSpec(memory_space=pltpu.VMEM),
        scratch_shapes=[pltpu.VMEM((D,), jnp.float32)] * 4
        + [pltpu.VMEM((KT, 2, HALF, D), bf16)] * 2
        + [pltpu.VMEM((2, 2, ROWS, 256), bf16)] * 4
        + [
            pltpu.VMEM((OWN, D), bf16),
            pltpu.VMEM((2, OWN, GRP), bf16),
            pltpu.VMEM((2, OWN, GRP), jnp.float32),
            pltpu.VMEM((2, OWN, GRP), jnp.float32),
            pltpu.VMEM((OWN, D), bf16),
            pltpu.VMEM((2, D, 2 * GRP), bf16),
            pltpu.VMEM((D, D), bf16),
            pltpu.VMEM((2, D, FF // 2), bf16),
            pltpu.VMEM((2, FF // 2, D), bf16),
        ]
        + [dma((10,)), dma((8,)), dma((2,))],
        compiler_params=pltpu.CompilerParams(vmem_limit_bytes=62 * MIB),
        name="block",
    )(counts, places, *vectors, tokens, queries, partial, logs, kv, *own, *other)


def shards(
    tokens,
    shift_attn,
    scale_attn,
    gate_attn,
    shift_mlp,
    scale_mlp,
    gate_mlp,
    w_query,
    w_key,
    w_value,
    w_out,
    w_fc1,
    w_fc2,
    contact_owner,
    contact_local,
    contact_count,
):
    vectors = (gate_attn, shift_mlp, scale_mlp, gate_mlp)
    own = (w_query, w_key, w_value, w_out, w_fc1, w_fc2)
    owners, blocks = contact_owner.T, contact_local.T
    kv, places, queries, partial, logs, *other = exchange(tokens, shift_attn, scale_attn, owners, blocks, own)
    return block(contact_count, places, vectors, tokens, queries, partial, logs, kv, own[1:], other)


def solution(mesh):
    placed = (
        P("pb", None),
        P(),
        P(),
        P(),
        P(),
        P(),
        P(),
        P(None, "ha"),
        P(None, "ha"),
        P(None, "ha"),
        P("ha", None),
        P(None, "ha"),
        P("ha", None),
        P(),
        P(),
        P("pb"),
    )
    return jax.shard_map(
        shards, mesh=mesh, in_specs=placed, out_specs=P(("pb", "ha"), None), check_vma=False
    )
```

```python
import jax
import jax.numpy as jnp
from jax import lax
from jax.experimental import pallas as pl
from jax.experimental.pallas import tpu as pltpu
from jax.sharding import PartitionSpec as P

D = 768
HEADS = 16
HDIM = 48
FF = 3072
QBLK = 128
KT = 8
QB_DEV = 8
N_PB = 64
SIDE = 4
HALF = QBLK // 2
PART = D // 3
GRP = D // 2
MIB = 2**20
MESH = pl.DeviceIdType.MESH

ORDERS = ((2, 1, 0), (1, 0, 2), (0, 2, 1))
STRIDES = (16, 4, 1)
OFFS = (0, 1, 3, 2)

CAP = 22
PIECES = 2
PIECE = CAP // PIECES
SLOTS = -(-CAP // 8) * 8

epsilon = 1e-06


def modulate(stream, shift, scale):
    center = stream - jnp.mean(stream, -1, keepdims=True)
    spread = jnp.mean(center * center, -1, keepdims=True)
    return center * lax.rsqrt(spread + epsilon) * (1.0 + scale) + shift


ROWS = KT * QBLK
OWN = 4 * QBLK
SHARP = HDIM**-0.5 * 1.4426950408889634
WINDOWS = ((0, (0, 1, 2, 3, 4), 255), (128, (5, 6, 7), 0))
CHUNK = 512
DEAD = -1e30


def with_lane(value, lane, fill):
    at = lax.broadcasted_iota(jnp.int32, (value.shape[0], 128), 1)
    left, right = value[:, :128], value[:, 128:]
    if lane == 0:
        left = jnp.where(at == 0, fill, left)
    else:
        right = jnp.where(at == 127, fill, right)
    return jnp.concatenate([left, right], 1)


def attend_windows(q, keys, values, biased):
    lane = lax.broadcasted_iota(jnp.int32, (QBLK, 256), 1)
    found = []
    for w, (lo, heads, spare) in enumerate(WINDOWS):
        q_part = q[:, lo : lo + 256]
        masks = [(lane >= h * HDIM - lo) & (lane < (h + 1) * HDIM - lo) for h in heads]
        fixed = jnp.zeros_like(q_part)
        if biased:
            fixed = jnp.where(lane == spare, jnp.ones_like(q_part), fixed)
        stacked = jnp.concatenate([jnp.where(m, q_part, fixed) for m in masks], 0)
        scores = lax.dot_general(
            stacked, keys[w], (((1,), (1,)), ((), ())), preferred_element_type=jnp.float32
        )
        top = jnp.max(scores, -1, keepdims=True)
        weights = jnp.exp2(scores - top).astype(jnp.bfloat16)
        outs = jnp.dot(weights, values[w], preferred_element_type=jnp.float32)
        totals = outs[:, spare : spare + 1]
        above = jnp.zeros((QBLK, 256), jnp.float32)
        below = jnp.ones((QBLK, 256), jnp.float32)
        tops = jnp.zeros((QBLK, 256), jnp.float32)
        for i, m in enumerate(masks):
            rows = slice(i * QBLK, (i + 1) * QBLK)
            above = jnp.where(m, outs[rows], above)
            below = jnp.where(m, totals[rows], below)
            tops = jnp.where(m, top[rows], tops)
        found.append((above, below, tops))
    use_first = lane[:, :128] + 128 < 5 * HDIM
    return [
        jnp.concatenate([one[:, :128], jnp.where(use_first, one[:, 128:], two[:, :128]), two[:, 128:]], 1)
        for one, two in zip(*found)
    ]


def exchange_kernel(tokens_ref, shift_ref, scale_ref, owner_ref, block_ref, *refs):
    w_in = refs[0:6]
    kv_ref, place_out, q_out, part_out, log_out = refs[6:11]
    w_out = refs[11:16]
    rows = [refs[16 + 4 * p : 20 + 4 * p] for p in range(3)]
    picked = refs[28]
    tok, shift, scale, owners, blocks, table, sel_ref, owner_s, places = refs[29:38]
    own, qkv_w, queries, mine, partial, logs = refs[38:44]
    (a_s, a_r, af_s, af_r, b_s, b_r, bf_s, bf_r, c_s, c_r, last_r, x_s, x_r, l_s, w_s, w_r, t_s, v_s) = refs[44:]

    pb = lax.axis_index("pb")
    ha = lax.axis_index("ha")
    me = (pb // 16, (pb // 4) % 4, pb % 4)

    def moved(base, axis, off):
        return base + (lax.rem(me[axis] + off, SIDE) - me[axis]) * STRIDES[axis]

    def chip(axis, off):
        return {"pb": moved(pb, axis, off), "ha": ha}

    other = {"pb": pb, "ha": 1 - ha}

    def remote(src, dst, ssem, rsem, dev):
        return pltpu.make_async_remote_copy(
            src_ref=src, dst_ref=dst, send_sem=ssem, recv_sem=rsem, device_id=dev, device_id_type=MESH
        )

    half_rows = pltpu.make_async_copy(
        tokens_ref.at[:, pl.ds(pl.multiple_of(ha * HALF, HALF), HALF)], tok, t_s
    )
    small = [
        pltpu.make_async_copy(src, dst, v_s.at[i])
        for i, (src, dst) in enumerate(
            (
                (shift_ref, shift),
                (scale_ref, scale),
                (owner_ref, owners),
                (block_ref, blocks),
                (owner_ref, owner_s),
                (tokens_ref.at[pl.ds(ha * 4, 4)], own),
                (w_in[0], qkv_w.at[0, ha]),
                (w_in[1], qkv_w.at[1, ha]),
                (w_in[2], qkv_w.at[2, ha]),
            )
        )
    ]
    for copy in small[:2] + [half_rows] + small[2:]:
        copy.start()

    barrier = pltpu.get_barrier_semaphore()
    for axis in range(3):
        for off in (1, 2, 3):
            pl.semaphore_signal(barrier, 1, device_id=chip(axis, off), device_id_type=MESH)
    pl.semaphore_signal(barrier, 1, device_id=other, device_id_type=MESH)
    small[0].wait()
    small[1].wait()
    half_rows.wait()
    for t in range(QB_DEV):
        n = modulate(tok[t].astype(jnp.float32), shift[...].reshape(1, D), scale[...].reshape(1, D))
        n = n.astype(jnp.bfloat16)
        for p in range(3):
            rows[p][0][0, t] = n[:, p * PART : (p + 1) * PART]
    pl.semaphore_wait(barrier, 10)

    def go(copy):
        copy.start()

    def arrived(ref, semaphore):
        remote(ref, ref, x_s, semaphore, other).wait_recv()

    local = []

    def send_a(p, d):
        a = ORDERS[p][0]
        return remote(
            rows[p][0].at[0],
            rows[p][0].at[3 if d == 0 else 1],
            a_s,
            a_r.at[p, d],
            chip(a, 1 if d == 0 else 3),
        )

    def forward_a(p, d):
        a = ORDERS[p][0]
        part = pl.ds(4 * d, 4)
        return remote(
            rows[p][0].at[3 if d == 0 else 1, part],
            rows[p][0].at[2, part],
            af_s,
            af_r.at[p],
            chip(a, 1 if d == 0 else 3),
        )

    def send_b(p, da, d):
        b = ORDERS[p][1]
        return remote(
            rows[p][0].at[da],
            rows[p][3 if d == 0 else 1].at[da],
            b_s,
            b_r.at[p, da, d],
            chip(b, 1 if d == 0 else 3),
        )

    def forward_b(p, da, d):
        b = ORDERS[p][1]
        part = pl.ds(4 * d, 4)
        return remote(
            rows[p][3 if d == 0 else 1].at[da, part],
            rows[p][2].at[da, part],
            bf_s,
            bf_r.at[p],
            chip(b, 1 if d == 0 else 3),
        )

    def send_c(p, db, g):
        c = ORDERS[p][2]
        off = OFFS[g]
        return remote(
            picked.at[p, g, db],
            kv_ref.at[p, 0, SIDE - off, db],
            c_s,
            last_r.at[p, g - 1] if db == 2 else c_r.at[p, db],
            chip(c, off),
        )

    def cross(p, db, g):
        src = picked.at[p, 0, db] if g == 0 else kv_ref.at[p, 0, SIDE - OFFS[g], db]
        return remote(src, kv_ref.at[p, 1, (SIDE - OFFS[g]) % SIDE, db], x_s, x_r, other)

    def keep(p, db):
        return pltpu.make_async_copy(picked.at[p, 0, db], kv_ref.at[p, 0, 0, db], l_s)

    def select(p, db):
        a, b, c = ORDERS[p]
        for g in range(4):
            dest = moved(pb, c, OFFS[g])

            def pick(j, carry):
                da, k = j // 2, j % 2
                owner = moved(moved(pb, b, db), a, da)
                code = sel_ref[owner, dest * QB_DEV]
                number = jnp.where(k == 0, code & 7, (code >> 9) & 7)
                picked[p, g, db, j] = rows[p][db][da, number]
                return carry

            lax.fori_loop(0, 8, pick, 0)
        for g in (3, 1, 2):
            go(send_c(p, db, g))
        keep(p, db).start()
        go(cross(p, db, 0))

    def relay(p, db, *groups):
        if db != 2:
            arrived(kv_ref.at[p, 0, pl.ds(1, 3), db], c_r.at[p, db])
        for g in groups:
            if db == 2:
                send_c(p, db, g).wait_recv()
            go(cross(p, db, g))

    for p in range(3):
        for d in range(2):
            go(send_a(p, d))
    for p in range(3):
        for d in range(2):
            go(send_b(p, 0, d))
    weights = [
        remote(w_in[i], qkv_w.at[i, ha] if i < 3 else w_out[i - 1], w_s.at[i], w_r.at[i], other)
        for i in range(6)
    ]
    for copy in weights:
        go(copy)

    def keep_local(src, dst, number):
        local.append(pltpu.make_async_copy(src, dst, v_s.at[number]))
        local[-1].start()

    def place_entry(e, carry):
        i, j = e // KT, e % KT
        owner = owner_s[j, pb * QB_DEV + ha * 4 + i]
        first = (sel_ref[owner, pb * QB_DEV] & 511) >> 3
        k = jnp.where(first == ha * 4 * KT + e, 0, 1)
        rel = ((owner // 16 - me[0]) & 3, (owner // 4 - me[1]) & 3, (owner - me[2]) & 3)
        for p in range(3):
            a, b, c = ORDERS[p]
            places[p, e] = ((rel[c] * 4 + rel[b]) * 4 + rel[a]) * 2 + k
        return carry

    def own_blocks():
        small[5].wait()
        stream = own[...].reshape(OWN, D).astype(jnp.float32)
        normed = modulate(stream, shift[...].reshape(1, D), scale[...].reshape(1, D))
        own[...] = normed.astype(jnp.bfloat16).reshape(4, QBLK, D)
        for i in range(3):
            small[6 + i].wait()
            remote(w_in[i], qkv_w.at[i, 1 - ha], w_s.at[i], w_r.at[i], other).wait_recv()
        keep_local(qkv_w.at[1, 1 - ha], w_out[0], 10)
        keep_local(qkv_w.at[2, 1 - ha], w_out[1], 11)

        def one_group(g, carry):
            def product(i):
                return jnp.dot(
                    own[...].reshape(OWN, D), qkv_w[i, g], preferred_element_type=jnp.float32
                )

            queries[g] = (product(0) * SHARP).astype(jnp.bfloat16)
            for i in range(2):
                result = product(1 + i).astype(jnp.bfloat16)
                for w, (lo, _, spare) in enumerate(WINDOWS):
                    window = result[:, lo : lo + 256]
                    if i == 1:
                        window = with_lane(window, spare, jnp.ones((OWN, 128), jnp.bfloat16))
                    mine[g, w, i] = window
            return carry

        lax.fori_loop(0, 2, one_group, 0)
        keep_local(queries, q_out, 12)
        lax.fori_loop(0, 4 * KT, place_entry, 0)
        keep_local(places, place_out, 14)

    def own_attention():
        def one_block(i, carry):
            g = i // 4
            at = pl.ds(pl.multiple_of((i % 4) * QBLK, QBLK), QBLK)
            above, below, tops = attend_windows(
                queries[g, at, :], [mine[g, w, 0, at, :] for w in range(2)], [mine[g, w, 1, at, :] for w in range(2)], False
            )
            partial[g, at, :] = above / below
            logs[g, at, :] = tops + jnp.log2(below)
            return carry

        lax.fori_loop(0, 8, one_block, 0)
        keep_local(partial, part_out, 13)
        keep_local(logs, log_out, 15)

    for p in range(3):
        for d in range(2):
            send_a(p, d).wait_recv()
            go(forward_a(p, d))
        for d in range(2):
            for da in (3, 1):
                go(send_b(p, da, d))
    for p in range(3):
        arrived(rows[p][0].at[2], af_r.at[p])
        for d in range(2):
            go(send_b(p, 2, d))
    small[2].wait()
    small[3].wait()
    lane = lax.broadcasted_iota(jnp.int32, (KT, N_PB * QB_DEV), 1)
    order = (lane & 7) * KT + lax.broadcasted_iota(jnp.int32, (KT, N_PB * QB_DEV), 0)
    code = order * 8 + blocks[...]
    size = N_PB * QB_DEV

    def tabulate(i, carry):
        firsts, lasts = [], []
        for o in range(8):
            hit = owners[...] == i * 8 + o
            firsts.append(jnp.min(jnp.where(hit, code, 511), 0, keepdims=True))
            lasts.append(jnp.max(jnp.where(hit, code, 0), 0, keepdims=True))
        first, last = jnp.concatenate(firsts, 0), jnp.concatenate(lasts, 0)
        for step in (1, 2, 4):
            first = jnp.minimum(first, pltpu.roll(first, size - step, 1))
            last = jnp.maximum(last, pltpu.roll(last, size - step, 1))
        table[pl.ds(pl.multiple_of(i * 8, 8), 8), :] = first + (last & 7) * 512
        return carry

    lax.fori_loop(0, N_PB // 8, tabulate, 0)
    to_scalars = pltpu.make_async_copy(table, sel_ref, v_s.at[9])
    to_scalars.start()

    to_scalars.wait()
    small[4].wait()
    for p in range(3):
        select(p, 0)
    for da in (0, 3, 1, 2):
        for p in range(3):
            for d in range(2):
                send_b(p, da, d).wait_recv()
                go(forward_b(p, da, d))
    for p in range(3):
        for db in (3, 1):
            select(p, db)
    own_blocks()
    own_attention()
    for p in range(3):
        relay(p, 0, 1, 2, 3)
    for p in range(3):
        arrived(rows[p][2], bf_r.at[p])
        select(p, 2)
    for db in (3, 1):
        for p in range(3):
            relay(p, db, 1, 2, 3)
    for g in (3, 1, 2):
        for p in range(3):
            relay(p, 2, g)
    arrived(kv_ref.at[:, 1], x_r)
    for copy in weights[3:]:
        copy.wait_recv()
    for copy in weights:
        copy.wait_send()
    two, one = pl.ds(0, 2), pl.ds(0, 1)
    for ref, semaphore in (
        (kv_ref.at[:, 0, one, two], a_s),
        (kv_ref.at[:, 0, one, one], af_s),
        (kv_ref.at[:, 0, two], b_s),
        (kv_ref.at[:, 0, one], bf_s),
        (kv_ref.at[:, 0, pl.ds(1, 3)], c_s),
        (kv_ref.at[:, 1], x_s),
    ):
        remote(ref, ref, semaphore, x_r, other).wait_send()
    pltpu.make_async_copy(picked.at[:, 0], kv_ref.at[:, 0, 0], l_s).wait()
    for copy in local:
        copy.wait()


HBM = pl.BlockSpec(memory_space=pltpu.HBM)


def exchange(tokens, shift, scale, owners, blocks, weights):
    dma = pltpu.SemaphoreType.DMA
    bf16 = jnp.bfloat16
    kv_shape = jax.ShapeDtypeStruct((3, 2, SIDE, SIDE, 8, HALF, PART), bf16)
    table = (N_PB, N_PB * QB_DEV)
    return pl.pallas_call(
        exchange_kernel,
        out_shape=[
            kv_shape,
            jax.ShapeDtypeStruct((8, 128), jnp.int32),
            jax.ShapeDtypeStruct((2, OWN, GRP), bf16),
            jax.ShapeDtypeStruct((2, OWN, GRP), jnp.float32),
            jax.ShapeDtypeStruct((2, OWN, GRP), jnp.float32),
        ]
        + [jax.ShapeDtypeStruct(w.shape, w.dtype) for w in weights[1:]],
        in_specs=[HBM] * 11,
        out_specs=[HBM] * 10,
        scratch_shapes=[pltpu.VMEM((SIDE, QB_DEV, HALF, PART), bf16)] * 12
        + [pltpu.VMEM((3, 4, SIDE, 8, HALF, PART), bf16)]
        + [pltpu.VMEM((QB_DEV, HALF, D), bf16)]
        + [pltpu.VMEM((D,), jnp.float32)] * 2
        + [pltpu.VMEM((KT, N_PB * QB_DEV), jnp.int32)] * 2
        + [pltpu.VMEM(table, jnp.int32), pltpu.SMEM(table, jnp.int32)]
        + [pltpu.SMEM((KT, N_PB * QB_DEV), jnp.int32), pltpu.SMEM((8, 128), jnp.int32)]
        + [
            pltpu.VMEM((4, QBLK, D), bf16),
            pltpu.VMEM((3, 2, D, GRP), bf16),
            pltpu.VMEM((2, OWN, GRP), bf16),
            pltpu.VMEM((2, 2, 2, OWN, 256), bf16),
            pltpu.VMEM((2, OWN, GRP), jnp.float32),
            pltpu.VMEM((2, OWN, GRP), jnp.float32),
        ]
        + [dma, dma((3, 2)), dma, dma((3,))]
        + [dma, dma((3, 4, 2)), dma, dma((3,))]
        + [dma, dma((3, 4)), dma((3, 3)), dma, dma, dma]
        + [dma((6,)), dma((6,)), dma, dma((16,))],
        compiler_params=pltpu.CompilerParams(
            collective_id=0, has_side_effects=True, vmem_limit_bytes=62 * MIB
        ),
        name="exchange",
    )(tokens.reshape(QB_DEV, QBLK, D), shift, scale, owners, blocks, *weights)


def pooled_kernel(tokens_ref, shift_ref, scale_ref, owner_ref, block_ref, *refs):
    w_in = refs[0:6]
    kv_ref, place_out, q_out, part_out, log_out, most_out = refs[6:12]
    w_out = refs[12:17]
    plane = refs[17:20]
    picked = refs[20]
    tok, shift, scale, owners, blocks, table, sel_ref, ranks, rank_s, owner_s, places, most = refs[21:33]
    own, qkv_w, queries, mine, partial, logs = refs[33:39]
    (a_s, a_r, af_s, af_r, b_s, b_r, bf_s, bf_r, c_s, c_r, x_s, x_r, l_s, w_s, w_r, t_s, v_s) = refs[39:]

    pb = lax.axis_index("pb")
    ha = lax.axis_index("ha")
    me = (pb // 16, (pb // 4) % 4, pb % 4)

    def moved(base, axis, off):
        return base + (lax.rem(me[axis] + off, SIDE) - me[axis]) * STRIDES[axis]

    def chip(axis, off):
        return {"pb": moved(pb, axis, off), "ha": ha}

    other = {"pb": pb, "ha": 1 - ha}

    def remote(src, dst, ssem, rsem, dev):
        return pltpu.make_async_remote_copy(
            src_ref=src, dst_ref=dst, send_sem=ssem, recv_sem=rsem, device_id=dev, device_id_type=MESH
        )

    half_rows = pltpu.make_async_copy(
        tokens_ref.at[:, pl.ds(pl.multiple_of(ha * HALF, HALF), HALF)], tok, t_s
    )
    small = [
        pltpu.make_async_copy(src, dst, v_s.at[i])
        for i, (src, dst) in enumerate(
            (
                (shift_ref, shift),
                (scale_ref, scale),
                (owner_ref, owners),
                (block_ref, blocks),
                (owner_ref, owner_s),
                (tokens_ref.at[pl.ds(ha * 4, 4)], own),
                (w_in[0], qkv_w.at[0, ha]),
                (w_in[1], qkv_w.at[1, ha]),
                (w_in[2], qkv_w.at[2, ha]),
            )
        )
    ]
    for copy in small[:2] + [half_rows] + small[2:]:
        copy.start()

    barrier = pltpu.get_barrier_semaphore()
    for axis in range(3):
        for off in (1, 2, 3):
            pl.semaphore_signal(barrier, 1, device_id=chip(axis, off), device_id_type=MESH)
    pl.semaphore_signal(barrier, 1, device_id=other, device_id_type=MESH)
    small[0].wait()
    small[1].wait()
    half_rows.wait()
    for t in range(QB_DEV):
        n = modulate(tok[t].astype(jnp.float32), shift[...].reshape(1, D), scale[...].reshape(1, D))
        n = n.astype(jnp.bfloat16)
        for p in range(3):
            plane[p][t] = n[:, p * PART : (p + 1) * PART]
    pl.semaphore_wait(barrier, 10)

    def go(copy):
        copy.start()

    def arrived(ref, semaphore):
        remote(ref, ref, x_s, semaphore, other).wait_recv()

    local = []

    def tiles(p, db, da, first=0, count=QB_DEV):
        return plane[p].at[pl.ds((db * SIDE + da) * QB_DEV + first, count)]

    def send_a(p, d):
        return remote(
            tiles(p, 0, 0), tiles(p, 0, 3 if d == 0 else 1), a_s, a_r.at[p, d], chip(ORDERS[p][0], 1 if d == 0 else 3)
        )

    def forward_a(p, d):
        return remote(
            tiles(p, 0, 3 if d == 0 else 1, 4 * d, 4),
            tiles(p, 0, 2, 4 * d, 4),
            af_s,
            af_r.at[p],
            chip(ORDERS[p][0], 1 if d == 0 else 3),
        )

    def send_b(p, da, d):
        return remote(
            tiles(p, 0, da),
            tiles(p, 3 if d == 0 else 1, da),
            b_s,
            b_r.at[p, da, d],
            chip(ORDERS[p][1], 1 if d == 0 else 3),
        )

    def forward_b(p, da, d):
        return remote(
            tiles(p, 3 if d == 0 else 1, da, 4 * d, 4),
            tiles(p, 2, da, 4 * d, 4),
            bf_s,
            bf_r.at[p],
            chip(ORDERS[p][1], 1 if d == 0 else 3),
        )

    def send_c(p, g, h):
        off = OFFS[g]
        return remote(
            picked.at[p, g, pl.ds(h * PIECE, PIECE)],
            kv_ref.at[p, 0, SIDE - off, pl.ds(h * PIECE, PIECE)],
            c_s,
            c_r.at[p, g - 1, h],
            chip(ORDERS[p][2], off),
        )

    def cross(p, g, h):
        part = pl.ds(h * PIECE, PIECE)
        src = picked.at[p, 0, part] if g == 0 else kv_ref.at[p, 0, SIDE - OFFS[g], part]
        return remote(src, kv_ref.at[p, 1, (SIDE - OFFS[g]) % SIDE, part], x_s, x_r, other)

    def select(p, g, h):
        lane = moved(pb, ORDERS[p][2], OFFS[g]) * QB_DEV

        def pick(i, carry):
            at = h * PIECE + i
            picked[p, g, at] = plane[p][sel_ref[p, at, lane]]
            return carry

        lax.fori_loop(0, PIECE, pick, 0, unroll=PIECE)

    for p in range(3):
        for d in range(2):
            go(send_a(p, d))
    for p in range(3):
        for d in range(2):
            go(send_b(p, 0, d))
    weights = [
        remote(w_in[i], qkv_w.at[i, ha] if i < 3 else w_out[i - 1], w_s.at[i], w_r.at[i], other)
        for i in range(6)
    ]
    for copy in weights:
        go(copy)

    def keep_local(src, dst, number):
        local.append(pltpu.make_async_copy(src, dst, v_s.at[number]))
        local[-1].start()

    def place_entry(e, carry):
        i, j = e // KT, e % KT
        at = pb * QB_DEV + ha * 4 + i
        owner = owner_s[j, at]
        for p in range(3):
            c = ORDERS[p][2]
            rel = (owner // STRIDES[c] - me[c]) & 3
            places[p, e] = rel * SIDE * 8 + jnp.minimum(rank_s[c, j, at], CAP - 1)
        return carry

    def own_blocks():
        small[5].wait()
        stream = own[...].reshape(OWN, D).astype(jnp.float32)
        normed = modulate(stream, shift[...].reshape(1, D), scale[...].reshape(1, D))
        own[...] = normed.astype(jnp.bfloat16).reshape(4, QBLK, D)
        for i in range(3):
            small[6 + i].wait()
            remote(w_in[i], qkv_w.at[i, 1 - ha], w_s.at[i], w_r.at[i], other).wait_recv()
        keep_local(qkv_w.at[1, 1 - ha], w_out[0], 16)
        keep_local(qkv_w.at[2, 1 - ha], w_out[1], 11)

        def one_group(g, carry):
            def product(i):
                return jnp.dot(
                    own[...].reshape(OWN, D), qkv_w[i, g], preferred_element_type=jnp.float32
                )

            queries[g] = (product(0) * SHARP).astype(jnp.bfloat16)
            for i in range(2):
                result = product(1 + i).astype(jnp.bfloat16)
                for w, (lo, _, spare) in enumerate(WINDOWS):
                    window = result[:, lo : lo + 256]
                    if i == 1:
                        window = with_lane(window, spare, jnp.ones((OWN, 128), jnp.bfloat16))
                    mine[g, w, i] = window
            return carry

        lax.fori_loop(0, 2, one_group, 0)
        keep_local(queries, q_out, 12)
        lax.fori_loop(0, 4 * KT, place_entry, 0)
        keep_local(places, place_out, 14)

    def own_attention():
        def one_block(i, carry):
            g = i // 4
            at = pl.ds(pl.multiple_of((i % 4) * QBLK, QBLK), QBLK)
            above, below, tops = attend_windows(
                queries[g, at, :], [mine[g, w, 0, at, :] for w in range(2)], [mine[g, w, 1, at, :] for w in range(2)], False
            )
            partial[g, at, :] = above / below
            logs[g, at, :] = tops + jnp.log2(below)
            return carry

        lax.fori_loop(0, 8, one_block, 0)
        keep_local(partial, part_out, 13)
        keep_local(logs, log_out, 15)

    for p in range(3):
        for d in range(2):
            send_a(p, d).wait_recv()
            go(forward_a(p, d))
        for d in range(2):
            for da in (3, 1):
                go(send_b(p, da, d))
    for p in range(3):
        arrived(tiles(p, 0, 2), af_r.at[p])
        for d in range(2):
            go(send_b(p, 2, d))
    small[2].wait()
    small[3].wait()
    size = N_PB * QB_DEV
    wide = (KT, size)
    lane = lax.broadcasted_iota(jnp.int32, wide, 1) & 7
    line = lax.broadcasted_iota(jnp.int32, wide, 0)
    coords = [(owners[...] // stride) & 3 for stride in STRIDES]

    def ranked(marks):
        column = marks
        for step in (1, 2, 4):
            column = column + jnp.where(line >= step, pltpu.roll(column, step, 0), 0)
        total = jnp.broadcast_to(jnp.sum(marks, 0, keepdims=True), wide)
        row = total
        for step in (1, 2, 4):
            row = row + jnp.where(lane >= step, pltpu.roll(row, step, 1), 0)
        return column - marks + row - total

    top = jnp.zeros(wide, jnp.int32)
    for axis in range(3):
        rank = jnp.zeros(wide, jnp.int32)
        for value in range(SIDE):
            here = coords[axis] == value
            rank = jnp.where(here, ranked(here.astype(jnp.int32)), rank)
        ranks[axis] = rank
        top = jnp.maximum(top, rank)
    most[...] = jnp.broadcast_to(jnp.max(jnp.max(top, 1, keepdims=True), 0, keepdims=True), (8, 128))

    for p in range(3):
        a, b, c = ORDERS[p]
        rel_b, rel_a = (coords[b] - me[b]) & 3, (coords[a] - me[a]) & 3
        number = (rel_b * SIDE + rel_a) * QB_DEV + blocks[...]
        slot = jnp.where(coords[c] == me[c], ranks[c], -1)

        def tabulate(i, carry):
            found = [
                jnp.max(jnp.where(slot == i * 8 + n, number, 0), 0, keepdims=True) for n in range(8)
            ]
            found = jnp.concatenate(found, 0)
            for step in (1, 2, 4):
                found = jnp.maximum(found, pltpu.roll(found, size - step, 1))
            table[p, pl.ds(pl.multiple_of(i * 8, 8), 8), :] = found
            return carry

        lax.fori_loop(0, SLOTS // 8, tabulate, 0)
    to_scalars = pltpu.make_async_copy(table, sel_ref, v_s.at[9])
    to_scalars.start()
    ranks_out = pltpu.make_async_copy(ranks, rank_s, v_s.at[10])
    ranks_out.start()
    for da in (0, 3, 1, 2):
        for p in range(3):
            for d in range(2):
                send_b(p, da, d).wait_recv()
                go(forward_b(p, da, d))
    to_scalars.wait()
    ranks_out.wait()
    small[4].wait()
    keep_local(most, most_out, 17)
    own_blocks()
    for p in range(3):
        arrived(plane[p].at[pl.ds(2 * SIDE * QB_DEV, SIDE * QB_DEV)], bf_r.at[p])
        for h in range(PIECES):
            for g in (3, 1, 2):
                select(p, g, h)
                go(send_c(p, g, h))
    for p in range(3):
        for h in range(PIECES):
            select(p, 0, h)
            go(cross(p, 0, h))
        pltpu.make_async_copy(picked.at[p, 0], kv_ref.at[p, 0, 0, pl.ds(0, CAP)], l_s).start()
    own_attention()
    for h in range(PIECES):
        for g in (3, 1, 2):
            for p in range(3):
                send_c(p, g, h).wait_recv()
                go(cross(p, g, h))
    arrived(kv_ref.at[:, 1, :, pl.ds(0, CAP)], x_r)
    for copy in weights[3:]:
        copy.wait_recv()
    for copy in weights:
        copy.wait_send()
    for ref, semaphore in (
        (kv_ref.at[:, 0, pl.ds(0, 2), pl.ds(0, 8)], a_s),
        (kv_ref.at[:, 0, pl.ds(0, 1), pl.ds(0, 8)], af_s),
        (kv_ref.at[:, 0, :, pl.ds(0, 16)], b_s),
        (kv_ref.at[:, 0, :, pl.ds(0, 8)], bf_s),
        (picked.at[:, pl.ds(1, 3)], c_s),
        (kv_ref.at[:, 1, :, pl.ds(0, CAP)], x_s),
    ):
        remote(ref, ref, semaphore, x_r, other).wait_send()
    pltpu.make_async_copy(picked.at[:, 0], kv_ref.at[:, 0, 0, pl.ds(0, CAP)], l_s).wait()
    for copy in local:
        copy.wait()


def exchange_pooled(tokens, shift, scale, owners, blocks, weights):
    dma = pltpu.SemaphoreType.DMA
    bf16 = jnp.bfloat16
    kv_shape = jax.ShapeDtypeStruct((3, 2, SIDE, SIDE * 8, HALF, PART), bf16)
    table = (3, SLOTS, N_PB * QB_DEV)
    ranks = (3, KT, N_PB * QB_DEV)
    return pl.pallas_call(
        pooled_kernel,
        out_shape=[
            kv_shape,
            jax.ShapeDtypeStruct((8, 128), jnp.int32),
            jax.ShapeDtypeStruct((2, OWN, GRP), bf16),
            jax.ShapeDtypeStruct((2, OWN, GRP), jnp.float32),
            jax.ShapeDtypeStruct((2, OWN, GRP), jnp.float32),
            jax.ShapeDtypeStruct((8, 128), jnp.int32),
        ]
        + [jax.ShapeDtypeStruct(w.shape, w.dtype) for w in weights[1:]],
        in_specs=[HBM] * 11,
        out_specs=[HBM] * 11,
        scratch_shapes=[pltpu.VMEM((SIDE * SIDE * QB_DEV, HALF, PART), bf16)] * 3
        + [pltpu.VMEM((3, 4, CAP, HALF, PART), bf16)]
        + [pltpu.VMEM((QB_DEV, HALF, D), bf16)]
        + [pltpu.VMEM((D,), jnp.float32)] * 2
        + [pltpu.VMEM((KT, N_PB * QB_DEV), jnp.int32)] * 2
        + [pltpu.VMEM(table, jnp.int32), pltpu.SMEM(table, jnp.int32)]
        + [pltpu.VMEM(ranks, jnp.int32), pltpu.SMEM(ranks, jnp.int32)]
        + [pltpu.SMEM((KT, N_PB * QB_DEV), jnp.int32), pltpu.SMEM((8, 128), jnp.int32)]
        + [pltpu.VMEM((8, 128), jnp.int32)]
        + [
            pltpu.VMEM((4, QBLK, D), bf16),
            pltpu.VMEM((3, 2, D, GRP), bf16),
            pltpu.VMEM((2, OWN, GRP), bf16),
            pltpu.VMEM((2, 2, 2, OWN, 256), bf16),
            pltpu.VMEM((2, OWN, GRP), jnp.float32),
            pltpu.VMEM((2, OWN, GRP), jnp.float32),
        ]
        + [dma, dma((3, 2)), dma, dma((3,))]
        + [dma, dma((3, 4, 2)), dma, dma((3,))]
        + [dma, dma((3, 3, PIECES)), dma, dma, dma]
        + [dma((6,)), dma((6,)), dma, dma((18,))],
        compiler_params=pltpu.CompilerParams(
            collective_id=1, has_side_effects=True, vmem_limit_bytes=62 * MIB
        ),
        name="exchange_pooled",
    )(tokens.reshape(QB_DEV, QBLK, D), shift, scale, owners, blocks, *weights)


def block_kernel(count_ref, place_ref, *refs):
    vectors_h = refs[0:4]
    tokens_ref, q_h, part_h, log_h, kv_ref = refs[4:9]
    own_h, other_h = refs[9:14], refs[14:19]
    out_ref = refs[19]
    vectors = refs[20:24]
    x_refs = refs[24:26]
    key_refs = refs[26:28]
    value_refs = refs[28:30]
    tok, queries, partial, logs, att = refs[30:35]
    wkv, wo, w1, w2 = refs[35:39]
    sem, vsem, gsem = refs[39:]
    gate_a, shift_m, scale_m, gate_m = vectors
    bf16 = jnp.bfloat16

    def row(vector):
        return vector[...].reshape(1, D)

    ha = lax.axis_index("ha")
    late = [
        pltpu.make_async_copy(src, dst, vsem.at[i])
        for i, (src, dst) in enumerate(
            [(vectors_h[i], vectors[i]) for i in range(4)]
            + [(tokens_ref.at[pl.ds(pl.multiple_of(ha * OWN, OWN), OWN)], tok)]
        )
    ]
    early = [
        pltpu.make_async_copy(src, dst, vsem.at[5 + i])
        for i, (src, dst) in enumerate(((q_h, queries), (part_h, partial), (log_h, logs)))
    ]
    loads = []
    for i in range(5):
        pair = []
        for src, at, number in ((own_h[i], ha, i), (other_h[i], 1 - ha, 5 + i)):
            if i < 2:
                dst = wkv.at[at, :, pl.ds(i * GRP, GRP)]
            elif i == 2:
                dst = wo.at[pl.ds(pl.multiple_of(at * GRP, GRP), GRP)]
            else:
                dst = (w1, w2)[i - 3].at[at]
            pair.append(pltpu.make_async_copy(src, dst, sem.at[number]))
        loads.append(pair)

    def begin(*numbers):
        for i in numbers:
            loads[i][0].start()
            loads[i][1].start()

    def ready(*numbers):
        for i in numbers:
            loads[i][0].wait()
            loads[i][1].wait()

    def gather(blk, slot):
        for j in range(KT):
            for p in range(3):
                pltpu.make_async_copy(
                    kv_ref.at[p, :, place_ref[p, blk * KT + j]],
                    x_refs[slot].at[j, :, :, pl.ds(p * PART, PART)],
                    gsem.at[slot],
                ).start()

    def gathered(slot):
        pltpu.make_async_copy(x_refs[slot], x_refs[slot], gsem.at[slot]).wait()

    def project(blk, slot):
        x = x_refs[slot][...].reshape(ROWS, D)
        live = count_ref[ha * 4 + blk] * QBLK
        place = lax.broadcasted_iota(jnp.int32, (ROWS, 128), 0)
        bias = jnp.where(place < live, 0.0, DEAD).astype(bf16)
        for g in range(2):
            both = jnp.dot(x, wkv[g], preferred_element_type=jnp.float32).astype(bf16)
            k, v = both[:, :GRP], both[:, GRP:]
            for w, (lo, _, spare) in enumerate(WINDOWS):
                key_refs[slot][g, w] = with_lane(k[:, lo : lo + 256], spare, bias)
                value_refs[slot][g, w] = with_lane(v[:, lo : lo + 256], spare, jnp.ones_like(bias))

    def attend(blk, slot):
        at = slice(blk * QBLK, (blk + 1) * QBLK)
        for g in range(2):
            above, below, tops = attend_windows(
                queries[g, at, :],
                [key_refs[slot].at[g, w][...] for w in range(2)],
                [value_refs[slot].at[g, w][...] for w in range(2)],
                True,
            )
            log = logs[g, at, :]
            most = jnp.maximum(tops, log)
            listed, mine = jnp.exp2(tops - most), jnp.exp2(log - most)
            result = (above * listed + partial[g, at, :] * mine) / (below * listed + mine)
            att[at, g * GRP : (g + 1) * GRP] = result.astype(bf16)

    begin(0, 1)
    gather(0, 0)
    ready(0, 1)
    gathered(0)
    for copy in early:
        copy.start()
    gather(1, 1)
    for copy in late:
        copy.start()
    begin(2, 3, 4)
    project(0, 0)
    for copy in early:
        copy.wait()
    for blk in range(4):
        slot = blk % 2
        if blk < 2:
            gather(blk + 2, slot)
        if blk < 3:
            gathered(1 - slot)
            project(blk + 1, 1 - slot)
        attend(blk, slot)

    for copy in late:
        copy.wait()
    ready(2)
    projected = jnp.dot(att[...], wo[...], preferred_element_type=jnp.float32)
    residual = (tok[...].astype(jnp.float32) + row(gate_a) * projected).astype(bf16)
    normed = modulate(residual.astype(jnp.float32), row(shift_m), row(scale_m)).astype(bf16)
    ready(3, 4)
    expanded = jnp.zeros((OWN, D), jnp.float32)
    for g in range(2):
        for lo in range(0, FF // 2, CHUNK):
            hidden = jnp.dot(normed, w1[g, :, lo : lo + CHUNK], preferred_element_type=jnp.float32)
            hidden = jax.nn.gelu(hidden, approximate=True).astype(bf16)
            expanded += jnp.dot(hidden, w2[g, lo : lo + CHUNK, :], preferred_element_type=jnp.float32)
    out_ref[...] = (residual.astype(jnp.float32) + row(gate_m) * expanded).astype(bf16)


def block(counts, places, vectors, tokens, queries, partial, logs, kv, own, other):
    bf16 = jnp.bfloat16
    dma = pltpu.SemaphoreType.DMA
    kv = kv.reshape(3, 2, -1, HALF, PART)
    return pl.pallas_call(
        block_kernel,
        out_shape=jax.ShapeDtypeStruct((OWN, D), bf16),
        in_specs=[pl.BlockSpec(memory_space=pltpu.SMEM)] * 2 + [HBM] * 19,
        out_specs=pl.BlockSpec(memory_space=pltpu.VMEM),
        scratch_shapes=[pltpu.VMEM((D,), jnp.float32)] * 4
        + [pltpu.VMEM((KT, 2, HALF, D), bf16)] * 2
        + [pltpu.VMEM((2, 2, ROWS, 256), bf16)] * 4
        + [
            pltpu.VMEM((OWN, D), bf16),
            pltpu.VMEM((2, OWN, GRP), bf16),
            pltpu.VMEM((2, OWN, GRP), jnp.float32),
            pltpu.VMEM((2, OWN, GRP), jnp.float32),
            pltpu.VMEM((OWN, D), bf16),
            pltpu.VMEM((2, D, 2 * GRP), bf16),
            pltpu.VMEM((D, D), bf16),
            pltpu.VMEM((2, D, FF // 2), bf16),
            pltpu.VMEM((2, FF // 2, D), bf16),
        ]
        + [dma((10,)), dma((8,)), dma((2,))],
        compiler_params=pltpu.CompilerParams(vmem_limit_bytes=62 * MIB),
        name="block",
    )(counts, places, *vectors, tokens, queries, partial, logs, kv, *own, *other)


def shards(
    tokens,
    shift_attn,
    scale_attn,
    gate_attn,
    shift_mlp,
    scale_mlp,
    gate_mlp,
    w_query,
    w_key,
    w_value,
    w_out,
    w_fc1,
    w_fc2,
    contact_owner,
    contact_local,
    contact_count,
):
    vectors = (gate_attn, shift_mlp, scale_mlp, gate_mlp)
    own = (w_query, w_key, w_value, w_out, w_fc1, w_fc2)
    owners, blocks = contact_owner.T, contact_local.T
    args = (tokens, shift_attn, scale_attn, owners, blocks, own)
    kv, places, queries, partial, logs, most, *other = exchange_pooled(*args)

    def crowded():
        other_kv, other_places, *_ = exchange(*args)
        return other_kv.reshape(kv.shape), other_places

    kv_used, places_used = lax.cond(most[0, 0] < CAP, lambda: (kv, places), crowded)
    return block(contact_count, places_used, vectors, tokens, queries, partial, logs, kv_used, own[1:], other)


def solution(mesh):
    placed = (
        P("pb", None),
        P(),
        P(),
        P(),
        P(),
        P(),
        P(),
        P(None, "ha"),
        P(None, "ha"),
        P(None, "ha"),
        P("ha", None),
        P(None, "ha"),
        P("ha", None),
        P(),
        P(),
        P("pb"),
    )
    return jax.shard_map(
        shards, mesh=mesh, in_specs=placed, out_specs=P(("pb", "ha"), None), check_vma=False
    )
```

```python
import jax
import jax.numpy as jnp
from jax import lax
from jax.experimental import pallas as pl
from jax.experimental.pallas import tpu as pltpu
from jax.sharding import PartitionSpec as P

D = 768
HEADS = 16
HDIM = 48
FF = 3072
QBLK = 128
KT = 8
QB_DEV = 8
N_PB = 64
SIDE = 4
HALF = QBLK // 2
PART = D // 3
GRP = D // 2
MIB = 2**20
MESH = pl.DeviceIdType.MESH

ORDERS = ((2, 1, 0), (1, 0, 2), (0, 2, 1))
STRIDES = (16, 4, 1)
OFFS = (0, 1, 3, 2)

CAP = 22
PIECES = 2
PIECE = CAP // PIECES
SLOTS = -(-CAP // 8) * 8

epsilon = 1e-06


def modulate(stream, shift, scale):
    center = stream - jnp.mean(stream, -1, keepdims=True)
    spread = jnp.mean(center * center, -1, keepdims=True)
    return center * lax.rsqrt(spread + epsilon) * (1.0 + scale) + shift


ROWS = KT * QBLK
OWN = 4 * QBLK
SHARP = HDIM**-0.5 * 1.4426950408889634
WINDOWS = ((0, (0, 1, 2, 3, 4), 255), (128, (5, 6, 7), 0))
CHUNK = 512
DEAD = -1e30


def with_lane(value, lane, fill):
    at = lax.broadcasted_iota(jnp.int32, (value.shape[0], 128), 1)
    left, right = value[:, :128], value[:, 128:]
    if lane == 0:
        left = jnp.where(at == 0, fill, left)
    else:
        right = jnp.where(at == 127, fill, right)
    return jnp.concatenate([left, right], 1)


def attend_windows(q, keys, values, biased):
    lane = lax.broadcasted_iota(jnp.int32, (QBLK, 256), 1)
    found = []
    for w, (lo, heads, spare) in enumerate(WINDOWS):
        q_part = q[:, lo : lo + 256]
        masks = [(lane >= h * HDIM - lo) & (lane < (h + 1) * HDIM - lo) for h in heads]
        fixed = jnp.zeros_like(q_part)
        if biased:
            fixed = jnp.where(lane == spare, jnp.ones_like(q_part), fixed)
        stacked = jnp.concatenate([jnp.where(m, q_part, fixed) for m in masks], 0)
        scores = lax.dot_general(
            stacked, keys[w], (((1,), (1,)), ((), ())), preferred_element_type=jnp.float32
        )
        top = jnp.max(scores, -1, keepdims=True)
        weights = jnp.exp2(scores - top).astype(jnp.bfloat16)
        outs = jnp.dot(weights, values[w], preferred_element_type=jnp.float32)
        totals = outs[:, spare : spare + 1]
        above = jnp.zeros((QBLK, 256), jnp.float32)
        below = jnp.ones((QBLK, 256), jnp.float32)
        tops = jnp.zeros((QBLK, 256), jnp.float32)
        for i, m in enumerate(masks):
            rows = slice(i * QBLK, (i + 1) * QBLK)
            above = jnp.where(m, outs[rows], above)
            below = jnp.where(m, totals[rows], below)
            tops = jnp.where(m, top[rows], tops)
        found.append((above, below, tops))
    use_first = lane[:, :128] + 128 < 5 * HDIM
    return [
        jnp.concatenate([one[:, :128], jnp.where(use_first, one[:, 128:], two[:, :128]), two[:, 128:]], 1)
        for one, two in zip(*found)
    ]


def exchange_kernel(tokens_ref, shift_ref, scale_ref, owner_ref, block_ref, *refs):
    w_in = refs[0:6]
    kv_ref, place_out, q_out, part_out, log_out = refs[6:11]
    w_out = refs[11:16]
    rows = [refs[16 + 4 * p : 20 + 4 * p] for p in range(3)]
    picked = refs[28]
    tok, shift, scale, owners, blocks, table, sel_ref, owner_s, places = refs[29:38]
    own, qkv_w, queries, mine, partial, logs = refs[38:44]
    (a_s, a_r, af_s, af_r, b_s, b_r, bf_s, bf_r, c_s, c_r, last_r, x_s, x_r, l_s, w_s, w_r, t_s, v_s) = refs[44:]

    pb = lax.axis_index("pb")
    ha = lax.axis_index("ha")
    me = (pb // 16, (pb // 4) % 4, pb % 4)

    def moved(base, axis, off):
        return base + (lax.rem(me[axis] + off, SIDE) - me[axis]) * STRIDES[axis]

    def chip(axis, off):
        return {"pb": moved(pb, axis, off), "ha": ha}

    other = {"pb": pb, "ha": 1 - ha}

    def remote(src, dst, ssem, rsem, dev):
        return pltpu.make_async_remote_copy(
            src_ref=src, dst_ref=dst, send_sem=ssem, recv_sem=rsem, device_id=dev, device_id_type=MESH
        )

    half_rows = pltpu.make_async_copy(
        tokens_ref.at[:, pl.ds(pl.multiple_of(ha * HALF, HALF), HALF)], tok, t_s
    )
    small = [
        pltpu.make_async_copy(src, dst, v_s.at[i])
        for i, (src, dst) in enumerate(
            (
                (shift_ref, shift),
                (scale_ref, scale),
                (owner_ref, owners),
                (block_ref, blocks),
                (owner_ref, owner_s),
                (tokens_ref.at[pl.ds(ha * 4, 4)], own),
                (w_in[0], qkv_w.at[0, ha]),
                (w_in[1], qkv_w.at[1, ha]),
                (w_in[2], qkv_w.at[2, ha]),
            )
        )
    ]
    for copy in small[:2] + [half_rows] + small[2:]:
        copy.start()

    barrier = pltpu.get_barrier_semaphore()
    for axis in range(3):
        for off in (1, 2, 3):
            pl.semaphore_signal(barrier, 1, device_id=chip(axis, off), device_id_type=MESH)
    pl.semaphore_signal(barrier, 1, device_id=other, device_id_type=MESH)
    small[0].wait()
    small[1].wait()
    half_rows.wait()
    for t in range(QB_DEV):
        n = modulate(tok[t].astype(jnp.float32), shift[...].reshape(1, D), scale[...].reshape(1, D))
        n = n.astype(jnp.bfloat16)
        for p in range(3):
            rows[p][0][0, t] = n[:, p * PART : (p + 1) * PART]
    pl.semaphore_wait(barrier, 10)

    def go(copy):
        copy.start()

    def arrived(ref, semaphore):
        remote(ref, ref, x_s, semaphore, other).wait_recv()

    local = []

    def send_a(p, d):
        a = ORDERS[p][0]
        return remote(
            rows[p][0].at[0],
            rows[p][0].at[3 if d == 0 else 1],
            a_s,
            a_r.at[p, d],
            chip(a, 1 if d == 0 else 3),
        )

    def forward_a(p, d):
        a = ORDERS[p][0]
        part = pl.ds(4 * d, 4)
        return remote(
            rows[p][0].at[3 if d == 0 else 1, part],
            rows[p][0].at[2, part],
            af_s,
            af_r.at[p],
            chip(a, 1 if d == 0 else 3),
        )

    def send_b(p, da, d):
        b = ORDERS[p][1]
        return remote(
            rows[p][0].at[da],
            rows[p][3 if d == 0 else 1].at[da],
            b_s,
            b_r.at[p, da, d],
            chip(b, 1 if d == 0 else 3),
        )

    def forward_b(p, da, d):
        b = ORDERS[p][1]
        part = pl.ds(4 * d, 4)
        return remote(
            rows[p][3 if d == 0 else 1].at[da, part],
            rows[p][2].at[da, part],
            bf_s,
            bf_r.at[p],
            chip(b, 1 if d == 0 else 3),
        )

    def send_c(p, db, g):
        c = ORDERS[p][2]
        off = OFFS[g]
        return remote(
            picked.at[p, g, db],
            kv_ref.at[p, 0, SIDE - off, db],
            c_s,
            last_r.at[p, g - 1] if db == 2 else c_r.at[p, db],
            chip(c, off),
        )

    def cross(p, db, g):
        src = picked.at[p, 0, db] if g == 0 else kv_ref.at[p, 0, SIDE - OFFS[g], db]
        return remote(src, kv_ref.at[p, 1, (SIDE - OFFS[g]) % SIDE, db], x_s, x_r, other)

    def keep(p, db):
        return pltpu.make_async_copy(picked.at[p, 0, db], kv_ref.at[p, 0, 0, db], l_s)

    def select(p, db):
        a, b, c = ORDERS[p]
        for g in range(4):
            dest = moved(pb, c, OFFS[g])

            def pick(j, carry):
                da, k = j // 2, j % 2
                owner = moved(moved(pb, b, db), a, da)
                code = sel_ref[owner, dest * QB_DEV]
                number = jnp.where(k == 0, code & 7, (code >> 9) & 7)
                picked[p, g, db, j] = rows[p][db][da, number]
                return carry

            lax.fori_loop(0, 8, pick, 0)
        for g in (3, 1, 2):
            go(send_c(p, db, g))
        keep(p, db).start()
        go(cross(p, db, 0))

    def relay(p, db, *groups):
        if db != 2:
            arrived(kv_ref.at[p, 0, pl.ds(1, 3), db], c_r.at[p, db])
        for g in groups:
            if db == 2:
                send_c(p, db, g).wait_recv()
            go(cross(p, db, g))

    for p in range(3):
        for d in range(2):
            go(send_a(p, d))
    for p in range(3):
        for d in range(2):
            go(send_b(p, 0, d))
    weights = [
        remote(w_in[i], qkv_w.at[i, ha] if i < 3 else w_out[i - 1], w_s.at[i], w_r.at[i], other)
        for i in range(6)
    ]
    for copy in weights:
        go(copy)

    def keep_local(src, dst, number):
        local.append(pltpu.make_async_copy(src, dst, v_s.at[number]))
        local[-1].start()

    def place_entry(e, carry):
        i, j = e // KT, e % KT
        owner = owner_s[j, pb * QB_DEV + ha * 4 + i]
        first = (sel_ref[owner, pb * QB_DEV] & 511) >> 3
        k = jnp.where(first == ha * 4 * KT + e, 0, 1)
        rel = ((owner // 16 - me[0]) & 3, (owner // 4 - me[1]) & 3, (owner - me[2]) & 3)
        for p in range(3):
            a, b, c = ORDERS[p]
            places[p, e] = ((rel[c] * 4 + rel[b]) * 4 + rel[a]) * 2 + k
        return carry

    def own_blocks():
        small[5].wait()
        stream = own[...].reshape(OWN, D).astype(jnp.float32)
        normed = modulate(stream, shift[...].reshape(1, D), scale[...].reshape(1, D))
        own[...] = normed.astype(jnp.bfloat16).reshape(4, QBLK, D)
        for i in range(3):
            small[6 + i].wait()
            remote(w_in[i], qkv_w.at[i, 1 - ha], w_s.at[i], w_r.at[i], other).wait_recv()
        keep_local(qkv_w.at[1, 1 - ha], w_out[0], 10)
        keep_local(qkv_w.at[2, 1 - ha], w_out[1], 11)

        def one_group(g, carry):
            def product(i):
                return jnp.dot(
                    own[...].reshape(OWN, D), qkv_w[i, g], preferred_element_type=jnp.float32
                )

            queries[g] = (product(0) * SHARP).astype(jnp.bfloat16)
            for i in range(2):
                result = product(1 + i).astype(jnp.bfloat16)
                for w, (lo, _, spare) in enumerate(WINDOWS):
                    window = result[:, lo : lo + 256]
                    if i == 1:
                        window = with_lane(window, spare, jnp.ones((OWN, 128), jnp.bfloat16))
                    mine[g, w, i] = window
            return carry

        lax.fori_loop(0, 2, one_group, 0)
        keep_local(queries, q_out, 12)
        lax.fori_loop(0, 4 * KT, place_entry, 0)
        keep_local(places, place_out, 14)

    def own_attention():
        def one_block(i, carry):
            g = i // 4
            at = pl.ds(pl.multiple_of((i % 4) * QBLK, QBLK), QBLK)
            above, below, tops = attend_windows(
                queries[g, at, :], [mine[g, w, 0, at, :] for w in range(2)], [mine[g, w, 1, at, :] for w in range(2)], False
            )
            partial[g, at, :] = above / below
            logs[g, at, :] = tops + jnp.log2(below)
            return carry

        lax.fori_loop(0, 8, one_block, 0)
        keep_local(partial, part_out, 13)
        keep_local(logs, log_out, 15)

    for p in range(3):
        for d in range(2):
            send_a(p, d).wait_recv()
            go(forward_a(p, d))
        for d in range(2):
            for da in (3, 1):
                go(send_b(p, da, d))
    for p in range(3):
        arrived(rows[p][0].at[2], af_r.at[p])
        for d in range(2):
            go(send_b(p, 2, d))
    small[2].wait()
    small[3].wait()
    lane = lax.broadcasted_iota(jnp.int32, (KT, N_PB * QB_DEV), 1)
    order = (lane & 7) * KT + lax.broadcasted_iota(jnp.int32, (KT, N_PB * QB_DEV), 0)
    code = order * 8 + blocks[...]
    size = N_PB * QB_DEV

    def tabulate(i, carry):
        firsts, lasts = [], []
        for o in range(8):
            hit = owners[...] == i * 8 + o
            firsts.append(jnp.min(jnp.where(hit, code, 511), 0, keepdims=True))
            lasts.append(jnp.max(jnp.where(hit, code, 0), 0, keepdims=True))
        first, last = jnp.concatenate(firsts, 0), jnp.concatenate(lasts, 0)
        for step in (1, 2, 4):
            first = jnp.minimum(first, pltpu.roll(first, size - step, 1))
            last = jnp.maximum(last, pltpu.roll(last, size - step, 1))
        table[pl.ds(pl.multiple_of(i * 8, 8), 8), :] = first + (last & 7) * 512
        return carry

    lax.fori_loop(0, N_PB // 8, tabulate, 0)
    to_scalars = pltpu.make_async_copy(table, sel_ref, v_s.at[9])
    to_scalars.start()

    to_scalars.wait()
    small[4].wait()
    for p in range(3):
        select(p, 0)
    for da in (0, 3, 1, 2):
        for p in range(3):
            for d in range(2):
                send_b(p, da, d).wait_recv()
                go(forward_b(p, da, d))
    for p in range(3):
        for db in (3, 1):
            select(p, db)
    own_blocks()
    own_attention()
    for p in range(3):
        relay(p, 0, 1, 2, 3)
    for p in range(3):
        arrived(rows[p][2], bf_r.at[p])
        select(p, 2)
    for db in (3, 1):
        for p in range(3):
            relay(p, db, 1, 2, 3)
    for g in (3, 1, 2):
        for p in range(3):
            relay(p, 2, g)
    arrived(kv_ref.at[:, 1], x_r)
    for copy in weights[3:]:
        copy.wait_recv()
    for copy in weights:
        copy.wait_send()
    two, one = pl.ds(0, 2), pl.ds(0, 1)
    for ref, semaphore in (
        (kv_ref.at[:, 0, one, two], a_s),
        (kv_ref.at[:, 0, one, one], af_s),
        (kv_ref.at[:, 0, two], b_s),
        (kv_ref.at[:, 0, one], bf_s),
        (kv_ref.at[:, 0, pl.ds(1, 3)], c_s),
        (kv_ref.at[:, 1], x_s),
    ):
        remote(ref, ref, semaphore, x_r, other).wait_send()
    pltpu.make_async_copy(picked.at[:, 0], kv_ref.at[:, 0, 0], l_s).wait()
    for copy in local:
        copy.wait()


HBM = pl.BlockSpec(memory_space=pltpu.HBM)


def exchange(tokens, shift, scale, owners, blocks, weights):
    dma = pltpu.SemaphoreType.DMA
    bf16 = jnp.bfloat16
    kv_shape = jax.ShapeDtypeStruct((3, 2, SIDE, SIDE, 8, HALF, PART), bf16)
    table = (N_PB, N_PB * QB_DEV)
    return pl.pallas_call(
        exchange_kernel,
        out_shape=[
            kv_shape,
            jax.ShapeDtypeStruct((8, 128), jnp.int32),
            jax.ShapeDtypeStruct((2, OWN, GRP), bf16),
            jax.ShapeDtypeStruct((2, OWN, GRP), jnp.float32),
            jax.ShapeDtypeStruct((2, OWN, GRP), jnp.float32),
        ]
        + [jax.ShapeDtypeStruct(w.shape, w.dtype) for w in weights[1:]],
        in_specs=[HBM] * 11,
        out_specs=[HBM] * 10,
        scratch_shapes=[pltpu.VMEM((SIDE, QB_DEV, HALF, PART), bf16)] * 12
        + [pltpu.VMEM((3, 4, SIDE, 8, HALF, PART), bf16)]
        + [pltpu.VMEM((QB_DEV, HALF, D), bf16)]
        + [pltpu.VMEM((D,), jnp.float32)] * 2
        + [pltpu.VMEM((KT, N_PB * QB_DEV), jnp.int32)] * 2
        + [pltpu.VMEM(table, jnp.int32), pltpu.SMEM(table, jnp.int32)]
        + [pltpu.SMEM((KT, N_PB * QB_DEV), jnp.int32), pltpu.SMEM((8, 128), jnp.int32)]
        + [
            pltpu.VMEM((4, QBLK, D), bf16),
            pltpu.VMEM((3, 2, D, GRP), bf16),
            pltpu.VMEM((2, OWN, GRP), bf16),
            pltpu.VMEM((2, 2, 2, OWN, 256), bf16),
            pltpu.VMEM((2, OWN, GRP), jnp.float32),
            pltpu.VMEM((2, OWN, GRP), jnp.float32),
        ]
        + [dma, dma((3, 2)), dma, dma((3,))]
        + [dma, dma((3, 4, 2)), dma, dma((3,))]
        + [dma, dma((3, 4)), dma((3, 3)), dma, dma, dma]
        + [dma((6,)), dma((6,)), dma, dma((16,))],
        compiler_params=pltpu.CompilerParams(
            collective_id=0, has_side_effects=True, vmem_limit_bytes=62 * MIB
        ),
        name="exchange",
    )(tokens.reshape(QB_DEV, QBLK, D), shift, scale, owners, blocks, *weights)


def pooled_kernel(tokens_ref, shift_ref, scale_ref, owner_ref, block_ref, *refs):
    w_in = refs[0:6]
    kv_ref, place_out, q_out, part_out, log_out, most_out = refs[6:12]
    w_out = refs[12:17]
    plane = refs[17:20]
    picked = refs[20]
    tok, shift, scale, owners, blocks, table, sel_ref, ranks, rank_s, owner_s, places = refs[21:32]
    own, qkv_w, queries, mine, partial, logs = refs[32:38]
    (a_s, a_r, af_s, af_r, b_s, b_r, bf_s, bf_r, c_s, c_r, x_s, x_r, l_s, w_s, w_r, t_s, v_s) = refs[38:]

    pb = lax.axis_index("pb")
    ha = lax.axis_index("ha")
    me = (pb // 16, (pb // 4) % 4, pb % 4)

    def moved(base, axis, off):
        return base + (lax.rem(me[axis] + off, SIDE) - me[axis]) * STRIDES[axis]

    def chip(axis, off):
        return {"pb": moved(pb, axis, off), "ha": ha}

    other = {"pb": pb, "ha": 1 - ha}

    def remote(src, dst, ssem, rsem, dev):
        return pltpu.make_async_remote_copy(
            src_ref=src, dst_ref=dst, send_sem=ssem, recv_sem=rsem, device_id=dev, device_id_type=MESH
        )

    half_rows = pltpu.make_async_copy(
        tokens_ref.at[:, pl.ds(pl.multiple_of(ha * HALF, HALF), HALF)], tok, t_s
    )
    small = [
        pltpu.make_async_copy(src, dst, v_s.at[i])
        for i, (src, dst) in enumerate(
            (
                (shift_ref, shift),
                (scale_ref, scale),
                (owner_ref, owners),
                (block_ref, blocks),
                (owner_ref, owner_s),
                (tokens_ref.at[pl.ds(ha * 4, 4)], own),
                (w_in[0], qkv_w.at[0, ha]),
                (w_in[1], qkv_w.at[1, ha]),
                (w_in[2], qkv_w.at[2, ha]),
            )
        )
    ]
    for copy in small[:2] + [half_rows] + small[2:]:
        copy.start()

    barrier = pltpu.get_barrier_semaphore()
    for axis in range(3):
        for off in (1, 2, 3):
            pl.semaphore_signal(barrier, 1, device_id=chip(axis, off), device_id_type=MESH)
    pl.semaphore_signal(barrier, 1, device_id=other, device_id_type=MESH)
    small[0].wait()
    small[1].wait()
    half_rows.wait()
    for t in range(QB_DEV):
        n = modulate(tok[t].astype(jnp.float32), shift[...].reshape(1, D), scale[...].reshape(1, D))
        n = n.astype(jnp.bfloat16)
        for p in range(3):
            plane[p][t] = n[:, p * PART : (p + 1) * PART]
    pl.semaphore_wait(barrier, 10)

    def go(copy):
        copy.start()

    def arrived(ref, semaphore):
        remote(ref, ref, x_s, semaphore, other).wait_recv()

    local = []

    def tiles(p, db, da, first=0, count=QB_DEV):
        return plane[p].at[pl.ds((db * SIDE + da) * QB_DEV + first, count)]

    def send_a(p, d):
        return remote(
            tiles(p, 0, 0), tiles(p, 0, 3 if d == 0 else 1), a_s, a_r.at[p, d], chip(ORDERS[p][0], 1 if d == 0 else 3)
        )

    def forward_a(p, d):
        return remote(
            tiles(p, 0, 3 if d == 0 else 1, 4 * d, 4),
            tiles(p, 0, 2, 4 * d, 4),
            af_s,
            af_r.at[p],
            chip(ORDERS[p][0], 1 if d == 0 else 3),
        )

    def send_b(p, da, d):
        return remote(
            tiles(p, 0, da),
            tiles(p, 3 if d == 0 else 1, da),
            b_s,
            b_r.at[p, da, d],
            chip(ORDERS[p][1], 1 if d == 0 else 3),
        )

    def forward_b(p, da, d):
        return remote(
            tiles(p, 3 if d == 0 else 1, da, 4 * d, 4),
            tiles(p, 2, da, 4 * d, 4),
            bf_s,
            bf_r.at[p],
            chip(ORDERS[p][1], 1 if d == 0 else 3),
        )

    def send_c(p, g, h):
        off = OFFS[g]
        return remote(
            picked.at[p, g, pl.ds(h * PIECE, PIECE)],
            kv_ref.at[p, 0, SIDE - off, pl.ds(h * PIECE, PIECE)],
            c_s,
            c_r.at[p, g - 1, h],
            chip(ORDERS[p][2], off),
        )

    def cross(p, g, h):
        part = pl.ds(h * PIECE, PIECE)
        src = picked.at[p, 0, part] if g == 0 else kv_ref.at[p, 0, SIDE - OFFS[g], part]
        return remote(src, kv_ref.at[p, 1, (SIDE - OFFS[g]) % SIDE, part], x_s, x_r, other)

    def select(p, g, h):
        lane = moved(pb, ORDERS[p][2], OFFS[g]) * QB_DEV

        def pick(i, carry):
            at = h * PIECE + i
            picked[p, g, at] = plane[p][sel_ref[p, at, lane]]
            return carry

        lax.fori_loop(0, PIECE, pick, 0, unroll=PIECE)

    for p in range(3):
        for d in range(2):
            go(send_a(p, d))
    for p in range(3):
        for d in range(2):
            go(send_b(p, 0, d))
    weights = [
        remote(w_in[i], qkv_w.at[i, ha] if i < 3 else w_out[i - 1], w_s.at[i], w_r.at[i], other)
        for i in range(6)
    ]
    for copy in weights:
        go(copy)

    def keep_local(src, dst, number):
        local.append(pltpu.make_async_copy(src, dst, v_s.at[number]))
        local[-1].start()

    def place_entry(e, carry):
        i, j = e // KT, e % KT
        at = pb * QB_DEV + ha * 4 + i
        owner = owner_s[j, at]
        for p in range(3):
            c = ORDERS[p][2]
            rel = (owner // STRIDES[c] - me[c]) & 3
            places[p, e] = rel * SIDE * 8 + jnp.minimum(rank_s[c, j, at], CAP - 1)
        return carry

    def own_blocks():
        small[5].wait()
        stream = own[...].reshape(OWN, D).astype(jnp.float32)
        normed = modulate(stream, shift[...].reshape(1, D), scale[...].reshape(1, D))
        own[...] = normed.astype(jnp.bfloat16).reshape(4, QBLK, D)
        for i in range(3):
            small[6 + i].wait()
            remote(w_in[i], qkv_w.at[i, 1 - ha], w_s.at[i], w_r.at[i], other).wait_recv()
        keep_local(qkv_w.at[1, 1 - ha], w_out[0], 16)
        keep_local(qkv_w.at[2, 1 - ha], w_out[1], 11)

        def one_group(g, carry):
            def product(i):
                return jnp.dot(
                    own[...].reshape(OWN, D), qkv_w[i, g], preferred_element_type=jnp.float32
                )

            queries[g] = (product(0) * SHARP).astype(jnp.bfloat16)
            for i in range(2):
                result = product(1 + i).astype(jnp.bfloat16)
                for w, (lo, _, spare) in enumerate(WINDOWS):
                    window = result[:, lo : lo + 256]
                    if i == 1:
                        window = with_lane(window, spare, jnp.ones((OWN, 128), jnp.bfloat16))
                    mine[g, w, i] = window
            return carry

        lax.fori_loop(0, 2, one_group, 0)
        keep_local(queries, q_out, 12)
        lax.fori_loop(0, 4 * KT, place_entry, 0)
        keep_local(places, place_out, 14)

    def own_attention():
        def one_block(i, carry):
            g = i // 4
            at = pl.ds(pl.multiple_of((i % 4) * QBLK, QBLK), QBLK)
            above, below, tops = attend_windows(
                queries[g, at, :], [mine[g, w, 0, at, :] for w in range(2)], [mine[g, w, 1, at, :] for w in range(2)], False
            )
            partial[g, at, :] = above / below
            logs[g, at, :] = tops + jnp.log2(below)
            return carry

        lax.fori_loop(0, 8, one_block, 0)
        keep_local(partial, part_out, 13)
        keep_local(logs, log_out, 15)

    for p in range(3):
        for d in range(2):
            send_a(p, d).wait_recv()
            go(forward_a(p, d))
        for d in range(2):
            for da in (3, 1):
                go(send_b(p, da, d))
    for p in range(3):
        arrived(tiles(p, 0, 2), af_r.at[p])
        for d in range(2):
            go(send_b(p, 2, d))
    small[2].wait()
    small[3].wait()
    size = N_PB * QB_DEV
    wide = (KT, size)
    lane = lax.broadcasted_iota(jnp.int32, wide, 1) & 7
    line = lax.broadcasted_iota(jnp.int32, wide, 0)
    coords = [(owners[...] // stride) & 3 for stride in STRIDES]

    def ranked(marks):
        column = marks
        for step in (1, 2, 4):
            column = column + jnp.where(line >= step, pltpu.roll(column, step, 0), 0)
        total = jnp.broadcast_to(jnp.sum(marks, 0, keepdims=True), wide)
        row = total
        for step in (1, 2, 4):
            row = row + jnp.where(lane >= step, pltpu.roll(row, step, 1), 0)
        return column - marks + row - total

    top = jnp.zeros(wide, jnp.int32)
    for axis in range(3):
        rank = jnp.zeros(wide, jnp.int32)
        for value in range(SIDE):
            here = coords[axis] == value
            rank = jnp.where(here, ranked(here.astype(jnp.int32)), rank)
        ranks[axis] = rank
        top = jnp.maximum(top, rank)
    most_out[0, 0] = jnp.max(top)

    for p in range(3):
        a, b, c = ORDERS[p]
        rel_b, rel_a = (coords[b] - me[b]) & 3, (coords[a] - me[a]) & 3
        number = (rel_b * SIDE + rel_a) * QB_DEV + blocks[...]
        slot = jnp.where(coords[c] == me[c], ranks[c], -1)

        def tabulate(i, carry):
            found = [
                jnp.max(jnp.where(slot == i * 8 + n, number, 0), 0, keepdims=True) for n in range(8)
            ]
            found = jnp.concatenate(found, 0)
            for step in (1, 2, 4):
                found = jnp.maximum(found, pltpu.roll(found, size - step, 1))
            table[p, pl.ds(pl.multiple_of(i * 8, 8), 8), :] = found
            return carry

        lax.fori_loop(0, SLOTS // 8, tabulate, 0)
    to_scalars = pltpu.make_async_copy(table, sel_ref, v_s.at[9])
    to_scalars.start()
    ranks_out = pltpu.make_async_copy(ranks, rank_s, v_s.at[10])
    ranks_out.start()
    for da in (0, 3, 1, 2):
        for p in range(3):
            for d in range(2):
                send_b(p, da, d).wait_recv()
                go(forward_b(p, da, d))
    to_scalars.wait()
    ranks_out.wait()
    small[4].wait()
    own_blocks()
    for p in range(3):
        arrived(plane[p].at[pl.ds(2 * SIDE * QB_DEV, SIDE * QB_DEV)], bf_r.at[p])
        for h in range(PIECES):
            for g in (3, 1, 2):
                select(p, g, h)
                go(send_c(p, g, h))
    for p in range(3):
        for h in range(PIECES):
            select(p, 0, h)
            go(cross(p, 0, h))
        pltpu.make_async_copy(picked.at[p, 0], kv_ref.at[p, 0, 0, pl.ds(0, CAP)], l_s).start()
    own_attention()
    for h in range(PIECES):
        for g in (3, 1, 2):
            for p in range(3):
                send_c(p, g, h).wait_recv()
                go(cross(p, g, h))
    arrived(kv_ref.at[:, 1, :, pl.ds(0, CAP)], x_r)
    for copy in weights[3:]:
        copy.wait_recv()
    for copy in weights:
        copy.wait_send()
    for ref, semaphore in (
        (kv_ref.at[:, 0, pl.ds(0, 2), pl.ds(0, 8)], a_s),
        (kv_ref.at[:, 0, pl.ds(0, 1), pl.ds(0, 8)], af_s),
        (kv_ref.at[:, 0, :, pl.ds(0, 16)], b_s),
        (kv_ref.at[:, 0, :, pl.ds(0, 8)], bf_s),
        (picked.at[:, pl.ds(1, 3)], c_s),
        (kv_ref.at[:, 1, :, pl.ds(0, CAP)], x_s),
    ):
        remote(ref, ref, semaphore, x_r, other).wait_send()
    pltpu.make_async_copy(picked.at[:, 0], kv_ref.at[:, 0, 0, pl.ds(0, CAP)], l_s).wait()
    for copy in local:
        copy.wait()


def exchange_pooled(tokens, shift, scale, owners, blocks, weights):
    dma = pltpu.SemaphoreType.DMA
    bf16 = jnp.bfloat16
    kv_shape = jax.ShapeDtypeStruct((3, 2, SIDE, SIDE * 8, HALF, PART), bf16)
    table = (3, SLOTS, N_PB * QB_DEV)
    ranks = (3, KT, N_PB * QB_DEV)
    return pl.pallas_call(
        pooled_kernel,
        out_shape=[
            kv_shape,
            jax.ShapeDtypeStruct((8, 128), jnp.int32),
            jax.ShapeDtypeStruct((2, OWN, GRP), bf16),
            jax.ShapeDtypeStruct((2, OWN, GRP), jnp.float32),
            jax.ShapeDtypeStruct((2, OWN, GRP), jnp.float32),
            jax.ShapeDtypeStruct((1, 1), jnp.int32),
        ]
        + [jax.ShapeDtypeStruct(w.shape, w.dtype) for w in weights[1:]],
        in_specs=[HBM] * 11,
        out_specs=[HBM] * 5 + [pl.BlockSpec(memory_space=pltpu.SMEM)] + [HBM] * 5,
        scratch_shapes=[pltpu.VMEM((SIDE * SIDE * QB_DEV, HALF, PART), bf16)] * 3
        + [pltpu.VMEM((3, 4, CAP, HALF, PART), bf16)]
        + [pltpu.VMEM((QB_DEV, HALF, D), bf16)]
        + [pltpu.VMEM((D,), jnp.float32)] * 2
        + [pltpu.VMEM((KT, N_PB * QB_DEV), jnp.int32)] * 2
        + [pltpu.VMEM(table, jnp.int32), pltpu.SMEM(table, jnp.int32)]
        + [pltpu.VMEM(ranks, jnp.int32), pltpu.SMEM(ranks, jnp.int32)]
        + [pltpu.SMEM((KT, N_PB * QB_DEV), jnp.int32), pltpu.SMEM((8, 128), jnp.int32)]
        + [
            pltpu.VMEM((4, QBLK, D), bf16),
            pltpu.VMEM((3, 2, D, GRP), bf16),
            pltpu.VMEM((2, OWN, GRP), bf16),
            pltpu.VMEM((2, 2, 2, OWN, 256), bf16),
            pltpu.VMEM((2, OWN, GRP), jnp.float32),
            pltpu.VMEM((2, OWN, GRP), jnp.float32),
        ]
        + [dma, dma((3, 2)), dma, dma((3,))]
        + [dma, dma((3, 4, 2)), dma, dma((3,))]
        + [dma, dma((3, 3, PIECES)), dma, dma, dma]
        + [dma((6,)), dma((6,)), dma, dma((17,))],
        compiler_params=pltpu.CompilerParams(
            collective_id=1, has_side_effects=True, vmem_limit_bytes=62 * MIB
        ),
        name="exchange_pooled",
    )(tokens.reshape(QB_DEV, QBLK, D), shift, scale, owners, blocks, *weights)


def block_kernel(count_ref, place_ref, *refs):
    vectors_h = refs[0:4]
    tokens_ref, q_h, part_h, log_h, kv_ref = refs[4:9]
    own_h, other_h = refs[9:14], refs[14:19]
    out_ref = refs[19]
    vectors = refs[20:24]
    x_refs = refs[24:26]
    key_refs = refs[26:28]
    value_refs = refs[28:30]
    tok, queries, partial, logs, att = refs[30:35]
    wkv, wo, w1, w2 = refs[35:39]
    sem, vsem, gsem = refs[39:]
    gate_a, shift_m, scale_m, gate_m = vectors
    bf16 = jnp.bfloat16

    def row(vector):
        return vector[...].reshape(1, D)

    ha = lax.axis_index("ha")
    late = [
        pltpu.make_async_copy(src, dst, vsem.at[i])
        for i, (src, dst) in enumerate(
            [(vectors_h[i], vectors[i]) for i in range(4)]
            + [(tokens_ref.at[pl.ds(pl.multiple_of(ha * OWN, OWN), OWN)], tok)]
        )
    ]
    early = [
        pltpu.make_async_copy(src, dst, vsem.at[5 + i])
        for i, (src, dst) in enumerate(((q_h, queries), (part_h, partial), (log_h, logs)))
    ]
    loads = []
    for i in range(5):
        pair = []
        for src, at, number in ((own_h[i], ha, i), (other_h[i], 1 - ha, 5 + i)):
            if i < 2:
                dst = wkv.at[at, :, pl.ds(i * GRP, GRP)]
            elif i == 2:
                dst = wo.at[pl.ds(pl.multiple_of(at * GRP, GRP), GRP)]
            else:
                dst = (w1, w2)[i - 3].at[at]
            pair.append(pltpu.make_async_copy(src, dst, sem.at[number]))
        loads.append(pair)

    def begin(*numbers):
        for i in numbers:
            loads[i][0].start()
            loads[i][1].start()

    def ready(*numbers):
        for i in numbers:
            loads[i][0].wait()
            loads[i][1].wait()

    def gather(blk, slot):
        for j in range(KT):
            for p in range(3):
                pltpu.make_async_copy(
                    kv_ref.at[p, :, place_ref[p, blk * KT + j]],
                    x_refs[slot].at[j, :, :, pl.ds(p * PART, PART)],
                    gsem.at[slot],
                ).start()

    def gathered(slot):
        pltpu.make_async_copy(x_refs[slot], x_refs[slot], gsem.at[slot]).wait()

    def project(blk, slot):
        x = x_refs[slot][...].reshape(ROWS, D)
        live = count_ref[ha * 4 + blk] * QBLK
        place = lax.broadcasted_iota(jnp.int32, (ROWS, 128), 0)
        bias = jnp.where(place < live, 0.0, DEAD).astype(bf16)
        for g in range(2):
            both = jnp.dot(x, wkv[g], preferred_element_type=jnp.float32).astype(bf16)
            k, v = both[:, :GRP], both[:, GRP:]
            for w, (lo, _, spare) in enumerate(WINDOWS):
                key_refs[slot][g, w] = with_lane(k[:, lo : lo + 256], spare, bias)
                value_refs[slot][g, w] = with_lane(v[:, lo : lo + 256], spare, jnp.ones_like(bias))

    def attend(blk, slot):
        at = slice(blk * QBLK, (blk + 1) * QBLK)
        for g in range(2):
            above, below, tops = attend_windows(
                queries[g, at, :],
                [key_refs[slot].at[g, w][...] for w in range(2)],
                [value_refs[slot].at[g, w][...] for w in range(2)],
                True,
            )
            log = logs[g, at, :]
            most = jnp.maximum(tops, log)
            listed, mine = jnp.exp2(tops - most), jnp.exp2(log - most)
            result = (above * listed + partial[g, at, :] * mine) / (below * listed + mine)
            att[at, g * GRP : (g + 1) * GRP] = result.astype(bf16)

    begin(0, 1)
    gather(0, 0)
    ready(0, 1)
    gathered(0)
    for copy in early:
        copy.start()
    gather(1, 1)
    for copy in late:
        copy.start()
    begin(2, 3, 4)
    project(0, 0)
    for copy in early:
        copy.wait()
    for blk in range(4):
        slot = blk % 2
        if blk < 2:
            gather(blk + 2, slot)
        if blk < 3:
            gathered(1 - slot)
            project(blk + 1, 1 - slot)
        attend(blk, slot)

    for copy in late:
        copy.wait()
    ready(2)
    projected = jnp.dot(att[...], wo[...], preferred_element_type=jnp.float32)
    residual = (tok[...].astype(jnp.float32) + row(gate_a) * projected).astype(bf16)
    normed = modulate(residual.astype(jnp.float32), row(shift_m), row(scale_m)).astype(bf16)
    ready(3, 4)
    expanded = jnp.zeros((OWN, D), jnp.float32)
    for g in range(2):
        for lo in range(0, FF // 2, CHUNK):
            hidden = jnp.dot(normed, w1[g, :, lo : lo + CHUNK], preferred_element_type=jnp.float32)
            hidden = jax.nn.gelu(hidden, approximate=True).astype(bf16)
            expanded += jnp.dot(hidden, w2[g, lo : lo + CHUNK, :], preferred_element_type=jnp.float32)
    out_ref[...] = (residual.astype(jnp.float32) + row(gate_m) * expanded).astype(bf16)


def block(counts, places, vectors, tokens, queries, partial, logs, kv, own, other):
    bf16 = jnp.bfloat16
    dma = pltpu.SemaphoreType.DMA
    kv = kv.reshape(3, 2, -1, HALF, PART)
    return pl.pallas_call(
        block_kernel,
        out_shape=jax.ShapeDtypeStruct((OWN, D), bf16),
        in_specs=[pl.BlockSpec(memory_space=pltpu.SMEM)] * 2 + [HBM] * 19,
        out_specs=pl.BlockSpec(memory_space=pltpu.VMEM),
        scratch_shapes=[pltpu.VMEM((D,), jnp.float32)] * 4
        + [pltpu.VMEM((KT, 2, HALF, D), bf16)] * 2
        + [pltpu.VMEM((2, 2, ROWS, 256), bf16)] * 4
        + [
            pltpu.VMEM((OWN, D), bf16),
            pltpu.VMEM((2, OWN, GRP), bf16),
            pltpu.VMEM((2, OWN, GRP), jnp.float32),
            pltpu.VMEM((2, OWN, GRP), jnp.float32),
            pltpu.VMEM((OWN, D), bf16),
            pltpu.VMEM((2, D, 2 * GRP), bf16),
            pltpu.VMEM((D, D), bf16),
            pltpu.VMEM((2, D, FF // 2), bf16),
            pltpu.VMEM((2, FF // 2, D), bf16),
        ]
        + [dma((10,)), dma((8,)), dma((2,))],
        compiler_params=pltpu.CompilerParams(vmem_limit_bytes=62 * MIB),
        name="block",
    )(counts, places, *vectors, tokens, queries, partial, logs, kv, *own, *other)


def shards(
    tokens,
    shift_attn,
    scale_attn,
    gate_attn,
    shift_mlp,
    scale_mlp,
    gate_mlp,
    w_query,
    w_key,
    w_value,
    w_out,
    w_fc1,
    w_fc2,
    contact_owner,
    contact_local,
    contact_count,
):
    vectors = (gate_attn, shift_mlp, scale_mlp, gate_mlp)
    own = (w_query, w_key, w_value, w_out, w_fc1, w_fc2)
    owners, blocks = contact_owner.T, contact_local.T
    args = (tokens, shift_attn, scale_attn, owners, blocks, own)
    kv, places, queries, partial, logs, most, *other = exchange_pooled(*args)

    def crowded():
        other_kv, other_places, *_ = exchange(*args)
        return other_kv.reshape(kv.shape), other_places

    kv_used, places_used = lax.cond(most[0, 0] < CAP, lambda: (kv, places), crowded)
    return block(contact_count, places_used, vectors, tokens, queries, partial, logs, kv_used, own[1:], other)


def solution(mesh):
    placed = (
        P("pb", None),
        P(),
        P(),
        P(),
        P(),
        P(),
        P(),
        P(None, "ha"),
        P(None, "ha"),
        P(None, "ha"),
        P("ha", None),
        P(None, "ha"),
        P("ha", None),
        P(),
        P(),
        P("pb"),
    )
    return jax.shard_map(
        shards, mesh=mesh, in_specs=placed, out_specs=P(("pb", "ha"), None), check_vma=False
    )
```

```python
import jax
import jax.numpy as jnp
from jax import lax
from jax.experimental import pallas as pl
from jax.experimental.pallas import tpu as pltpu
from jax.sharding import PartitionSpec as P

D = 768
HEADS = 16
HDIM = 48
FF = 3072
QBLK = 128
KT = 8
QB_DEV = 8
N_PB = 64
SIDE = 4
HALF = QBLK // 2
PART = D // 3
GRP = D // 2
MIB = 2**20
MESH = pl.DeviceIdType.MESH

ORDERS = ((2, 1, 0), (1, 0, 2), (0, 2, 1))
STRIDES = (16, 4, 1)
OFFS = (0, 1, 3, 2)

CAP = 22
PIECES = 2
PIECE = CAP // PIECES
SLOTS = -(-CAP // 8) * 8

epsilon = 1e-06


def modulate(stream, shift, scale):
    center = stream - jnp.mean(stream, -1, keepdims=True)
    spread = jnp.mean(center * center, -1, keepdims=True)
    return center * lax.rsqrt(spread + epsilon) * (1.0 + scale) + shift


ROWS = KT * QBLK
OWN = 4 * QBLK
SHARP = HDIM**-0.5 * 1.4426950408889634
WINDOWS = ((0, (0, 1, 2, 3, 4), 255), (128, (5, 6, 7), 0))
CHUNK = 512
DEAD = -1e30


def with_lane(value, lane, fill):
    at = lax.broadcasted_iota(jnp.int32, (value.shape[0], 128), 1)
    left, right = value[:, :128], value[:, 128:]
    if lane == 0:
        left = jnp.where(at == 0, fill, left)
    else:
        right = jnp.where(at == 127, fill, right)
    return jnp.concatenate([left, right], 1)


def attend_windows(q, keys, values, biased):
    lane = lax.broadcasted_iota(jnp.int32, (QBLK, 256), 1)
    found = []
    for w, (lo, heads, spare) in enumerate(WINDOWS):
        q_part = q[:, lo : lo + 256]
        masks = [(lane >= h * HDIM - lo) & (lane < (h + 1) * HDIM - lo) for h in heads]
        fixed = jnp.zeros_like(q_part)
        if biased:
            fixed = jnp.where(lane == spare, jnp.ones_like(q_part), fixed)
        stacked = jnp.concatenate([jnp.where(m, q_part, fixed) for m in masks], 0)
        scores = lax.dot_general(
            stacked, keys[w], (((1,), (1,)), ((), ())), preferred_element_type=jnp.float32
        )
        top = jnp.max(scores, -1, keepdims=True)
        weights = jnp.exp2(scores - top).astype(jnp.bfloat16)
        outs = jnp.dot(weights, values[w], preferred_element_type=jnp.float32)
        totals = outs[:, spare : spare + 1]
        above = jnp.zeros((QBLK, 256), jnp.float32)
        below = jnp.ones((QBLK, 256), jnp.float32)
        tops = jnp.zeros((QBLK, 256), jnp.float32)
        for i, m in enumerate(masks):
            rows = slice(i * QBLK, (i + 1) * QBLK)
            above = jnp.where(m, outs[rows], above)
            below = jnp.where(m, totals[rows], below)
            tops = jnp.where(m, top[rows], tops)
        found.append((above, below, tops))
    use_first = lane[:, :128] + 128 < 5 * HDIM
    return [
        jnp.concatenate([one[:, :128], jnp.where(use_first, one[:, 128:], two[:, :128]), two[:, 128:]], 1)
        for one, two in zip(*found)
    ]


def exchange_kernel(tokens_ref, shift_ref, scale_ref, owner_ref, block_ref, *refs):
    w_in = refs[0:6]
    kv_ref, place_out, q_out, part_out, log_out = refs[6:11]
    w_out = refs[11:16]
    rows = [refs[16 + 4 * p : 20 + 4 * p] for p in range(3)]
    picked = refs[28]
    tok, shift, scale, owners, blocks, table, sel_ref, owner_s, places = refs[29:38]
    own, qkv_w, queries, mine, partial, logs = refs[38:44]
    (a_s, a_r, af_s, af_r, b_s, b_r, bf_s, bf_r, c_s, c_r, last_r, x_s, x_r, l_s, w_s, w_r, t_s, v_s) = refs[44:]

    pb = lax.axis_index("pb")
    ha = lax.axis_index("ha")
    me = (pb // 16, (pb // 4) % 4, pb % 4)

    def moved(base, axis, off):
        return base + (lax.rem(me[axis] + off, SIDE) - me[axis]) * STRIDES[axis]

    def chip(axis, off):
        return {"pb": moved(pb, axis, off), "ha": ha}

    other = {"pb": pb, "ha": 1 - ha}

    def remote(src, dst, ssem, rsem, dev):
        return pltpu.make_async_remote_copy(
            src_ref=src, dst_ref=dst, send_sem=ssem, recv_sem=rsem, device_id=dev, device_id_type=MESH
        )

    half_rows = pltpu.make_async_copy(
        tokens_ref.at[:, pl.ds(pl.multiple_of(ha * HALF, HALF), HALF)], tok, t_s
    )
    small = [
        pltpu.make_async_copy(src, dst, v_s.at[i])
        for i, (src, dst) in enumerate(
            (
                (shift_ref, shift),
                (scale_ref, scale),
                (owner_ref, owners),
                (block_ref, blocks),
                (owner_ref, owner_s),
                (tokens_ref.at[pl.ds(ha * 4, 4)], own),
                (w_in[0], qkv_w.at[0, ha]),
                (w_in[1], qkv_w.at[1, ha]),
                (w_in[2], qkv_w.at[2, ha]),
            )
        )
    ]
    for copy in small[:2] + [half_rows] + small[2:]:
        copy.start()

    barrier = pltpu.get_barrier_semaphore()
    for axis in range(3):
        for off in (1, 2, 3):
            pl.semaphore_signal(barrier, 1, device_id=chip(axis, off), device_id_type=MESH)
    pl.semaphore_signal(barrier, 1, device_id=other, device_id_type=MESH)
    small[0].wait()
    small[1].wait()
    half_rows.wait()
    for t in range(QB_DEV):
        n = modulate(tok[t].astype(jnp.float32), shift[...].reshape(1, D), scale[...].reshape(1, D))
        n = n.astype(jnp.bfloat16)
        for p in range(3):
            rows[p][0][0, t] = n[:, p * PART : (p + 1) * PART]
    pl.semaphore_wait(barrier, 10)

    def go(copy):
        copy.start()

    def arrived(ref, semaphore):
        remote(ref, ref, x_s, semaphore, other).wait_recv()

    local = []

    def send_a(p, d):
        a = ORDERS[p][0]
        return remote(
            rows[p][0].at[0],
            rows[p][0].at[3 if d == 0 else 1],
            a_s,
            a_r.at[p, d],
            chip(a, 1 if d == 0 else 3),
        )

    def forward_a(p, d):
        a = ORDERS[p][0]
        part = pl.ds(4 * d, 4)
        return remote(
            rows[p][0].at[3 if d == 0 else 1, part],
            rows[p][0].at[2, part],
            af_s,
            af_r.at[p],
            chip(a, 1 if d == 0 else 3),
        )

    def send_b(p, da, d):
        b = ORDERS[p][1]
        return remote(
            rows[p][0].at[da],
            rows[p][3 if d == 0 else 1].at[da],
            b_s,
            b_r.at[p, da, d],
            chip(b, 1 if d == 0 else 3),
        )

    def forward_b(p, da, d):
        b = ORDERS[p][1]
        part = pl.ds(4 * d, 4)
        return remote(
            rows[p][3 if d == 0 else 1].at[da, part],
            rows[p][2].at[da, part],
            bf_s,
            bf_r.at[p],
            chip(b, 1 if d == 0 else 3),
        )

    def send_c(p, db, g):
        c = ORDERS[p][2]
        off = OFFS[g]
        return remote(
            picked.at[p, g, db],
            kv_ref.at[p, 0, SIDE - off, db],
            c_s,
            last_r.at[p, g - 1] if db == 2 else c_r.at[p, db],
            chip(c, off),
        )

    def cross(p, db, g):
        src = picked.at[p, 0, db] if g == 0 else kv_ref.at[p, 0, SIDE - OFFS[g], db]
        return remote(src, kv_ref.at[p, 1, (SIDE - OFFS[g]) % SIDE, db], x_s, x_r, other)

    def keep(p, db):
        return pltpu.make_async_copy(picked.at[p, 0, db], kv_ref.at[p, 0, 0, db], l_s)

    def select(p, db):
        a, b, c = ORDERS[p]
        for g in range(4):
            dest = moved(pb, c, OFFS[g])

            def pick(j, carry):
                da, k = j // 2, j % 2
                owner = moved(moved(pb, b, db), a, da)
                code = sel_ref[owner, dest * QB_DEV]
                number = jnp.where(k == 0, code & 7, (code >> 9) & 7)
                picked[p, g, db, j] = rows[p][db][da, number]
                return carry

            lax.fori_loop(0, 8, pick, 0)
        for g in (3, 1, 2):
            go(send_c(p, db, g))
        keep(p, db).start()
        go(cross(p, db, 0))

    def relay(p, db, *groups):
        if db != 2:
            arrived(kv_ref.at[p, 0, pl.ds(1, 3), db], c_r.at[p, db])
        for g in groups:
            if db == 2:
                send_c(p, db, g).wait_recv()
            go(cross(p, db, g))

    for p in range(3):
        for d in range(2):
            go(send_a(p, d))
    for p in range(3):
        for d in range(2):
            go(send_b(p, 0, d))
    weights = [
        remote(w_in[i], qkv_w.at[i, ha] if i < 3 else w_out[i - 1], w_s.at[i], w_r.at[i], other)
        for i in range(6)
    ]
    for copy in weights:
        go(copy)

    def keep_local(src, dst, number):
        local.append(pltpu.make_async_copy(src, dst, v_s.at[number]))
        local[-1].start()

    def place_entry(e, carry):
        i, j = e // KT, e % KT
        owner = owner_s[j, pb * QB_DEV + ha * 4 + i]
        first = (sel_ref[owner, pb * QB_DEV] & 511) >> 3
        k = jnp.where(first == ha * 4 * KT + e, 0, 1)
        rel = ((owner // 16 - me[0]) & 3, (owner // 4 - me[1]) & 3, (owner - me[2]) & 3)
        for p in range(3):
            a, b, c = ORDERS[p]
            places[p, e] = ((rel[c] * 4 + rel[b]) * 4 + rel[a]) * 2 + k
        return carry

    def own_blocks():
        small[5].wait()
        stream = own[...].reshape(OWN, D).astype(jnp.float32)
        normed = modulate(stream, shift[...].reshape(1, D), scale[...].reshape(1, D))
        own[...] = normed.astype(jnp.bfloat16).reshape(4, QBLK, D)
        for i in range(3):
            small[6 + i].wait()
            remote(w_in[i], qkv_w.at[i, 1 - ha], w_s.at[i], w_r.at[i], other).wait_recv()
        keep_local(qkv_w.at[1, 1 - ha], w_out[0], 10)
        keep_local(qkv_w.at[2, 1 - ha], w_out[1], 11)

        def one_group(g, carry):
            def product(i):
                return jnp.dot(
                    own[...].reshape(OWN, D), qkv_w[i, g], preferred_element_type=jnp.float32
                )

            queries[g] = (product(0) * SHARP).astype(jnp.bfloat16)
            for i in range(2):
                result = product(1 + i).astype(jnp.bfloat16)
                for w, (lo, _, spare) in enumerate(WINDOWS):
                    window = result[:, lo : lo + 256]
                    if i == 1:
                        window = with_lane(window, spare, jnp.ones((OWN, 128), jnp.bfloat16))
                    mine[g, w, i] = window
            return carry

        lax.fori_loop(0, 2, one_group, 0)
        keep_local(queries, q_out, 12)
        lax.fori_loop(0, 4 * KT, place_entry, 0)
        keep_local(places, place_out, 14)

    def own_attention():
        def one_block(i, carry):
            g = i // 4
            at = pl.ds(pl.multiple_of((i % 4) * QBLK, QBLK), QBLK)
            above, below, tops = attend_windows(
                queries[g, at, :], [mine[g, w, 0, at, :] for w in range(2)], [mine[g, w, 1, at, :] for w in range(2)], False
            )
            partial[g, at, :] = above / below
            logs[g, at, :] = tops + jnp.log2(below)
            return carry

        lax.fori_loop(0, 8, one_block, 0)
        keep_local(partial, part_out, 13)
        keep_local(logs, log_out, 15)

    for p in range(3):
        for d in range(2):
            send_a(p, d).wait_recv()
            go(forward_a(p, d))
        for d in range(2):
            for da in (3, 1):
                go(send_b(p, da, d))
    for p in range(3):
        arrived(rows[p][0].at[2], af_r.at[p])
        for d in range(2):
            go(send_b(p, 2, d))
    small[2].wait()
    small[3].wait()
    lane = lax.broadcasted_iota(jnp.int32, (KT, N_PB * QB_DEV), 1)
    order = (lane & 7) * KT + lax.broadcasted_iota(jnp.int32, (KT, N_PB * QB_DEV), 0)
    code = order * 8 + blocks[...]
    size = N_PB * QB_DEV

    def tabulate(i, carry):
        firsts, lasts = [], []
        for o in range(8):
            hit = owners[...] == i * 8 + o
            firsts.append(jnp.min(jnp.where(hit, code, 511), 0, keepdims=True))
            lasts.append(jnp.max(jnp.where(hit, code, 0), 0, keepdims=True))
        first, last = jnp.concatenate(firsts, 0), jnp.concatenate(lasts, 0)
        for step in (1, 2, 4):
            first = jnp.minimum(first, pltpu.roll(first, size - step, 1))
            last = jnp.maximum(last, pltpu.roll(last, size - step, 1))
        table[pl.ds(pl.multiple_of(i * 8, 8), 8), :] = first + (last & 7) * 512
        return carry

    lax.fori_loop(0, N_PB // 8, tabulate, 0)
    to_scalars = pltpu.make_async_copy(table, sel_ref, v_s.at[9])
    to_scalars.start()

    to_scalars.wait()
    small[4].wait()
    for p in range(3):
        select(p, 0)
    for da in (0, 3, 1, 2):
        for p in range(3):
            for d in range(2):
                send_b(p, da, d).wait_recv()
                go(forward_b(p, da, d))
    for p in range(3):
        for db in (3, 1):
            select(p, db)
    own_blocks()
    own_attention()
    for p in range(3):
        relay(p, 0, 1, 2, 3)
    for p in range(3):
        arrived(rows[p][2], bf_r.at[p])
        select(p, 2)
    for db in (3, 1):
        for p in range(3):
            relay(p, db, 1, 2, 3)
    for g in (3, 1, 2):
        for p in range(3):
            relay(p, 2, g)
    arrived(kv_ref.at[:, 1], x_r)
    for copy in weights[3:]:
        copy.wait_recv()
    for copy in weights:
        copy.wait_send()
    two, one = pl.ds(0, 2), pl.ds(0, 1)
    for ref, semaphore in (
        (kv_ref.at[:, 0, one, two], a_s),
        (kv_ref.at[:, 0, one, one], af_s),
        (kv_ref.at[:, 0, two], b_s),
        (kv_ref.at[:, 0, one], bf_s),
        (kv_ref.at[:, 0, pl.ds(1, 3)], c_s),
        (kv_ref.at[:, 1], x_s),
    ):
        remote(ref, ref, semaphore, x_r, other).wait_send()
    pltpu.make_async_copy(picked.at[:, 0], kv_ref.at[:, 0, 0], l_s).wait()
    for copy in local:
        copy.wait()


HBM = pl.BlockSpec(memory_space=pltpu.HBM)


def exchange(tokens, shift, scale, owners, blocks, weights):
    dma = pltpu.SemaphoreType.DMA
    bf16 = jnp.bfloat16
    kv_shape = jax.ShapeDtypeStruct((3, 2, SIDE, SIDE, 8, HALF, PART), bf16)
    table = (N_PB, N_PB * QB_DEV)
    return pl.pallas_call(
        exchange_kernel,
        out_shape=[
            kv_shape,
            jax.ShapeDtypeStruct((8, 128), jnp.int32),
            jax.ShapeDtypeStruct((2, OWN, GRP), bf16),
            jax.ShapeDtypeStruct((2, OWN, GRP), jnp.float32),
            jax.ShapeDtypeStruct((2, OWN, GRP), jnp.float32),
        ]
        + [jax.ShapeDtypeStruct(w.shape, w.dtype) for w in weights[1:]],
        in_specs=[HBM] * 11,
        out_specs=[HBM] * 10,
        scratch_shapes=[pltpu.VMEM((SIDE, QB_DEV, HALF, PART), bf16)] * 12
        + [pltpu.VMEM((3, 4, SIDE, 8, HALF, PART), bf16)]
        + [pltpu.VMEM((QB_DEV, HALF, D), bf16)]
        + [pltpu.VMEM((D,), jnp.float32)] * 2
        + [pltpu.VMEM((KT, N_PB * QB_DEV), jnp.int32)] * 2
        + [pltpu.VMEM(table, jnp.int32), pltpu.SMEM(table, jnp.int32)]
        + [pltpu.SMEM((KT, N_PB * QB_DEV), jnp.int32), pltpu.SMEM((8, 128), jnp.int32)]
        + [
            pltpu.VMEM((4, QBLK, D), bf16),
            pltpu.VMEM((3, 2, D, GRP), bf16),
            pltpu.VMEM((2, OWN, GRP), bf16),
            pltpu.VMEM((2, 2, 2, OWN, 256), bf16),
            pltpu.VMEM((2, OWN, GRP), jnp.float32),
            pltpu.VMEM((2, OWN, GRP), jnp.float32),
        ]
        + [dma, dma((3, 2)), dma, dma((3,))]
        + [dma, dma((3, 4, 2)), dma, dma((3,))]
        + [dma, dma((3, 4)), dma((3, 3)), dma, dma, dma]
        + [dma((6,)), dma((6,)), dma, dma((16,))],
        compiler_params=pltpu.CompilerParams(
            collective_id=0, has_side_effects=True, vmem_limit_bytes=62 * MIB
        ),
        name="exchange",
    )(tokens.reshape(QB_DEV, QBLK, D), shift, scale, owners, blocks, *weights)


def pooled_kernel(tokens_ref, shift_ref, scale_ref, owner_ref, block_ref, *refs):
    w_in = refs[0:6]
    kv_ref, place_out, q_out, part_out, log_out, most_out = refs[6:12]
    w_out = refs[12:17]
    plane = refs[17:20]
    picked = refs[20]
    tok, shift, scale, owners, blocks, table, sel_ref, ranks, rank_s, owner_s, places = refs[21:32]
    own, qkv_w, queries, mine, partial, logs = refs[32:38]
    (a_s, a_r, af_s, af_r, b_s, b_r, bf_s, bf_r, c_s, c_r, x_s, x_r, l_s, w_s, w_r, t_s, v_s) = refs[38:]

    pb = lax.axis_index("pb")
    ha = lax.axis_index("ha")
    me = (pb // 16, (pb // 4) % 4, pb % 4)

    def moved(base, axis, off):
        return base + (lax.rem(me[axis] + off, SIDE) - me[axis]) * STRIDES[axis]

    def chip(axis, off):
        return {"pb": moved(pb, axis, off), "ha": ha}

    other = {"pb": pb, "ha": 1 - ha}

    def remote(src, dst, ssem, rsem, dev):
        return pltpu.make_async_remote_copy(
            src_ref=src, dst_ref=dst, send_sem=ssem, recv_sem=rsem, device_id=dev, device_id_type=MESH
        )

    half_rows = pltpu.make_async_copy(
        tokens_ref.at[:, pl.ds(pl.multiple_of(ha * HALF, HALF), HALF)], tok, t_s
    )
    small = [
        pltpu.make_async_copy(src, dst, v_s.at[i])
        for i, (src, dst) in enumerate(
            (
                (shift_ref, shift),
                (scale_ref, scale),
                (owner_ref, owners),
                (block_ref, blocks),
                (owner_ref, owner_s),
                (tokens_ref.at[pl.ds(ha * 4, 4)], own),
                (w_in[0], qkv_w.at[0, ha]),
                (w_in[1], qkv_w.at[1, ha]),
                (w_in[2], qkv_w.at[2, ha]),
            )
        )
    ]
    for copy in small[:2] + [half_rows] + small[2:]:
        copy.start()

    barrier = pltpu.get_barrier_semaphore()
    for axis in range(3):
        for off in (1, 2, 3):
            pl.semaphore_signal(barrier, 1, device_id=chip(axis, off), device_id_type=MESH)
    pl.semaphore_signal(barrier, 1, device_id=other, device_id_type=MESH)
    small[0].wait()
    small[1].wait()
    half_rows.wait()
    for t in range(QB_DEV):
        n = modulate(tok[t].astype(jnp.float32), shift[...].reshape(1, D), scale[...].reshape(1, D))
        n = n.astype(jnp.bfloat16)
        for p in range(3):
            plane[p][t] = n[:, p * PART : (p + 1) * PART]
    pl.semaphore_wait(barrier, 10)

    def go(copy):
        copy.start()

    def arrived(ref, semaphore):
        remote(ref, ref, x_s, semaphore, other).wait_recv()

    local = []

    def tiles(p, db, da, first=0, count=QB_DEV):
        return plane[p].at[pl.ds((db * SIDE + da) * QB_DEV + first, count)]

    def send_a(p, d):
        return remote(
            tiles(p, 0, 0), tiles(p, 0, 3 if d == 0 else 1), a_s, a_r.at[p, d], chip(ORDERS[p][0], 1 if d == 0 else 3)
        )

    def forward_a(p, d):
        return remote(
            tiles(p, 0, 3 if d == 0 else 1, 4 * d, 4),
            tiles(p, 0, 2, 4 * d, 4),
            af_s,
            af_r.at[p],
            chip(ORDERS[p][0], 1 if d == 0 else 3),
        )

    def send_b(p, da, d):
        return remote(
            tiles(p, 0, da),
            tiles(p, 3 if d == 0 else 1, da),
            b_s,
            b_r.at[p, da, d],
            chip(ORDERS[p][1], 1 if d == 0 else 3),
        )

    def forward_b(p, da, d):
        return remote(
            tiles(p, 3 if d == 0 else 1, da, 4 * d, 4),
            tiles(p, 2, da, 4 * d, 4),
            bf_s,
            bf_r.at[p],
            chip(ORDERS[p][1], 1 if d == 0 else 3),
        )

    def send_c(p, g, h):
        off = OFFS[g]
        return remote(
            picked.at[p, g, pl.ds(h * PIECE, PIECE)],
            kv_ref.at[p, 0, SIDE - off, pl.ds(h * PIECE, PIECE)],
            c_s,
            c_r.at[p, g - 1, h],
            chip(ORDERS[p][2], off),
        )

    def cross(p, g, h):
        part = pl.ds(h * PIECE, PIECE)
        src = picked.at[p, 0, part] if g == 0 else kv_ref.at[p, 0, SIDE - OFFS[g], part]
        return remote(src, kv_ref.at[p, 1, (SIDE - OFFS[g]) % SIDE, part], x_s, x_r, other)

    def select(p, g, h):
        lane = moved(pb, ORDERS[p][2], OFFS[g]) * QB_DEV

        def pick(i, carry):
            at = h * PIECE + i
            picked[p, g, at] = plane[p][sel_ref[p, at, lane]]
            return carry

        lax.fori_loop(0, PIECE, pick, 0, unroll=PIECE)

    for p in range(3):
        for d in range(2):
            go(send_a(p, d))
    for p in range(3):
        for d in range(2):
            go(send_b(p, 0, d))
    weights = [
        remote(w_in[i], qkv_w.at[i, ha] if i < 3 else w_out[i - 1], w_s.at[i], w_r.at[i], other)
        for i in range(6)
    ]
    for copy in weights:
        go(copy)

    def keep_local(src, dst, number):
        local.append(pltpu.make_async_copy(src, dst, v_s.at[number]))
        local[-1].start()

    def place_entry(e, carry):
        i, j = e // KT, e % KT
        at = pb * QB_DEV + ha * 4 + i
        owner = owner_s[j, at]
        for p in range(3):
            c = ORDERS[p][2]
            rel = (owner // STRIDES[c] - me[c]) & 3
            places[p, e] = rel * SIDE * 8 + jnp.minimum(rank_s[c, j, at], CAP - 1)
        return carry

    def own_blocks():
        small[5].wait()
        stream = own[...].reshape(OWN, D).astype(jnp.float32)
        normed = modulate(stream, shift[...].reshape(1, D), scale[...].reshape(1, D))
        own[...] = normed.astype(jnp.bfloat16).reshape(4, QBLK, D)
        for i in range(3):
            small[6 + i].wait()
            remote(w_in[i], qkv_w.at[i, 1 - ha], w_s.at[i], w_r.at[i], other).wait_recv()
        keep_local(qkv_w.at[1, 1 - ha], w_out[0], 16)
        keep_local(qkv_w.at[2, 1 - ha], w_out[1], 11)

        def one_group(g, carry):
            def product(i):
                return jnp.dot(
                    own[...].reshape(OWN, D), qkv_w[i, g], preferred_element_type=jnp.float32
                )

            queries[g] = (product(0) * SHARP).astype(jnp.bfloat16)
            for i in range(2):
                result = product(1 + i).astype(jnp.bfloat16)
                for w, (lo, _, spare) in enumerate(WINDOWS):
                    window = result[:, lo : lo + 256]
                    if i == 1:
                        window = with_lane(window, spare, jnp.ones((OWN, 128), jnp.bfloat16))
                    mine[g, w, i] = window
            return carry

        lax.fori_loop(0, 2, one_group, 0)
        keep_local(queries, q_out, 12)
        lax.fori_loop(0, 4 * KT, place_entry, 0)
        keep_local(places, place_out, 14)

    def own_attention():
        def one_block(i, carry):
            g = i // 4
            at = pl.ds(pl.multiple_of((i % 4) * QBLK, QBLK), QBLK)
            above, below, tops = attend_windows(
                queries[g, at, :], [mine[g, w, 0, at, :] for w in range(2)], [mine[g, w, 1, at, :] for w in range(2)], False
            )
            partial[g, at, :] = above / below
            logs[g, at, :] = tops + jnp.log2(below)
            return carry

        lax.fori_loop(0, 8, one_block, 0)
        keep_local(partial, part_out, 13)
        keep_local(logs, log_out, 15)

    for p in range(3):
        for d in range(2):
            send_a(p, d).wait_recv()
            go(forward_a(p, d))
        for d in range(2):
            for da in (3, 1):
                go(send_b(p, da, d))
    for p in range(3):
        arrived(tiles(p, 0, 2), af_r.at[p])
        for d in range(2):
            go(send_b(p, 2, d))
    for da in (0, 3):
        for p in range(3):
            for d in range(2):
                send_b(p, da, d).wait_recv()
                go(forward_b(p, da, d))
    small[2].wait()
    small[3].wait()
    size = N_PB * QB_DEV
    wide = (KT, size)
    lane = lax.broadcasted_iota(jnp.int32, wide, 1) & 7
    line = lax.broadcasted_iota(jnp.int32, wide, 0)
    coords = [(owners[...] // stride) & 3 for stride in STRIDES]

    def ranked(marks):
        column = marks
        for step in (1, 2, 4):
            column = column + jnp.where(line >= step, pltpu.roll(column, step, 0), 0)
        total = jnp.broadcast_to(jnp.sum(marks, 0, keepdims=True), wide)
        row = total
        for step in (1, 2, 4):
            row = row + jnp.where(lane >= step, pltpu.roll(row, step, 1), 0)
        return column - marks + row - total

    top = jnp.zeros(wide, jnp.int32)
    for axis in range(3):
        rank = jnp.zeros(wide, jnp.int32)
        for value in range(SIDE):
            here = coords[axis] == value
            rank = jnp.where(here, ranked(here.astype(jnp.int32)), rank)
        ranks[axis] = rank
        top = jnp.maximum(top, rank)
    most_out[0, 0] = jnp.max(top)

    for p in range(3):
        a, b, c = ORDERS[p]
        rel_b, rel_a = (coords[b] - me[b]) & 3, (coords[a] - me[a]) & 3
        number = (rel_b * SIDE + rel_a) * QB_DEV + blocks[...]
        slot = jnp.where(coords[c] == me[c], ranks[c], -1)

        def tabulate(i, carry):
            found = [
                jnp.max(jnp.where(slot == i * 8 + n, number, 0), 0, keepdims=True) for n in range(8)
            ]
            found = jnp.concatenate(found, 0)
            for step in (1, 2, 4):
                found = jnp.maximum(found, pltpu.roll(found, size - step, 1))
            table[p, pl.ds(pl.multiple_of(i * 8, 8), 8), :] = found
            return carry

        lax.fori_loop(0, SLOTS // 8, tabulate, 0)
    to_scalars = pltpu.make_async_copy(table, sel_ref, v_s.at[9])
    to_scalars.start()
    ranks_out = pltpu.make_async_copy(ranks, rank_s, v_s.at[10])
    ranks_out.start()
    for da in (1, 2):
        for p in range(3):
            for d in range(2):
                send_b(p, da, d).wait_recv()
                go(forward_b(p, da, d))
    to_scalars.wait()
    ranks_out.wait()
    small[4].wait()
    own_blocks()
    for p in range(3):
        arrived(plane[p].at[pl.ds(2 * SIDE * QB_DEV, SIDE * QB_DEV)], bf_r.at[p])
        for h in range(PIECES):
            for g in (3, 1, 2):
                select(p, g, h)
                go(send_c(p, g, h))
    for p in range(3):
        for h in range(PIECES):
            select(p, 0, h)
            go(cross(p, 0, h))
        pltpu.make_async_copy(picked.at[p, 0], kv_ref.at[p, 0, 0, pl.ds(0, CAP)], l_s).start()
    own_attention()
    for h in range(PIECES):
        for g in (3, 1, 2):
            for p in range(3):
                send_c(p, g, h).wait_recv()
                go(cross(p, g, h))
    arrived(kv_ref.at[:, 1, :, pl.ds(0, CAP)], x_r)
    for copy in weights[3:]:
        copy.wait_recv()
    for copy in weights:
        copy.wait_send()
    for ref, semaphore in (
        (kv_ref.at[:, 0, pl.ds(0, 2), pl.ds(0, 8)], a_s),
        (kv_ref.at[:, 0, pl.ds(0, 1), pl.ds(0, 8)], af_s),
        (kv_ref.at[:, 0, :, pl.ds(0, 16)], b_s),
        (kv_ref.at[:, 0, :, pl.ds(0, 8)], bf_s),
        (picked.at[:, pl.ds(1, 3)], c_s),
        (kv_ref.at[:, 1, :, pl.ds(0, CAP)], x_s),
    ):
        remote(ref, ref, semaphore, x_r, other).wait_send()
    pltpu.make_async_copy(picked.at[:, 0], kv_ref.at[:, 0, 0, pl.ds(0, CAP)], l_s).wait()
    for copy in local:
        copy.wait()


def exchange_pooled(tokens, shift, scale, owners, blocks, weights):
    dma = pltpu.SemaphoreType.DMA
    bf16 = jnp.bfloat16
    kv_shape = jax.ShapeDtypeStruct((3, 2, SIDE, SIDE * 8, HALF, PART), bf16)
    table = (3, SLOTS, N_PB * QB_DEV)
    ranks = (3, KT, N_PB * QB_DEV)
    return pl.pallas_call(
        pooled_kernel,
        out_shape=[
            kv_shape,
            jax.ShapeDtypeStruct((8, 128), jnp.int32),
            jax.ShapeDtypeStruct((2, OWN, GRP), bf16),
            jax.ShapeDtypeStruct((2, OWN, GRP), jnp.float32),
            jax.ShapeDtypeStruct((2, OWN, GRP), jnp.float32),
            jax.ShapeDtypeStruct((1, 1), jnp.int32),
        ]
        + [jax.ShapeDtypeStruct(w.shape, w.dtype) for w in weights[1:]],
        in_specs=[HBM] * 11,
        out_specs=[HBM] * 5 + [pl.BlockSpec(memory_space=pltpu.SMEM)] + [HBM] * 5,
        scratch_shapes=[pltpu.VMEM((SIDE * SIDE * QB_DEV, HALF, PART), bf16)] * 3
        + [pltpu.VMEM((3, 4, CAP, HALF, PART), bf16)]
        + [pltpu.VMEM((QB_DEV, HALF, D), bf16)]
        + [pltpu.VMEM((D,), jnp.float32)] * 2
        + [pltpu.VMEM((KT, N_PB * QB_DEV), jnp.int32)] * 2
        + [pltpu.VMEM(table, jnp.int32), pltpu.SMEM(table, jnp.int32)]
        + [pltpu.VMEM(ranks, jnp.int32), pltpu.SMEM(ranks, jnp.int32)]
        + [pltpu.SMEM((KT, N_PB * QB_DEV), jnp.int32), pltpu.SMEM((8, 128), jnp.int32)]
        + [
            pltpu.VMEM((4, QBLK, D), bf16),
            pltpu.VMEM((3, 2, D, GRP), bf16),
            pltpu.VMEM((2, OWN, GRP), bf16),
            pltpu.VMEM((2, 2, 2, OWN, 256), bf16),
            pltpu.VMEM((2, OWN, GRP), jnp.float32),
            pltpu.VMEM((2, OWN, GRP), jnp.float32),
        ]
        + [dma, dma((3, 2)), dma, dma((3,))]
        + [dma, dma((3, 4, 2)), dma, dma((3,))]
        + [dma, dma((3, 3, PIECES)), dma, dma, dma]
        + [dma((6,)), dma((6,)), dma, dma((17,))],
        compiler_params=pltpu.CompilerParams(
            collective_id=1, has_side_effects=True, vmem_limit_bytes=62 * MIB
        ),
        name="exchange_pooled",
    )(tokens.reshape(QB_DEV, QBLK, D), shift, scale, owners, blocks, *weights)


def block_kernel(count_ref, place_ref, *refs):
    vectors_h = refs[0:4]
    tokens_ref, q_h, part_h, log_h, kv_ref = refs[4:9]
    own_h, other_h = refs[9:14], refs[14:19]
    out_ref = refs[19]
    vectors = refs[20:24]
    x_refs = refs[24:26]
    key_refs = refs[26:28]
    value_refs = refs[28:30]
    tok, queries, partial, logs, att = refs[30:35]
    wkv, wo, w1, w2 = refs[35:39]
    sem, vsem, gsem = refs[39:]
    gate_a, shift_m, scale_m, gate_m = vectors
    bf16 = jnp.bfloat16

    def row(vector):
        return vector[...].reshape(1, D)

    ha = lax.axis_index("ha")
    late = [
        pltpu.make_async_copy(src, dst, vsem.at[i])
        for i, (src, dst) in enumerate(
            [(vectors_h[i], vectors[i]) for i in range(4)]
            + [(tokens_ref.at[pl.ds(pl.multiple_of(ha * OWN, OWN), OWN)], tok)]
        )
    ]
    early = [
        pltpu.make_async_copy(src, dst, vsem.at[5 + i])
        for i, (src, dst) in enumerate(((q_h, queries), (part_h, partial), (log_h, logs)))
    ]
    loads = []
    for i in range(5):
        pair = []
        for src, at, number in ((own_h[i], ha, i), (other_h[i], 1 - ha, 5 + i)):
            if i < 2:
                dst = wkv.at[at, :, pl.ds(i * GRP, GRP)]
            elif i == 2:
                dst = wo.at[pl.ds(pl.multiple_of(at * GRP, GRP), GRP)]
            else:
                dst = (w1, w2)[i - 3].at[at]
            pair.append(pltpu.make_async_copy(src, dst, sem.at[number]))
        loads.append(pair)

    def begin(*numbers):
        for i in numbers:
            loads[i][0].start()
            loads[i][1].start()

    def ready(*numbers):
        for i in numbers:
            loads[i][0].wait()
            loads[i][1].wait()

    def gather(blk, slot):
        for j in range(KT):
            for p in range(3):
                pltpu.make_async_copy(
                    kv_ref.at[p, :, place_ref[p, blk * KT + j]],
                    x_refs[slot].at[j, :, :, pl.ds(p * PART, PART)],
                    gsem.at[slot],
                ).start()

    def gathered(slot):
        pltpu.make_async_copy(x_refs[slot], x_refs[slot], gsem.at[slot]).wait()

    def project(blk, slot):
        x = x_refs[slot][...].reshape(ROWS, D)
        live = count_ref[ha * 4 + blk] * QBLK
        place = lax.broadcasted_iota(jnp.int32, (ROWS, 128), 0)
        bias = jnp.where(place < live, 0.0, DEAD).astype(bf16)
        for g in range(2):
            both = jnp.dot(x, wkv[g], preferred_element_type=jnp.float32).astype(bf16)
            k, v = both[:, :GRP], both[:, GRP:]
            for w, (lo, _, spare) in enumerate(WINDOWS):
                key_refs[slot][g, w] = with_lane(k[:, lo : lo + 256], spare, bias)
                value_refs[slot][g, w] = with_lane(v[:, lo : lo + 256], spare, jnp.ones_like(bias))

    def attend(blk, slot):
        at = slice(blk * QBLK, (blk + 1) * QBLK)
        for g in range(2):
            above, below, tops = attend_windows(
                queries[g, at, :],
                [key_refs[slot].at[g, w][...] for w in range(2)],
                [value_refs[slot].at[g, w][...] for w in range(2)],
                True,
            )
            log = logs[g, at, :]
            most = jnp.maximum(tops, log)
            listed, mine = jnp.exp2(tops - most), jnp.exp2(log - most)
            result = (above * listed + partial[g, at, :] * mine) / (below * listed + mine)
            att[at, g * GRP : (g + 1) * GRP] = result.astype(bf16)

    begin(0, 1)
    gather(0, 0)
    ready(0, 1)
    gathered(0)
    for copy in early:
        copy.start()
    gather(1, 1)
    for copy in late:
        copy.start()
    begin(2, 3, 4)
    project(0, 0)
    for copy in early:
        copy.wait()
    for blk in range(4):
        slot = blk % 2
        if blk < 2:
            gather(blk + 2, slot)
        if blk < 3:
            gathered(1 - slot)
            project(blk + 1, 1 - slot)
        attend(blk, slot)

    for copy in late:
        copy.wait()
    ready(2)
    projected = jnp.dot(att[...], wo[...], preferred_element_type=jnp.float32)
    residual = (tok[...].astype(jnp.float32) + row(gate_a) * projected).astype(bf16)
    normed = modulate(residual.astype(jnp.float32), row(shift_m), row(scale_m)).astype(bf16)
    ready(3, 4)
    expanded = jnp.zeros((OWN, D), jnp.float32)
    for g in range(2):
        for lo in range(0, FF // 2, CHUNK):
            hidden = jnp.dot(normed, w1[g, :, lo : lo + CHUNK], preferred_element_type=jnp.float32)
            hidden = jax.nn.gelu(hidden, approximate=True).astype(bf16)
            expanded += jnp.dot(hidden, w2[g, lo : lo + CHUNK, :], preferred_element_type=jnp.float32)
    out_ref[...] = (residual.astype(jnp.float32) + row(gate_m) * expanded).astype(bf16)


def block(counts, places, vectors, tokens, queries, partial, logs, kv, own, other):
    bf16 = jnp.bfloat16
    dma = pltpu.SemaphoreType.DMA
    kv = kv.reshape(3, 2, -1, HALF, PART)
    return pl.pallas_call(
        block_kernel,
        out_shape=jax.ShapeDtypeStruct((OWN, D), bf16),
        in_specs=[pl.BlockSpec(memory_space=pltpu.SMEM)] * 2 + [HBM] * 19,
        out_specs=pl.BlockSpec(memory_space=pltpu.VMEM),
        scratch_shapes=[pltpu.VMEM((D,), jnp.float32)] * 4
        + [pltpu.VMEM((KT, 2, HALF, D), bf16)] * 2
        + [pltpu.VMEM((2, 2, ROWS, 256), bf16)] * 4
        + [
            pltpu.VMEM((OWN, D), bf16),
            pltpu.VMEM((2, OWN, GRP), bf16),
            pltpu.VMEM((2, OWN, GRP), jnp.float32),
            pltpu.VMEM((2, OWN, GRP), jnp.float32),
            pltpu.VMEM((OWN, D), bf16),
            pltpu.VMEM((2, D, 2 * GRP), bf16),
            pltpu.VMEM((D, D), bf16),
            pltpu.VMEM((2, D, FF // 2), bf16),
            pltpu.VMEM((2, FF // 2, D), bf16),
        ]
        + [dma((10,)), dma((8,)), dma((2,))],
        compiler_params=pltpu.CompilerParams(vmem_limit_bytes=62 * MIB),
        name="block",
    )(counts, places, *vectors, tokens, queries, partial, logs, kv, *own, *other)


def shards(
    tokens,
    shift_attn,
    scale_attn,
    gate_attn,
    shift_mlp,
    scale_mlp,
    gate_mlp,
    w_query,
    w_key,
    w_value,
    w_out,
    w_fc1,
    w_fc2,
    contact_owner,
    contact_local,
    contact_count,
):
    vectors = (gate_attn, shift_mlp, scale_mlp, gate_mlp)
    own = (w_query, w_key, w_value, w_out, w_fc1, w_fc2)
    owners, blocks = contact_owner.T, contact_local.T
    args = (tokens, shift_attn, scale_attn, owners, blocks, own)
    kv, places, queries, partial, logs, most, *other = exchange_pooled(*args)

    def crowded():
        other_kv, other_places, *_ = exchange(*args)
        return other_kv.reshape(kv.shape), other_places

    kv_used, places_used = lax.cond(most[0, 0] < CAP, lambda: (kv, places), crowded)
    return block(contact_count, places_used, vectors, tokens, queries, partial, logs, kv_used, own[1:], other)


def solution(mesh):
    placed = (
        P("pb", None),
        P(),
        P(),
        P(),
        P(),
        P(),
        P(),
        P(None, "ha"),
        P(None, "ha"),
        P(None, "ha"),
        P("ha", None),
        P(None, "ha"),
        P("ha", None),
        P(),
        P(),
        P("pb"),
    )
    return jax.shard_map(
        shards, mesh=mesh, in_specs=placed, out_specs=P(("pb", "ha"), None), check_vma=False
    )
```
